512 devices in a mesh: row: 32 (over y_lo, z, core), col: 16 (over y_hi, x).
Axes of the slice: x: 4, y: 8 (y_hi: 4, y_lo: 2; y = y_hi * 2 + y_lo), z: 8, core: 2. Of those that a mesh axis runs over, the one named last changes fastest.
Arguments:
- active_flags: int32 [256, 128], P('row', 'col'), may hold values 0 or 1
- port_index: int32 [256, 128], P('row', 'col'), may hold values from 0 to 7
- drive_weights: float32 [2, 4, 256, 128], P(None, None, 'row', 'col'), may hold values from -6 to 6
- feed_table: float32 [2, 8, 1024], replicated, may hold values from -6 to 6
- cell_map: bfloat16 [2, 1024, 1024], replicated, may hold values from -0.125 to 0.125
- probe_weights: float32 [2, 1024], replicated, may hold values from -0.1875 to 0.1875
Outputs:
- currents: float32 [2, 4, 256, 128], P(None, None, 'row', 'col')
- far_pattern: float32 [2, 4, 1024, 512], P(None, None, 'row', 'col')
The draws below stay inside these ranges and needn't reach their ends.
All inputs are finite; a program needn't handle non-finite values. No bound on the sum of `active_flags` on one device may be relied on, other than what follows from the above.
Results may differ from the reference program's by a relative error of at most 0.0024.
Values sent between devices are 32-bit elements; how exact they have to be, the bound alone decides.
No kernel may reach another device: no remote copies, remote signals or barrier semaphores. Data moves between devices by JAX's collectives and lax.ppermute only.
A program may use at most 64 MiB of HBM per device.

```python
import math
import jax
import jax.numpy as jnp
from jax import lax

U = 1024
PORTS = 8
S = 4
ITERS = 2
NR = 256
NC = 128
KX = 1024
KY = 512


def with_ends(entries, own_key, low, largest):
    longest = entries.shape.index(max(entries.shape))
    spots = []
    for shift in (0, 1):
        where = [jax.random.randint(jax.random.fold_in(own_key, axis), (), 0, length) for axis, length in enumerate(entries.shape)]
        where[longest] = (where[longest] + shift) % entries.shape[longest]
        spots.append(tuple(where))
    return entries.at[spots[0]].set(low).at[spots[1]].set(largest)


def block_scale(rng, shape, shards, low, top_value):
    level = 1.0
    for position, blocks in shards:
        heights = jax.random.uniform(jax.random.fold_in(jax.random.fold_in(rng, 6), position), (blocks,), jnp.float32, low / len(shards), top_value / len(shards))
        level = level * jnp.repeat(jnp.exp(heights), shape[position] // blocks).reshape((-1,) + (1,) * (len(shape) - 1 - position))
    return level


def centred(key, extent, width, limit, shards=(), kind=jnp.bfloat16):
    loudness = block_scale(key, extent, shards, -0.22, 0.18) if shards else 1.0
    drawn = jax.random.normal(key, extent, jnp.float32) * width * loudness
    return jnp.minimum(jnp.maximum(drawn, -limit), limit).astype(kind)


def setup_inputs(seed: int = 0) -> dict:
    keys = jax.random.split(jax.random.key(seed), 7)
    return {
        "active_flags": with_ends((jax.random.randint(keys[0], (NR, NC), 0, 4) < 3).astype(jnp.int32), jax.random.fold_in(keys[0], 1), 0, 1),
        "port_index": with_ends(jax.random.randint(keys[1], (NR, NC), 0, PORTS), jax.random.fold_in(keys[1], 1), 0, PORTS - 1).astype(jnp.int32),
        "drive_weights": centred(keys[2], (2, S, NR, NC), 1.0, 6.0, ((2, 32), (3, 16)), jnp.float32),
        "feed_table": centred(keys[3], (2, PORTS, U), 1.0, 6.0, (), jnp.float32),
        "cell_map": centred(keys[4], (2, U, U), (2 * U) ** -0.5, 0.125),
        "probe_weights": centred(keys[5], (2, U), U ** -0.5, 0.1875, (), jnp.float32),
    }


relaxation = 0.75
reflect_re = -0.3
reflect_im = 0.2


def reflect(edge_wave):
    return jnp.stack([reflect_re * edge_wave[0] - reflect_im * edge_wave[1],
                      reflect_re * edge_wave[1] + reflect_im * edge_wave[0]])


def couple(outgoing, previous):
    edge_size = outgoing.shape[-1] // 4
    north = outgoing[..., 0:edge_size]
    south = outgoing[..., edge_size:2 * edge_size]
    west = outgoing[..., 2 * edge_size:3 * edge_size]
    east = outgoing[..., 3 * edge_size:]
    north_in = jnp.concatenate([reflect(north[:, :1]), south[:, :-1]], axis=1)
    south_in = jnp.concatenate([north[:, 1:], reflect(south[:, -1:])], axis=1)
    west_in = jnp.concatenate([reflect(west[:, :, :1]), east[:, :, :-1]], axis=2)
    east_in = jnp.concatenate([west[:, :, 1:], reflect(east[:, :, -1:])], axis=2)
    arrived = jnp.concatenate([north_in, south_in, west_in, east_in], axis=-1)
    return relaxation * arrived + (1.0 - relaxation) * previous


def apply_map(rounded, weights):
    layout = rounded.shape
    flattened = rounded.reshape(-1, layout[-1])
    real_part = jnp.dot(flattened, weights[0], preferred_element_type=jnp.float32).reshape(layout[:-1] + (weights.shape[2],))
    imag_part = jnp.dot(flattened, weights[1], preferred_element_type=jnp.float32).reshape(layout[:-1] + (weights.shape[2],))
    return jnp.stack([real_part[0] - imag_part[1], imag_part[0] + real_part[1]])


def one_state(state_drive, feed_cells, cell_map, probe_weights):
    amp_re = state_drive[0][..., None]
    amp_im = state_drive[1][..., None]
    source = jnp.stack([amp_re * feed_cells[0] - amp_im * feed_cells[1],
                        amp_re * feed_cells[1] + amp_im * feed_cells[0]])
    outgoing = source
    incoming = jnp.zeros_like(source)
    for iteration in range(ITERS):
        incoming = couple(outgoing, incoming)
        outgoing = apply_map(incoming.astype(jnp.bfloat16), cell_map) + source
    totals = outgoing + incoming
    return jnp.stack([jnp.sum(probe_weights[0] * totals[0] - probe_weights[1] * totals[1], axis=-1),
                      jnp.sum(probe_weights[0] * totals[1] + probe_weights[1] * totals[0], axis=-1)])


def twiddle(first_index, second_index, length):
    products = (first_index[:, None] * second_index[None, :]) % length
    angles = products.astype(jnp.float32) * (2.0 * math.pi / length)
    return jnp.cos(angles), -jnp.sin(angles)


def along_columns(values, cos_table, sin_table):
    highest = lax.Precision.HIGHEST
    real_part = jnp.einsum("xsrc,ck->xsrk", values, cos_table, precision=highest)
    imag_part = jnp.einsum("xsrc,ck->xsrk", values, sin_table, precision=highest)
    return jnp.stack([real_part[0] - imag_part[1], imag_part[0] + real_part[1]])


def along_rows(values, cos_table, sin_table):
    highest = lax.Precision.HIGHEST
    real_part = jnp.einsum("xsrk,rl->xslk", values, cos_table, precision=highest)
    imag_part = jnp.einsum("xsrk,rl->xslk", values, sin_table, precision=highest)
    return jnp.stack([real_part[0] - imag_part[1], imag_part[0] + real_part[1]])


def reference(active_flags, port_index, drive_weights, feed_table, cell_map, probe_weights):
    feed_cells = feed_table[:, port_index]
    amplitude = drive_weights * active_flags.astype(jnp.float32)[None, None]
    per_state = jnp.moveaxis(amplitude, 1, 0)
    currents = lax.map(lambda state_drive: one_state(state_drive, feed_cells, cell_map, probe_weights), per_state)
    currents = jnp.moveaxis(currents, 0, 1)
    cos_y, sin_y = twiddle(jnp.arange(NC, dtype=jnp.int32), jnp.arange(KY, dtype=jnp.int32), KY)
    cos_x, sin_x = twiddle(jnp.arange(NR, dtype=jnp.int32), jnp.arange(KX, dtype=jnp.int32), KX)
    section_one = along_columns(currents, cos_y, sin_y)
    far_pattern = along_rows(section_one, cos_x, sin_x) * (NR * NC) ** -0.5
    return currents, far_pattern
```

```python
import functools
import math

import jax
import jax.numpy as jnp
import numpy as np
from jax import lax
from jax.experimental import pallas as pl
from jax.experimental.pallas import tpu as pltpu
from jax.sharding import PartitionSpec as P

OVER = 4
PORTS = 8
STATES = 4
BLOCK = 8
REACH = 2
WIDE = 12
LANES = 128

relaxation = 0.75
reflect_re = -0.3
reflect_im = 0.2

STEP = ((-1, 0), (1, 0), (0, -1), (0, 1))
PLACES = tuple(
    (dr, dc) for dr in range(-2, 3) for dc in range(-2, 3) if abs(dr) + abs(dc) <= 2
)
CLASSES = 13
ROWS = 32


def path_matrix():
    twice = relaxation * relaxation
    once = relaxation * (1.0 - relaxation) + relaxation
    mix = np.zeros((CLASSES * ROWS, 18 * 24), np.float32)

    def add(weight, first, second, place, kind):
        d = PLACES.index(place)
        for part, left, right, sign in ((0, 0, 0, 1), (0, 1, 1, -1), (1, 0, 1, 1), (1, 1, 0, 1)):
            at = 16 + right if second is None else right * 8 + second
            mix[kind * ROWS + part * 13 + d, (first * 2 + left) * 24 + at] += sign * weight

    def corner(e, f):
        return 9 + (min(e, f) % 2) * 2 + (max(e, f) % 2)

    add(1.0, 0, None, (0, 0), 0)
    for e in range(4):
        add(once, 0, e, STEP[e], 0)
        add(once, 0, 4 + e, (0, 0), 1 + e)
        for f in range(4):
            both = (STEP[e][0] + STEP[f][0], STEP[e][1] + STEP[f][1])
            crossed = e // 2 != f // 2
            add(twice, 1 + e, f, both, 0)
            if f == e ^ 1:
                add(-twice, 1 + e, f, both, 1 + e)
            if f != e:
                add(twice, 5 + e, f, STEP[f], 1 + e)
            if f == e:
                add(twice, 1 + e, 4 + f, STEP[e], 5 + e)
                add(twice, 5 + e, 4 + f, (0, 0), 1 + e)
            elif crossed:
                add(twice, 1 + e, 4 + f, STEP[e], 1 + f)
                add(twice, 5 + e, 4 + f, (0, 0), corner(e, f))
    return mix


def halves(value):
    high = value.astype(jnp.bfloat16)
    return high, (value - high.astype(jnp.float32)).astype(jnp.bfloat16)


def cosine(turns, length):
    centred = jnp.where(turns >= length // 2, length - turns, turns)
    angle = (length // 4 - centred).astype(jnp.float32) * (2.0 * math.pi / length)
    square = angle * angle
    value = 1.0 / 6227020800.0
    value = value * square - 1.0 / 39916800.0
    value = value * square + 1.0 / 362880.0
    value = value * square - 1.0 / 5040.0
    value = value * square + 1.0 / 120.0
    value = value * square - 1.0 / 6.0
    return angle + angle * square * value


def dot(left, right, dims=((1,), (0,))):
    return lax.dot_general(left, right, (dims, ((), ())), preferred_element_type=jnp.float32)


def dot3(left, right):
    high, low = left
    high_right, low_right = right
    return dot(high, high_right) + (dot(low, high_right) + dot(high, low_right))


def pack_kernel(drive_ref, flag_ref, port_ref, out_ref):
    active = flag_ref[...].astype(jnp.float32)
    pieces = [drive_ref[x, s] * active for x in range(2) for s in range(STATES)]
    pieces.append(port_ref[...].astype(jnp.float32))
    pieces.append(jnp.zeros((BLOCK, LANES - 9 * BLOCK), jnp.float32))
    packed = jnp.concatenate(pieces, axis=1)
    out_ref[...] = jnp.broadcast_to(packed[None], out_ref.shape)


def table_kernel(place, rows, cols, feed_ref, map_ref, probe_ref, mix_ref, table_ref, row_high_ref, row_low_ref, col_high_ref, col_low_ref, hops_ref):
    row_at, col_at = place()
    edge = feed_ref.shape[2] // 4
    units = 4 * edge

    def block(value, e):
        return value[:, e * edge : (e + 1) * edge]

    feed_re, feed_im = feed_ref[0], feed_ref[1]
    back_re = reflect_re * feed_re - reflect_im * feed_im
    back_im = reflect_re * feed_im + reflect_im * feed_re
    hops_ref[0:8, :] = feed_re
    hops_ref[8:16, :] = feed_im
    for a in range(4):
        e = a ^ 1
        enter = jnp.concatenate(
            [block(feed_re, e), block(feed_im, e), block(back_re, a), block(back_im, a)], axis=0
        )
        enter = jnp.concatenate(halves(enter), axis=0)
        by_re = dot(enter, map_ref[0, a * edge : (a + 1) * edge, :])
        by_im = dot(enter, map_ref[1, a * edge : (a + 1) * edge, :])
        by_re = by_re[0:32] + by_re[32:64]
        by_im = by_im[0:32] + by_im[32:64]
        for first, at in ((1 + e, 0), (5 + a, 16)):
            hops_ref[first * 16 : first * 16 + 8, :] = by_re[at : at + 8] - by_im[at + 8 : at + 16]
            hops_ref[first * 16 + 8 : first * 16 + 16, :] = (
                by_re[at + 8 : at + 16] + by_im[at : at + 8]
            )
    probe_re, probe_im = probe_ref[0:1, :], probe_ref[1:2, :]
    probes = jnp.concatenate(halves(jnp.concatenate([probe_re, probe_im] + [probe_re] * 6, axis=0)), axis=0)
    through_re = dot(probes, map_ref[0], ((1,), (1,)))
    through_im = dot(probes, map_ref[1], ((1,), (1,)))
    through_re = through_re[0:8] + through_re[8:16]
    through_im = through_im[0:8] + through_im[8:16]
    total_re = probe_re + through_re[0:1] - through_im[1:2]
    total_im = probe_im + through_im[0:1] + through_re[1:2]

    def swapped(value):
        return jnp.concatenate([block(value, e ^ 1) for e in range(4)], axis=1)

    sub = lax.broadcasted_iota(jnp.int32, (8, units), 0)
    lane = lax.broadcasted_iota(jnp.int32, (8, units), 1)
    own = lane // edge == sub % 4
    passed = sub < 4
    out_re = jnp.where(passed, swapped(total_re), reflect_re * total_re - reflect_im * total_im)
    out_im = jnp.where(passed, swapped(total_im), reflect_re * total_im + reflect_im * total_re)
    leave = jnp.concatenate(
        [
            jnp.where(own, out_re, 0.0),
            jnp.where(own, out_im, 0.0),
            jnp.where(sub == 0, probe_re, jnp.where(sub == 1, probe_im, 0.0)),
        ],
        axis=0,
    )
    products = lax.dot_general(
        leave, hops_ref[...], (((1,), (1,)), ((), ())),
        precision=lax.Precision.HIGHEST, preferred_element_type=jnp.float32,
    )
    flat = jnp.concatenate([products[:, 8 * k : 8 * k + 8] for k in range(18)], axis=0)
    table = lax.dot_general(
        mix_ref[...], flat, (((1,), (0,)), ((), ())),
        precision=lax.Precision.HIGHEST, preferred_element_type=jnp.float32,
    )
    wide = [table[k * ROWS : (k + 1) * ROWS, :] for k in range(CLASSES)]
    wide.append(jnp.zeros((ROWS, LANES - 8 * CLASSES), jnp.float32))
    table_ref[...] = jnp.concatenate(halves(jnp.concatenate(wide, axis=1)), axis=0)

    span = OVER * rows
    r = lax.broadcasted_iota(jnp.int32, (rows, LANES), 0)
    k = lax.broadcasted_iota(jnp.int32, (rows, LANES), 1)
    samples = OVER * BLOCK
    turns = (r * (row_at * samples + k)) & (span - 1)
    cos = jnp.where(k < samples, cosine(turns, span), 0.0)
    sin = jnp.where(k < samples, cosine((turns - span // 4) & (span - 1), span), 0.0)
    pick = (k >= samples) & (k < samples + BLOCK) & (r == row_at * BLOCK + k - samples)
    pick = jnp.where(pick, 1.0, 0.0)
    turn = jnp.concatenate(
        [
            jnp.concatenate([cos + pick, -sin], axis=1),
            jnp.concatenate([sin, cos + pick], axis=1),
        ],
        axis=0,
    )
    row_high_ref[...], row_low_ref[...] = halves(turn)

    span = OVER * cols
    shape = (samples, 2 * cols)
    q = lax.broadcasted_iota(jnp.int32, shape, 0) + col_at * samples
    k = lax.broadcasted_iota(jnp.int32, shape, 1)
    c = (k // 16) * BLOCK + k % 16 - REACH
    inside = (k % 16 < WIDE) & (c >= 0) & (c < cols)
    turns = (q * c) & (span - 1)
    scale = (rows * cols) ** -0.5
    cos = jnp.where(inside, cosine(turns, span) * scale, 0.0)
    sin = jnp.where(inside, cosine((turns - span // 4) & (span - 1), span) * scale, 0.0)
    turn = jnp.concatenate(
        [jnp.concatenate([cos, sin], axis=1), jnp.concatenate([-sin, cos], axis=1)], axis=0
    )
    col_high_ref[...], col_low_ref[...] = halves(turn)


def stencil_kernel(place, rows, cols, cells_ref, table_ref, row_high_ref, row_low_ref, out_ref, own_ref, coef_ref):
    _, col_at = place()
    across = cells_ref[...].T
    amps = [[across[(x * 4 + s) * 8 : (x * 4 + s) * 8 + 8] for s in range(STATES)] for x in range(2)]
    ports = across[64:72]

    sub = lax.broadcasted_iota(jnp.int32, (8, rows), 0).astype(jnp.float32)
    r = lax.broadcasted_iota(jnp.int32, (8, rows), 1)

    def flag(mask):
        return jnp.where(mask, 1.0, 0.0)

    north, south, north2, south2 = flag(r == 0), flag(r == rows - 1), flag(r == 1), flag(r == rows - 2)
    table = table_ref[...]
    for j in range(BLOCK):
        c = col_at * BLOCK + j
        west, east = flag(c == 0), flag(c == cols - 1)
        west2, east2 = flag(c == 1), flag(c == cols - 2)
        chosen = flag(jnp.broadcast_to(ports[j : j + 1], (8, rows)) == sub)
        at_north, at_south = chosen * north, chosen * south
        kinds = [
            chosen, at_north, at_south, chosen * west, chosen * east,
            chosen * north2, chosen * south2, chosen * west2, chosen * east2,
            at_north * west, at_north * east, at_south * west, at_south * east,
            jnp.zeros((LANES - 8 * CLASSES, rows), jnp.float32),
        ]
        found = dot(table, jnp.concatenate(kinds, axis=0).astype(jnp.bfloat16))
        found = found[0:ROWS] + found[ROWS : 2 * ROWS]
        for half in range(rows // LANES):
            coef_ref[half, j * ROWS : (j + 1) * ROWS, :] = found[:, half * LANES : (half + 1) * LANES]

    def coef(index):
        return jnp.concatenate(
            [coef_ref[half, pl.ds(index, 8, stride=ROWS), :] for half in range(rows // LANES)], axis=1
        )

    def moved(value, dr):
        if dr == 0:
            return value
        value = pltpu.roll(value, dr % rows, axis=1)
        return jnp.where(r >= dr if dr > 0 else r < rows + dr, value, 0.0)

    sums = {}
    for d, (dr, dc) in enumerate(PLACES):
        k_re, k_im = coef(d), coef(13 + d)
        for s in range(STATES):
            a_re, a_im = amps[0][s], amps[1][s]
            for x, value in ((0, k_re * a_re - k_im * a_im), (1, k_re * a_im + k_im * a_re)):
                value = moved(value, dr)
                key = (dc, s, x)
                sums[key] = sums[key] + value if key in sums else value

    spread = jnp.concatenate(
        [
            jnp.concatenate([sums[dc, s, 0], sums[dc, s, 1]], axis=1)
            for dc in range(-2, 3)
            for s in range(STATES)
        ],
        axis=0,
    )
    turned = dot3(halves(spread), (row_high_ref[...], row_low_ref[...]))
    samples = OVER * BLOCK
    lane = lax.broadcasted_iota(jnp.int32, (8, LANES), 1)
    first, second = lane < samples, (lane >= samples) & (lane < samples + BLOCK)
    nothing = jnp.zeros((16, LANES), jnp.float32)
    for x in range(2):
        main, near = nothing, nothing
        for i, dc in enumerate(range(-2, 3)):
            wave, own = jnp.zeros((8, LANES), jnp.float32), jnp.zeros((8, LANES), jnp.float32)
            for s in range(STATES):
                part = turned[(i * STATES + s) * 8 : (i * STATES + s) * 8 + 8, x * LANES : (x + 1) * LANES]
                a, b = jnp.where(first, part, 0.0), jnp.where(second, part, 0.0)
                wave = wave + (pltpu.roll(a, s * samples, axis=1) if s else a)
                own = own + pltpu.roll(b, (s - 1) * samples % LANES, axis=1) if s != 1 else own + b
            for_main = jnp.concatenate([wave, jnp.zeros((8, LANES), jnp.float32)], axis=0)
            for_near = jnp.concatenate([own, jnp.zeros((8, LANES), jnp.float32)], axis=0)
            shift = REACH + dc
            main = main + (pltpu.roll(for_main, shift, axis=0) if shift else for_main)
            near = near + (pltpu.roll(for_near, shift, axis=0) if shift else for_near)
        piece = jnp.concatenate([main[0:12], near[0:2], near[10:12]], axis=0)
        out_ref[:, :, x * LANES : (x + 1) * LANES] = jnp.broadcast_to(piece[None], (out_ref.shape[0], 16, LANES))
        own_ref[:, x * LANES : (x + 1) * LANES] = near


def pattern_kernel(place, blocks, got_ref, own_ref, col_high_ref, col_low_ref, currents_ref, far_ref):
    _, col_at = place()
    samples = OVER * BLOCK
    got = jnp.concatenate(
        [got_ref[:, :, x * LANES : (x + 1) * LANES].reshape(blocks * 16, LANES) for x in range(2)], axis=0
    )
    far = dot3((col_high_ref[...], col_low_ref[...]), halves(got))
    far = jnp.concatenate([far, jnp.zeros_like(far)], axis=0).T
    for x in range(2):
        for s in range(STATES):
            far_ref[x, s] = far[s * samples : (s + 1) * samples, x * samples : (x + 1) * samples]
    left, right = jnp.maximum(col_at - 1, 0), jnp.minimum(col_at + 1, blocks - 1)
    from_left = jnp.where(col_at > 0, 1.0, 0.0) * got_ref[left]
    from_right = jnp.where(col_at < blocks - 1, 1.0, 0.0) * got_ref[right]
    own = own_ref[...]
    whole = jnp.concatenate(
        [own[2:4] + from_left[14:16], own[4:8], own[8:10] + from_right[12:14]], axis=0
    )
    for x in range(2):
        flat = jnp.concatenate([whole[:, x * LANES : (x + 1) * LANES], jnp.zeros((LANES - 8, LANES), jnp.float32)], axis=0).T
        for s in range(STATES):
            currents_ref[x, s] = flat[s * samples : s * samples + BLOCK, 0:BLOCK]


def spot():
    return lax.axis_index("row"), lax.axis_index("col")


def call(kernel, out_shape, scratch=(), flops=0, size=0, **options):
    return pl.pallas_call(
        kernel,
        out_shape=out_shape,
        scratch_shapes=list(scratch),
        compiler_params=pltpu.CompilerParams(vmem_limit_bytes=40 * 1024 * 1024),
        cost_estimate=pl.CostEstimate(flops=flops, bytes_accessed=size, transcendentals=0),
        **options,
    )


def body(row_blocks, col_blocks, place, active_flags, port_index, drive_weights, feed_table, cell_map, probe_weights):
    rows, cols = row_blocks * BLOCK, col_blocks * BLOCK
    samples = OVER * BLOCK
    f32, b16 = jnp.float32, jnp.bfloat16
    shape = jax.ShapeDtypeStruct
    packed = call(pack_kernel, shape((row_blocks, BLOCK, LANES), f32), name="pack")(
        drive_weights, active_flags, port_index
    )
    cells = lax.all_to_all(packed, "row", 0, 0).reshape(rows, LANES)
    table, row_high, row_low, col_high, col_low = call(
        functools.partial(table_kernel, place, rows, cols),
        (
            shape((2 * ROWS, LANES), b16),
            shape((2 * rows, 2 * LANES), b16),
            shape((2 * rows, 2 * LANES), b16),
            shape((2 * samples, 4 * cols), b16),
            shape((2 * samples, 4 * cols), b16),
        ),
        scratch=[pltpu.VMEM((144, cell_map.shape[1]), f32)],
        flops=2 * 80 * 2 * 1024 * 1024,
        size=5 * 1024 * 1024,
        name="tables",
    )(feed_table, cell_map, probe_weights, jnp.asarray(path_matrix()))
    pieces, own = call(
        functools.partial(stencil_kernel, place, rows, cols),
        (shape((col_blocks, 16, 2 * LANES), f32), shape((16, 2 * LANES), f32)),
        scratch=[pltpu.VMEM((rows // LANES, BLOCK * ROWS, LANES), f32)],
        name="stencil",
    )(cells, table, row_high, row_low)
    got = lax.all_to_all(pieces, "col", 0, 0)
    return call(
        functools.partial(pattern_kernel, place, col_blocks),
        (shape((2, STATES, BLOCK, BLOCK), f32), shape((2, STATES, samples, samples), f32)),
        name="pattern",
    )(got, own, col_high, col_low)


def solution(mesh):
    placed = (P("row", "col"), P("row", "col"), P(None, None, "row", "col"), P(), P(), P())
    return jax.shard_map(
        functools.partial(body, mesh.shape["row"], mesh.shape["col"], spot),
        mesh=mesh,
        in_specs=placed,
        out_specs=(P(None, None, "row", "col"), P(None, None, "row", "col")),
        check_vma=False,
    )
```

```python
import functools
import math

import jax
import jax.numpy as jnp
import numpy as np
from jax import lax
from jax.experimental import pallas as pl
from jax.experimental.pallas import tpu as pltpu
from jax.sharding import PartitionSpec as P

OVER = 4
PORTS = 8
STATES = 4
BLOCK = 8
REACH = 2
WIDE = 12
LANES = 128

relaxation = 0.75
reflect_re = -0.3
reflect_im = 0.2

STEP = ((-1, 0), (1, 0), (0, -1), (0, 1))
PLACES = tuple(
    (dr, dc) for dr in range(-2, 3) for dc in range(-2, 3) if abs(dr) + abs(dc) <= 2
)
CLASSES = 13
ROWS = 32


def path_matrix():
    twice = relaxation * relaxation
    once = relaxation * (1.0 - relaxation) + relaxation
    mix = np.zeros((CLASSES * ROWS, 18 * 24), np.float32)

    def add(weight, first, second, place, kind):
        d = PLACES.index(place)
        for part, left, right, sign in ((0, 0, 0, 1), (0, 1, 1, -1), (1, 0, 1, 1), (1, 1, 0, 1)):
            at = 16 + right if second is None else right * 8 + second
            mix[kind * ROWS + part * 13 + d, (first * 2 + left) * 24 + at] += sign * weight

    def corner(e, f):
        return 9 + (min(e, f) % 2) * 2 + (max(e, f) % 2)

    add(1.0, 0, None, (0, 0), 0)
    for e in range(4):
        add(once, 0, e, STEP[e], 0)
        add(once, 0, 4 + e, (0, 0), 1 + e)
        for f in range(4):
            both = (STEP[e][0] + STEP[f][0], STEP[e][1] + STEP[f][1])
            crossed = e // 2 != f // 2
            add(twice, 1 + e, f, both, 0)
            if f == e ^ 1:
                add(-twice, 1 + e, f, both, 1 + e)
            if f != e:
                add(twice, 5 + e, f, STEP[f], 1 + e)
            if f == e:
                add(twice, 1 + e, 4 + f, STEP[e], 5 + e)
                add(twice, 5 + e, 4 + f, (0, 0), 1 + e)
            elif crossed:
                add(twice, 1 + e, 4 + f, STEP[e], 1 + f)
                add(twice, 5 + e, 4 + f, (0, 0), corner(e, f))
    return mix


def halves(value):
    high = value.astype(jnp.bfloat16)
    return high, (value - high.astype(jnp.float32)).astype(jnp.bfloat16)


def thirds(value):
    high, low = halves(value)
    return high, low, (value - high.astype(jnp.float32) - low.astype(jnp.float32)).astype(jnp.bfloat16)


def cosine(turns, length):
    centred = jnp.where(turns >= length // 2, length - turns, turns)
    angle = (length // 4 - centred).astype(jnp.float32) * (2.0 * math.pi / length)
    square = angle * angle
    value = 1.0 / 6227020800.0
    value = value * square - 1.0 / 39916800.0
    value = value * square + 1.0 / 362880.0
    value = value * square - 1.0 / 5040.0
    value = value * square + 1.0 / 120.0
    value = value * square - 1.0 / 6.0
    return angle + angle * square * value


def dot(left, right, dims=((1,), (0,))):
    return lax.dot_general(left, right, (dims, ((), ())), preferred_element_type=jnp.float32)


def dot3(left, right, dims=((1,), (0,))):
    high, low = left
    high_right, low_right = right
    return dot(high, high_right, dims) + (dot(low, high_right, dims) + dot(high, low_right, dims))


def fetch(sems, *pairs, wait=False):
    copies = [pltpu.make_async_copy(src, dst, sems.at[i]) for i, (src, dst) in enumerate(pairs)]
    for copy in copies:
        copy.start()
    if wait:
        for copy in copies:
            copy.wait()
    return copies


def pack_kernel(drive_hbm, flag_hbm, port_hbm, out_ref, drive_ref, flag_ref, port_ref, sems):
    fetch(sems, (drive_hbm, drive_ref), (flag_hbm, flag_ref), (port_hbm, port_ref), wait=True)
    active = flag_ref[...].astype(jnp.float32)
    pieces = [drive_ref[x, s] * active for x in range(2) for s in range(STATES)]
    pieces.append(port_ref[...].astype(jnp.float32))
    pieces.append(jnp.zeros((BLOCK, LANES - 9 * BLOCK), jnp.float32))
    packed = jnp.concatenate(pieces, axis=1)
    out_ref[...] = jnp.broadcast_to(packed[None], out_ref.shape)


def twiddles(place, rows, cols, row_high_ref, row_low_ref, col_high_ref, col_low_ref):
    row_at, col_at = place()
    span = OVER * rows
    r = lax.broadcasted_iota(jnp.int32, (rows, LANES), 0)
    k = lax.broadcasted_iota(jnp.int32, (rows, LANES), 1)
    samples = OVER * BLOCK
    turns = (r * (row_at * samples + k)) & (span - 1)
    cos = jnp.where(k < samples, cosine(turns, span), 0.0)
    sin = jnp.where(k < samples, cosine((turns - span // 4) & (span - 1), span), 0.0)
    pick = (k >= samples) & (k < samples + BLOCK) & (r == row_at * BLOCK + k - samples)
    pick = jnp.where(pick, 1.0, 0.0)
    turn = jnp.concatenate(
        [
            jnp.concatenate([cos + pick, -sin], axis=1),
            jnp.concatenate([sin, cos + pick], axis=1),
        ],
        axis=0,
    )
    row_high_ref[...], row_low_ref[...] = halves(turn)

    span = OVER * cols
    shape = (samples, 2 * cols)
    q = lax.broadcasted_iota(jnp.int32, shape, 0) + col_at * samples
    k = lax.broadcasted_iota(jnp.int32, shape, 1)
    c = (k // 16) * BLOCK + k % 16 - REACH
    inside = (k % 16 < WIDE) & (c >= 0) & (c < cols)
    turns = (q * c) & (span - 1)
    scale = (rows * cols) ** -0.5
    cos = jnp.where(inside, cosine(turns, span) * scale, 0.0)
    sin = jnp.where(inside, cosine((turns - span // 4) & (span - 1), span) * scale, 0.0)
    turn = jnp.concatenate(
        [jnp.concatenate([cos, sin], axis=1), jnp.concatenate([-sin, cos], axis=1)], axis=0
    )
    col_high_ref[...], col_low_ref[...] = halves(turn)


def table_kernel(
    place, rows, cols, feed_hbm, map_hbm, probe_hbm, mix_hbm,
    table_ref, row_high_ref, row_low_ref, col_high_ref, col_low_ref,
    feed_ref, map_ref, probe_ref, mix_ref, hops_ref, sems,
):
    edge = feed_ref.shape[2] // 4
    chunks = [(map_hbm.at[:, pl.ds(a * edge, edge)], map_ref.at[:, pl.ds(a * edge, edge)]) for a in range(4)]
    copies = fetch(sems, (feed_hbm, feed_ref), (probe_hbm, probe_ref), *chunks, (mix_hbm, mix_ref))
    twiddles(place, rows, cols, row_high_ref, row_low_ref, col_high_ref, col_low_ref)
    copies[0].wait()
    copies[1].wait()
    units = 4 * edge

    def block(value, e):
        return value[:, e * edge : (e + 1) * edge]

    feed_re, feed_im = feed_ref[0], feed_ref[1]
    back_re = reflect_re * feed_re - reflect_im * feed_im
    back_im = reflect_re * feed_im + reflect_im * feed_re
    hops_ref[0:8, :] = feed_re
    hops_ref[8:16, :] = feed_im
    for a in range(4):
        e = a ^ 1
        enter = jnp.concatenate(
            [block(feed_re, e), block(feed_im, e), block(back_re, a), block(back_im, a)], axis=0
        )
        enter = jnp.concatenate(halves(enter), axis=0)
        copies[2 + a].wait()
        by_re = dot(enter, map_ref[0, a * edge : (a + 1) * edge, :])
        by_im = dot(enter, map_ref[1, a * edge : (a + 1) * edge, :])
        by_re = by_re[0:32] + by_re[32:64]
        by_im = by_im[0:32] + by_im[32:64]
        for first, at in ((1 + e, 0), (5 + a, 16)):
            hops_ref[first * 16 : first * 16 + 8, :] = by_re[at : at + 8] - by_im[at + 8 : at + 16]
            hops_ref[first * 16 + 8 : first * 16 + 16, :] = (
                by_re[at + 8 : at + 16] + by_im[at : at + 8]
            )
    probe_re, probe_im = probe_ref[0:1, :], probe_ref[1:2, :]
    probes = jnp.concatenate(halves(jnp.concatenate([probe_re, probe_im] + [probe_re] * 6, axis=0)), axis=0)
    through_re = dot(probes, map_ref[0], ((1,), (1,)))
    through_im = dot(probes, map_ref[1], ((1,), (1,)))
    through_re = through_re[0:8] + through_re[8:16]
    through_im = through_im[0:8] + through_im[8:16]
    total_re = probe_re + through_re[0:1] - through_im[1:2]
    total_im = probe_im + through_im[0:1] + through_re[1:2]

    def swapped(value):
        return jnp.concatenate([block(value, e ^ 1) for e in range(4)], axis=1)

    sub = lax.broadcasted_iota(jnp.int32, (8, units), 0)
    lane = lax.broadcasted_iota(jnp.int32, (8, units), 1)
    own = lane // edge == sub % 4
    passed = sub < 4
    out_re = jnp.where(passed, swapped(total_re), reflect_re * total_re - reflect_im * total_im)
    out_im = jnp.where(passed, swapped(total_im), reflect_re * total_im + reflect_im * total_re)
    leave = jnp.concatenate(
        [
            jnp.where(own, out_re, 0.0),
            jnp.where(own, out_im, 0.0),
            jnp.where(sub == 0, probe_re, jnp.where(sub == 1, probe_im, 0.0)),
        ],
        axis=0,
    )
    products = dot3(halves(leave), halves(hops_ref[...]), ((1,), (1,)))
    copies[6].wait()
    flat = jnp.concatenate([products[:, 8 * k : 8 * k + 8] for k in range(18)], axis=0)
    table = dot(mix_ref[...], jnp.concatenate(thirds(flat), axis=1))
    table = table[:, 0:8] + table[:, 8:16] + table[:, 16:24]
    wide = [table[k * ROWS : (k + 1) * ROWS, :] for k in range(CLASSES)]
    wide.append(jnp.zeros((ROWS, LANES - 8 * CLASSES), jnp.float32))
    table_ref[...] = jnp.concatenate(halves(jnp.concatenate(wide, axis=1)), axis=0)


def stencil_kernel(place, rows, cols, cells_ref, table_ref, row_high_ref, row_low_ref, out_ref, own_ref, coef_ref):
    _, col_at = place()
    across = cells_ref[...].T
    amps = [[across[(x * 4 + s) * 8 : (x * 4 + s) * 8 + 8] for s in range(STATES)] for x in range(2)]
    ports = across[64:72]

    sub = lax.broadcasted_iota(jnp.int32, (8, rows), 0).astype(jnp.float32)
    r = lax.broadcasted_iota(jnp.int32, (8, rows), 1)

    def flag(mask):
        return jnp.where(mask, 1.0, 0.0)

    north, south, north2, south2 = flag(r == 0), flag(r == rows - 1), flag(r == 1), flag(r == rows - 2)
    table = table_ref[...]
    for j in range(BLOCK):
        c = col_at * BLOCK + j
        west, east = flag(c == 0), flag(c == cols - 1)
        west2, east2 = flag(c == 1), flag(c == cols - 2)
        chosen = flag(jnp.broadcast_to(ports[j : j + 1], (8, rows)) == sub)
        at_north, at_south = chosen * north, chosen * south
        kinds = [
            chosen, at_north, at_south, chosen * west, chosen * east,
            chosen * north2, chosen * south2, chosen * west2, chosen * east2,
            at_north * west, at_north * east, at_south * west, at_south * east,
            jnp.zeros((LANES - 8 * CLASSES, rows), jnp.float32),
        ]
        found = dot(table, jnp.concatenate(kinds, axis=0).astype(jnp.bfloat16))
        found = found[0:ROWS] + found[ROWS : 2 * ROWS]
        for half in range(rows // LANES):
            coef_ref[half, j * ROWS : (j + 1) * ROWS, :] = found[:, half * LANES : (half + 1) * LANES]

    def coef(index):
        return jnp.concatenate(
            [coef_ref[half, pl.ds(index, 8, stride=ROWS), :] for half in range(rows // LANES)], axis=1
        )

    def moved(value, dr):
        if dr == 0:
            return value
        value = pltpu.roll(value, dr % rows, axis=1)
        return jnp.where(r >= dr if dr > 0 else r < rows + dr, value, 0.0)

    sums = {}
    for d, (dr, dc) in enumerate(PLACES):
        k_re, k_im = coef(d), coef(13 + d)
        for s in range(STATES):
            a_re, a_im = amps[0][s], amps[1][s]
            for x, value in ((0, k_re * a_re - k_im * a_im), (1, k_re * a_im + k_im * a_re)):
                value = moved(value, dr)
                key = (dc, s, x)
                sums[key] = sums[key] + value if key in sums else value

    spread = jnp.concatenate(
        [
            jnp.concatenate([sums[dc, s, 0], sums[dc, s, 1]], axis=1)
            for dc in range(-2, 3)
            for s in range(STATES)
        ],
        axis=0,
    )
    turned = dot3(halves(spread), (row_high_ref[...], row_low_ref[...]))
    samples = OVER * BLOCK
    lane = lax.broadcasted_iota(jnp.int32, (8, LANES), 1)
    first, second = lane < samples, (lane >= samples) & (lane < samples + BLOCK)
    nothing = jnp.zeros((16, LANES), jnp.float32)
    for x in range(2):
        main, near = nothing, nothing
        for i, dc in enumerate(range(-2, 3)):
            wave, own = jnp.zeros((8, LANES), jnp.float32), jnp.zeros((8, LANES), jnp.float32)
            for s in range(STATES):
                part = turned[(i * STATES + s) * 8 : (i * STATES + s) * 8 + 8, x * LANES : (x + 1) * LANES]
                a, b = jnp.where(first, part, 0.0), jnp.where(second, part, 0.0)
                wave = wave + (pltpu.roll(a, s * samples, axis=1) if s else a)
                own = own + pltpu.roll(b, (s - 1) * samples % LANES, axis=1) if s != 1 else own + b
            for_main = jnp.concatenate([wave, jnp.zeros((8, LANES), jnp.float32)], axis=0)
            for_near = jnp.concatenate([own, jnp.zeros((8, LANES), jnp.float32)], axis=0)
            shift = REACH + dc
            main = main + (pltpu.roll(for_main, shift, axis=0) if shift else for_main)
            near = near + (pltpu.roll(for_near, shift, axis=0) if shift else for_near)
        piece = jnp.concatenate([main[0:12], near[0:2], near[10:12]], axis=0)
        out_ref[:, :, x * LANES : (x + 1) * LANES] = jnp.broadcast_to(piece[None], (out_ref.shape[0], 16, LANES))
        own_ref[:, x * LANES : (x + 1) * LANES] = near


def pattern_kernel(place, blocks, got_ref, own_ref, col_high_ref, col_low_ref, currents_ref, far_ref):
    _, col_at = place()
    samples = OVER * BLOCK
    got = jnp.concatenate(
        [got_ref[:, :, x * LANES : (x + 1) * LANES].reshape(blocks * 16, LANES) for x in range(2)], axis=0
    )
    far = dot3((col_high_ref[...], col_low_ref[...]), halves(got))
    far = jnp.concatenate([far, jnp.zeros_like(far)], axis=0).T
    for x in range(2):
        for s in range(STATES):
            far_ref[x, s] = far[s * samples : (s + 1) * samples, x * samples : (x + 1) * samples]
    left, right = jnp.maximum(col_at - 1, 0), jnp.minimum(col_at + 1, blocks - 1)
    from_left = jnp.where(col_at > 0, 1.0, 0.0) * got_ref[left]
    from_right = jnp.where(col_at < blocks - 1, 1.0, 0.0) * got_ref[right]
    own = own_ref[...]
    whole = jnp.concatenate(
        [own[2:4] + from_left[14:16], own[4:8], own[8:10] + from_right[12:14]], axis=0
    )
    for x in range(2):
        flat = jnp.concatenate([whole[:, x * LANES : (x + 1) * LANES], jnp.zeros((LANES - 8, LANES), jnp.float32)], axis=0).T
        for s in range(STATES):
            currents_ref[x, s] = flat[s * samples : s * samples + BLOCK, 0:BLOCK]


def spot():
    return lax.axis_index("row"), lax.axis_index("col")


HBM = pl.BlockSpec(memory_space=pltpu.HBM)


def call(kernel, out_shape, scratch=(), flops=0, size=0, grant=40960, **options):
    return pl.pallas_call(
        kernel,
        out_shape=out_shape,
        scratch_shapes=list(scratch),
        compiler_params=pltpu.CompilerParams(vmem_limit_bytes=grant * 1024),
        cost_estimate=pl.CostEstimate(flops=flops, bytes_accessed=size, transcendentals=0),
        **options,
    )


def body(row_blocks, col_blocks, place, active_flags, port_index, drive_weights, feed_table, cell_map, probe_weights):
    rows, cols = row_blocks * BLOCK, col_blocks * BLOCK
    samples = OVER * BLOCK
    f32, b16 = jnp.float32, jnp.bfloat16
    shape = jax.ShapeDtypeStruct
    taken = (drive_weights, active_flags, port_index)
    packed = call(
        pack_kernel,
        shape((row_blocks, BLOCK, LANES), f32),
        scratch=[pltpu.VMEM(x.shape, x.dtype) for x in taken] + [pltpu.SemaphoreType.DMA((3,))],
        in_specs=[HBM] * 3,
        name="pack",
        grant=61440,
    )(*taken)
    cells = lax.all_to_all(packed, "row", 0, 0).reshape(rows, LANES)
    taken = (feed_table, cell_map, probe_weights, jnp.asarray(path_matrix(), b16))
    table, row_high, row_low, col_high, col_low = call(
        functools.partial(table_kernel, place, rows, cols),
        (
            shape((2 * ROWS, LANES), b16),
            shape((2 * rows, 2 * LANES), b16),
            shape((2 * rows, 2 * LANES), b16),
            shape((2 * samples, 4 * cols), b16),
            shape((2 * samples, 4 * cols), b16),
        ),
        scratch=[pltpu.VMEM(x.shape, x.dtype) for x in taken]
        + [pltpu.VMEM((144, cell_map.shape[1]), f32), pltpu.SemaphoreType.DMA((7,))],
        in_specs=[HBM] * 4,
        flops=2 * 80 * 2 * 1024 * 1024,
        size=5 * 1024 * 1024,
        name="tables",
        grant=54272,
    )(*taken)
    pieces, own = call(
        functools.partial(stencil_kernel, place, rows, cols),
        (shape((col_blocks, 16, 2 * LANES), f32), shape((16, 2 * LANES), f32)),
        scratch=[pltpu.VMEM((rows // LANES, BLOCK * ROWS, LANES), f32)],
        name="stencil",
    )(cells, table, row_high, row_low)
    got = lax.all_to_all(pieces, "col", 0, 0)
    return call(
        functools.partial(pattern_kernel, place, col_blocks),
        (shape((2, STATES, BLOCK, BLOCK), f32), shape((2, STATES, samples, samples), f32)),
        name="pattern",
    )(got, own, col_high, col_low)


def solution(mesh):
    placed = (P("row", "col"), P("row", "col"), P(None, None, "row", "col"), P(), P(), P())
    return jax.shard_map(
        functools.partial(body, mesh.shape["row"], mesh.shape["col"], spot),
        mesh=mesh,
        in_specs=placed,
        out_specs=(P(None, None, "row", "col"), P(None, None, "row", "col")),
        check_vma=False,
    )
```

```python
import functools
import math

import jax
import jax.numpy as jnp
import numpy as np
from jax import lax
from jax.experimental import pallas as pl
from jax.experimental.pallas import tpu as pltpu
from jax.sharding import PartitionSpec as P

OVER = 4
PORTS = 8
STATES = 4
BLOCK = 8
REACH = 2
WIDE = 12
LANES = 128
USED = 72

relaxation = 0.75
reflect_re = -0.3
reflect_im = 0.2

STEP = ((-1, 0), (1, 0), (0, -1), (0, 1))
PLACES = tuple(
    (dr, dc) for dr in range(-2, 3) for dc in range(-2, 3) if abs(dr) + abs(dc) <= 2
)
CLASSES = 13
SHARE = 52
ROWS = 32


def path_matrix():
    twice = relaxation * relaxation
    once = relaxation * (1.0 - relaxation) + relaxation
    mix = np.zeros((CLASSES * ROWS, 18 * 24), np.float32)

    def add(weight, first, second, place, kind):
        d = PLACES.index(place)
        for part, left, right, sign in ((0, 0, 0, 1), (0, 1, 1, -1), (1, 0, 1, 1), (1, 1, 0, 1)):
            at = 16 + right if second is None else right * 8 + second
            mix[kind * ROWS + part * 13 + d, (first * 2 + left) * 24 + at] += sign * weight

    def corner(e, f):
        return 9 + (min(e, f) % 2) * 2 + (max(e, f) % 2)

    add(1.0, 0, None, (0, 0), 0)
    for e in range(4):
        add(once, 0, e, STEP[e], 0)
        add(once, 0, 4 + e, (0, 0), 1 + e)
        for f in range(4):
            both = (STEP[e][0] + STEP[f][0], STEP[e][1] + STEP[f][1])
            crossed = e // 2 != f // 2
            add(twice, 1 + e, f, both, 0)
            if f == e ^ 1:
                add(-twice, 1 + e, f, both, 1 + e)
            if f != e:
                add(twice, 5 + e, f, STEP[f], 1 + e)
            if f == e:
                add(twice, 1 + e, 4 + f, STEP[e], 5 + e)
                add(twice, 5 + e, 4 + f, (0, 0), 1 + e)
            elif crossed:
                add(twice, 1 + e, 4 + f, STEP[e], 1 + f)
                add(twice, 5 + e, 4 + f, (0, 0), corner(e, f))
    return mix


def halves(value):
    high = value.astype(jnp.bfloat16)
    return high, (value - high.astype(jnp.float32)).astype(jnp.bfloat16)


def thirds(value):
    high, low = halves(value)
    return high, low, (value - high.astype(jnp.float32) - low.astype(jnp.float32)).astype(jnp.bfloat16)


def cosine(turns, length):
    centred = jnp.where(turns >= length // 2, length - turns, turns)
    angle = (length // 4 - centred).astype(jnp.float32) * (2.0 * math.pi / length)
    square = angle * angle
    value = 1.0 / 6227020800.0
    value = value * square - 1.0 / 39916800.0
    value = value * square + 1.0 / 362880.0
    value = value * square - 1.0 / 5040.0
    value = value * square + 1.0 / 120.0
    value = value * square - 1.0 / 6.0
    return angle + angle * square * value


def dot(left, right, dims=((1,), (0,))):
    return lax.dot_general(left, right, (dims, ((), ())), preferred_element_type=jnp.float32)


def dot3(left, right, dims=((1,), (0,))):
    high, low = left
    high_right, low_right = right
    return dot(high, high_right, dims) + (dot(low, high_right, dims) + dot(high, low_right, dims))


def fetch(sems, *pairs, wait=False):
    copies = [pltpu.make_async_copy(src, dst, sems.at[i]) for i, (src, dst) in enumerate(pairs)]
    for copy in copies:
        copy.start()
    if wait:
        for copy in copies:
            copy.wait()
    return copies


def turn_kernel(place, rows, cols, row_high_ref, row_low_ref, col_high_ref, col_low_ref):
    row_at, col_at = place()
    span = OVER * rows
    r = lax.broadcasted_iota(jnp.int32, (rows, LANES), 0)
    k = lax.broadcasted_iota(jnp.int32, (rows, LANES), 1)
    samples = OVER * BLOCK
    turns = (r * (row_at * samples + k)) & (span - 1)
    cos = jnp.where(k < samples, cosine(turns, span), 0.0)
    sin = jnp.where(k < samples, cosine((turns - span // 4) & (span - 1), span), 0.0)
    pick = (k >= samples) & (k < samples + BLOCK) & (r == row_at * BLOCK + k - samples)
    pick = jnp.where(pick, 1.0, 0.0)
    turn = jnp.concatenate(
        [
            jnp.concatenate([cos + pick, -sin], axis=1),
            jnp.concatenate([sin, cos + pick], axis=1),
        ],
        axis=0,
    )
    row_high_ref[...], row_low_ref[...] = halves(turn)

    span = OVER * cols
    shape = (samples, 2 * cols)
    q = lax.broadcasted_iota(jnp.int32, shape, 0) + col_at * samples
    k = lax.broadcasted_iota(jnp.int32, shape, 1)
    c = (k // 16) * BLOCK + k % 16 - REACH
    inside = (k % 16 < WIDE) & (c >= 0) & (c < cols)
    turns = (q * c) & (span - 1)
    scale = (rows * cols) ** -0.5
    cos = jnp.where(inside, cosine(turns, span) * scale, 0.0)
    sin = jnp.where(inside, cosine((turns - span // 4) & (span - 1), span) * scale, 0.0)
    turn = jnp.concatenate(
        [jnp.concatenate([cos, sin], axis=1), jnp.concatenate([-sin, cos], axis=1)], axis=0
    )
    col_high_ref[...], col_low_ref[...] = halves(turn)


def make_table(feed_hbm, map_hbm, probe_hbm, mix_hbm, table_ref, feed_ref, map_ref, probe_ref, mix_ref, hops_ref, sems):
    edge = feed_ref.shape[2] // 4
    chunks = [(map_hbm.at[:, pl.ds(a * edge, edge)], map_ref.at[:, pl.ds(a * edge, edge)]) for a in range(4)]
    copies = fetch(sems, (feed_hbm, feed_ref), (probe_hbm, probe_ref), *chunks, (mix_hbm, mix_ref))
    copies[0].wait()
    copies[1].wait()
    units = 4 * edge

    def block(value, e):
        return value[:, e * edge : (e + 1) * edge]

    feed_re, feed_im = feed_ref[0], feed_ref[1]
    back_re = reflect_re * feed_re - reflect_im * feed_im
    back_im = reflect_re * feed_im + reflect_im * feed_re
    hops_ref[0:8, :] = feed_re
    hops_ref[8:16, :] = feed_im
    for a in range(4):
        e = a ^ 1
        enter = jnp.concatenate(
            [block(feed_re, e), block(feed_im, e), block(back_re, a), block(back_im, a)], axis=0
        )
        enter = jnp.concatenate(halves(enter), axis=0)
        copies[2 + a].wait()
        by_re = dot(enter, map_ref[0, a * edge : (a + 1) * edge, :])
        by_im = dot(enter, map_ref[1, a * edge : (a + 1) * edge, :])
        by_re = by_re[0:32] + by_re[32:64]
        by_im = by_im[0:32] + by_im[32:64]
        for first, at in ((1 + e, 0), (5 + a, 16)):
            hops_ref[first * 16 : first * 16 + 8, :] = by_re[at : at + 8] - by_im[at + 8 : at + 16]
            hops_ref[first * 16 + 8 : first * 16 + 16, :] = (
                by_re[at + 8 : at + 16] + by_im[at : at + 8]
            )
    probe_re, probe_im = probe_ref[0:1, :], probe_ref[1:2, :]
    probes = jnp.concatenate(halves(jnp.concatenate([probe_re, probe_im] + [probe_re] * 6, axis=0)), axis=0)
    through_re = dot(probes, map_ref[0], ((1,), (1,)))
    through_im = dot(probes, map_ref[1], ((1,), (1,)))
    through_re = through_re[0:8] + through_re[8:16]
    through_im = through_im[0:8] + through_im[8:16]
    total_re = probe_re + through_re[0:1] - through_im[1:2]
    total_im = probe_im + through_im[0:1] + through_re[1:2]

    def swapped(value):
        return jnp.concatenate([block(value, e ^ 1) for e in range(4)], axis=1)

    sub = lax.broadcasted_iota(jnp.int32, (8, units), 0)
    lane = lax.broadcasted_iota(jnp.int32, (8, units), 1)
    own = lane // edge == sub % 4
    passed = sub < 4
    out_re = jnp.where(passed, swapped(total_re), reflect_re * total_re - reflect_im * total_im)
    out_im = jnp.where(passed, swapped(total_im), reflect_re * total_im + reflect_im * total_re)
    leave = jnp.concatenate(
        [
            jnp.where(own, out_re, 0.0),
            jnp.where(own, out_im, 0.0),
            jnp.where(sub == 0, probe_re, jnp.where(sub == 1, probe_im, 0.0)),
        ],
        axis=0,
    )
    products = dot3(halves(leave), halves(hops_ref[...]), ((1,), (1,)))
    copies[6].wait()
    flat = jnp.concatenate([products[:, 8 * k : 8 * k + 8] for k in range(18)], axis=0)
    table = dot(mix_ref[...], jnp.concatenate(thirds(flat), axis=1))
    table = table[:, 0:8] + table[:, 8:16] + table[:, 16:24]
    wide = [table[k * ROWS : (k + 1) * ROWS, :] for k in range(CLASSES)]
    wide.append(jnp.zeros((ROWS, LANES - 8 * CLASSES), jnp.float32))
    table_ref[...] = jnp.concatenate(wide, axis=1)


def maker(row_at):
    return row_at % 16 < 4, row_at % 4 + 4 * (row_at // 16)


def pack_kernel(
    place, drive_hbm, flag_hbm, port_hbm, feed_hbm, map_hbm, probe_hbm, mix_hbm, out_ref,
    drive_ref, flag_ref, port_ref, feed_ref, map_ref, probe_ref, mix_ref, hops_ref, table_ref, piece_ref, sems, table_sems,
):
    makes, share = maker(place()[0])
    fetch(sems, (drive_hbm, drive_ref), (flag_hbm, flag_ref), (port_hbm, port_ref), wait=True)
    active = flag_ref[...].astype(jnp.float32)
    pieces = [drive_ref[x, s] * active for x in range(2) for s in range(STATES)]
    pieces.append(port_ref[...].astype(jnp.float32))
    pieces.append(jnp.zeros((BLOCK, LANES - USED), jnp.float32))
    piece_ref[...] = jnp.concatenate(pieces, axis=1)

    @pl.when(makes)
    def _():
        make_table(
            feed_hbm, map_hbm, probe_hbm, mix_hbm, table_ref,
            feed_ref, map_ref, probe_ref, mix_ref, hops_ref, table_sems,
        )
        part = table_ref[pl.ds(pl.multiple_of(share // 2 * 8, 8), 8), :]
        part = jnp.where(share % 2 == 0, pltpu.roll(part, USED, axis=1), pltpu.roll(part, USED - SHARE, axis=1))
        lane = lax.broadcasted_iota(jnp.int32, (BLOCK, LANES), 1)
        piece_ref[...] += jnp.where((lane >= USED) & (lane < USED + SHARE), part, 0.0)

    out_ref[...] = jnp.broadcast_to(piece_ref[...][None], out_ref.shape)


def stencil_kernel(place, rows, cols, cells_ref, row_high_ref, row_low_ref, out_ref, own_ref, coef_ref):
    _, col_at = place()
    across = cells_ref[...].T
    amps = [[across[(x * 4 + s) * 8 : (x * 4 + s) * 8 + 8] for s in range(STATES)] for x in range(2)]
    ports = across[64:72]

    sub = lax.broadcasted_iota(jnp.int32, (8, rows), 0).astype(jnp.float32)
    r = lax.broadcasted_iota(jnp.int32, (8, rows), 1)

    def flag(mask):
        return jnp.where(mask, 1.0, 0.0)

    north, south, north2, south2 = flag(r == 0), flag(r == rows - 1), flag(r == 1), flag(r == rows - 2)
    lane = lax.broadcasted_iota(jnp.int32, (BLOCK, LANES), 1)
    parts = [cells_ref[(k % 4 + 16 * (k // 4)) * BLOCK : (k % 4 + 16 * (k // 4) + 1) * BLOCK, :] for k in range(8)]
    firsts = [jnp.where(lane < SHARE, pltpu.roll(part, LANES - USED, axis=1), 0.0) for part in parts[0::2]]
    seconds = [
        jnp.where((lane >= SHARE) & (lane < 2 * SHARE), pltpu.roll(part, LANES - USED + SHARE, axis=1), 0.0)
        for part in parts[1::2]
    ]
    table = jnp.concatenate(halves(jnp.concatenate([a + b for a, b in zip(firsts, seconds)], axis=0)), axis=0)
    for j in range(BLOCK):
        c = col_at * BLOCK + j
        west, east = flag(c == 0), flag(c == cols - 1)
        west2, east2 = flag(c == 1), flag(c == cols - 2)
        chosen = flag(jnp.broadcast_to(ports[j : j + 1], (8, rows)) == sub)
        at_north, at_south = chosen * north, chosen * south
        kinds = [
            chosen, at_north, at_south, chosen * west, chosen * east,
            chosen * north2, chosen * south2, chosen * west2, chosen * east2,
            at_north * west, at_north * east, at_south * west, at_south * east,
            jnp.zeros((LANES - 8 * CLASSES, rows), jnp.float32),
        ]
        found = dot(table, jnp.concatenate(kinds, axis=0).astype(jnp.bfloat16))
        found = found[0:ROWS] + found[ROWS : 2 * ROWS]
        for half in range(rows // LANES):
            coef_ref[half, j * ROWS : (j + 1) * ROWS, :] = found[:, half * LANES : (half + 1) * LANES]

    def coef(index):
        return jnp.concatenate(
            [coef_ref[half, pl.ds(index, 8, stride=ROWS), :] for half in range(rows // LANES)], axis=1
        )

    def moved(value, dr):
        if dr == 0:
            return value
        value = pltpu.roll(value, dr % rows, axis=1)
        return jnp.where(r >= dr if dr > 0 else r < rows + dr, value, 0.0)

    sums = {}
    for d, (dr, dc) in enumerate(PLACES):
        k_re, k_im = coef(d), coef(13 + d)
        for s in range(STATES):
            a_re, a_im = amps[0][s], amps[1][s]
            for x, value in ((0, k_re * a_re - k_im * a_im), (1, k_re * a_im + k_im * a_re)):
                value = moved(value, dr)
                key = (dc, s, x)
                sums[key] = sums[key] + value if key in sums else value

    spread = jnp.concatenate(
        [
            jnp.concatenate([sums[dc, s, 0], sums[dc, s, 1]], axis=1)
            for dc in range(-2, 3)
            for s in range(STATES)
        ],
        axis=0,
    )
    turned = dot3(halves(spread), (row_high_ref[...], row_low_ref[...]))
    samples = OVER * BLOCK
    lane = lax.broadcasted_iota(jnp.int32, (8, LANES), 1)
    first, second = lane < samples, (lane >= samples) & (lane < samples + BLOCK)
    nothing = jnp.zeros((16, LANES), jnp.float32)
    for x in range(2):
        main, near = nothing, nothing
        for i, dc in enumerate(range(-2, 3)):
            wave, own = jnp.zeros((8, LANES), jnp.float32), jnp.zeros((8, LANES), jnp.float32)
            for s in range(STATES):
                part = turned[(i * STATES + s) * 8 : (i * STATES + s) * 8 + 8, x * LANES : (x + 1) * LANES]
                a, b = jnp.where(first, part, 0.0), jnp.where(second, part, 0.0)
                wave = wave + (pltpu.roll(a, s * samples, axis=1) if s else a)
                own = own + pltpu.roll(b, (s - 1) * samples % LANES, axis=1) if s != 1 else own + b
            for_main = jnp.concatenate([wave, jnp.zeros((8, LANES), jnp.float32)], axis=0)
            for_near = jnp.concatenate([own, jnp.zeros((8, LANES), jnp.float32)], axis=0)
            shift = REACH + dc
            main = main + (pltpu.roll(for_main, shift, axis=0) if shift else for_main)
            near = near + (pltpu.roll(for_near, shift, axis=0) if shift else for_near)
        piece = jnp.concatenate([main[0:12], near[0:2], near[10:12]], axis=0)
        out_ref[:, :, x * LANES : (x + 1) * LANES] = jnp.broadcast_to(piece[None], (out_ref.shape[0], 16, LANES))
        own_ref[:, x * LANES : (x + 1) * LANES] = near


def pattern_kernel(place, blocks, got_ref, own_ref, col_high_ref, col_low_ref, currents_ref, far_ref):
    _, col_at = place()
    samples = OVER * BLOCK
    got = jnp.concatenate(
        [got_ref[:, :, x * LANES : (x + 1) * LANES].reshape(blocks * 16, LANES) for x in range(2)], axis=0
    )
    far = dot3((col_high_ref[...], col_low_ref[...]), halves(got))
    far = jnp.concatenate([far, jnp.zeros_like(far)], axis=0).T
    for x in range(2):
        for s in range(STATES):
            far_ref[x, s] = far[s * samples : (s + 1) * samples, x * samples : (x + 1) * samples]
    left, right = jnp.maximum(col_at - 1, 0), jnp.minimum(col_at + 1, blocks - 1)
    from_left = jnp.where(col_at > 0, 1.0, 0.0) * got_ref[left]
    from_right = jnp.where(col_at < blocks - 1, 1.0, 0.0) * got_ref[right]
    own = own_ref[...]
    whole = jnp.concatenate(
        [own[2:4] + from_left[14:16], own[4:8], own[8:10] + from_right[12:14]], axis=0
    )
    for x in range(2):
        flat = jnp.concatenate([whole[:, x * LANES : (x + 1) * LANES], jnp.zeros((LANES - 8, LANES), jnp.float32)], axis=0).T
        for s in range(STATES):
            currents_ref[x, s] = flat[s * samples : s * samples + BLOCK, 0:BLOCK]


def spot():
    return lax.axis_index("row"), lax.axis_index("col")


HBM = pl.BlockSpec(memory_space=pltpu.HBM)


def call(kernel, out_shape, scratch=(), flops=0, size=0, grant=40960, **options):
    return pl.pallas_call(
        kernel,
        out_shape=out_shape,
        scratch_shapes=list(scratch),
        compiler_params=pltpu.CompilerParams(vmem_limit_bytes=grant * 1024),
        cost_estimate=pl.CostEstimate(flops=flops, bytes_accessed=size, transcendentals=0),
        **options,
    )


def body(row_blocks, col_blocks, place, active_flags, port_index, drive_weights, feed_table, cell_map, probe_weights):
    rows, cols = row_blocks * BLOCK, col_blocks * BLOCK
    samples = OVER * BLOCK
    f32, b16 = jnp.float32, jnp.bfloat16
    shape = jax.ShapeDtypeStruct
    taken = (
        drive_weights, active_flags, port_index,
        feed_table, cell_map, probe_weights, jnp.asarray(path_matrix(), b16),
    )
    packed = call(
        functools.partial(pack_kernel, place),
        shape((row_blocks, BLOCK, LANES), f32),
        scratch=[pltpu.VMEM(x.shape, x.dtype) for x in taken]
        + [
            pltpu.VMEM((144, cell_map.shape[1]), f32),
            pltpu.VMEM((ROWS, LANES), f32),
            pltpu.VMEM((BLOCK, LANES), f32),
            pltpu.SemaphoreType.DMA((3,)),
            pltpu.SemaphoreType.DMA((7,)),
        ],
        in_specs=[HBM] * 7,
        name="pack",
        grant=61440,
    )(*taken)
    cells = lax.all_to_all(packed, "row", 0, 0).reshape(rows, LANES)
    row_high, row_low, col_high, col_low = call(
        functools.partial(turn_kernel, place, rows, cols),
        (
            shape((2 * rows, 2 * LANES), b16),
            shape((2 * rows, 2 * LANES), b16),
            shape((2 * samples, 4 * cols), b16),
            shape((2 * samples, 4 * cols), b16),
        ),
        flops=2 * 80 * 2 * 1024 * 1024,
        size=5 * 1024 * 1024,
        name="turns",
    )()
    pieces, own = call(
        functools.partial(stencil_kernel, place, rows, cols),
        (shape((col_blocks, 16, 2 * LANES), f32), shape((16, 2 * LANES), f32)),
        scratch=[pltpu.VMEM((rows // LANES, BLOCK * ROWS, LANES), f32)],
        name="stencil",
    )(cells, row_high, row_low)
    got = lax.all_to_all(pieces, "col", 0, 0)
    return call(
        functools.partial(pattern_kernel, place, col_blocks),
        (shape((2, STATES, BLOCK, BLOCK), f32), shape((2, STATES, samples, samples), f32)),
        name="pattern",
    )(got, own, col_high, col_low)


def solution(mesh):
    placed = (P("row", "col"), P("row", "col"), P(None, None, "row", "col"), P(), P(), P())
    return jax.shard_map(
        functools.partial(body, mesh.shape["row"], mesh.shape["col"], spot),
        mesh=mesh,
        in_specs=placed,
        out_specs=(P(None, None, "row", "col"), P(None, None, "row", "col")),
        check_vma=False,
    )
```

```python
import functools
import math

import jax
import jax.numpy as jnp
import numpy as np
from jax import lax
from jax.experimental import pallas as pl
from jax.experimental.pallas import tpu as pltpu
from jax.sharding import PartitionSpec as P

OVER = 4
PORTS = 8
STATES = 4
BLOCK = 8
REACH = 2
WIDE = 12
LANES = 128
PIECE = 26
USED = 72

relaxation = 0.75
reflect_re = -0.3
reflect_im = 0.2

STEP = ((-1, 0), (1, 0), (0, -1), (0, 1))
PLACES = tuple(
    (dr, dc) for dr in range(-2, 3) for dc in range(-2, 3) if abs(dr) + abs(dc) <= 2
)
CLASSES = 13
SHARE = 52
ROWS = 32


def path_matrix():
    twice = relaxation * relaxation
    once = relaxation * (1.0 - relaxation) + relaxation
    mix = np.zeros((CLASSES * ROWS, 18 * 24), np.float32)

    def add(weight, first, second, place, kind):
        d = PLACES.index(place)
        for part, left, right, sign in ((0, 0, 0, 1), (0, 1, 1, -1), (1, 0, 1, 1), (1, 1, 0, 1)):
            at = 16 + right if second is None else right * 8 + second
            mix[kind * ROWS + part * 13 + d, (first * 2 + left) * 24 + at] += sign * weight

    def corner(e, f):
        return 9 + (min(e, f) % 2) * 2 + (max(e, f) % 2)

    add(1.0, 0, None, (0, 0), 0)
    for e in range(4):
        add(once, 0, e, STEP[e], 0)
        add(once, 0, 4 + e, (0, 0), 1 + e)
        for f in range(4):
            both = (STEP[e][0] + STEP[f][0], STEP[e][1] + STEP[f][1])
            crossed = e // 2 != f // 2
            add(twice, 1 + e, f, both, 0)
            if f == e ^ 1:
                add(-twice, 1 + e, f, both, 1 + e)
            if f != e:
                add(twice, 5 + e, f, STEP[f], 1 + e)
            if f == e:
                add(twice, 1 + e, 4 + f, STEP[e], 5 + e)
                add(twice, 5 + e, 4 + f, (0, 0), 1 + e)
            elif crossed:
                add(twice, 1 + e, 4 + f, STEP[e], 1 + f)
                add(twice, 5 + e, 4 + f, (0, 0), corner(e, f))
    return mix


def halves(value):
    high = value.astype(jnp.bfloat16)
    return high, (value - high.astype(jnp.float32)).astype(jnp.bfloat16)


def thirds(value):
    high, low = halves(value)
    return high, low, (value - high.astype(jnp.float32) - low.astype(jnp.float32)).astype(jnp.bfloat16)


def cosine(turns, length):
    centred = jnp.where(turns >= length // 2, length - turns, turns)
    angle = (length // 4 - centred).astype(jnp.float32) * (2.0 * math.pi / length)
    square = angle * angle
    value = 1.0 / 6227020800.0
    value = value * square - 1.0 / 39916800.0
    value = value * square + 1.0 / 362880.0
    value = value * square - 1.0 / 5040.0
    value = value * square + 1.0 / 120.0
    value = value * square - 1.0 / 6.0
    return angle + angle * square * value


def dot(left, right, dims=((1,), (0,))):
    return lax.dot_general(left, right, (dims, ((), ())), preferred_element_type=jnp.float32)


def dot3(left, right, dims=((1,), (0,))):
    high, low = left
    high_right, low_right = right
    return dot(high, high_right, dims) + (dot(low, high_right, dims) + dot(high, low_right, dims))


def fetch(sems, *pairs, wait=False):
    copies = [pltpu.make_async_copy(src, dst, sems.at[i]) for i, (src, dst) in enumerate(pairs)]
    for copy in copies:
        copy.start()
    if wait:
        for copy in copies:
            copy.wait()
    return copies


def turn_kernel(place, rows, cols, row_high_ref, row_low_ref, col_high_ref, col_low_ref):
    row_at, col_at = place()
    span = OVER * rows
    r = lax.broadcasted_iota(jnp.int32, (rows, LANES), 0)
    k = lax.broadcasted_iota(jnp.int32, (rows, LANES), 1)
    samples = OVER * BLOCK
    turns = (r * (row_at * samples + k)) & (span - 1)
    cos = jnp.where(k < samples, cosine(turns, span), 0.0)
    sin = jnp.where(k < samples, cosine((turns - span // 4) & (span - 1), span), 0.0)
    pick = (k >= samples) & (k < samples + BLOCK) & (r == row_at * BLOCK + k - samples)
    pick = jnp.where(pick, 1.0, 0.0)
    turn = jnp.concatenate(
        [
            jnp.concatenate([cos + pick, -sin], axis=1),
            jnp.concatenate([sin, cos + pick], axis=1),
        ],
        axis=0,
    )
    row_high_ref[...], row_low_ref[...] = halves(turn)

    span = OVER * cols
    blocks = cols // BLOCK
    shape = (samples, blocks * PIECE)
    q = lax.broadcasted_iota(jnp.int32, shape, 0) + col_at * samples
    k = lax.broadcasted_iota(jnp.int32, shape, 1)
    block = jnp.zeros(shape, jnp.int32)
    for b in range(1, blocks):
        block = block + jnp.where(k >= b * PIECE, 1, 0)
    at = k - block * PIECE
    imaginary = at >= WIDE
    c = block * BLOCK + at - jnp.where(imaginary, WIDE, 0) - REACH
    inside = (at < 2 * WIDE) & (c >= 0) & (c < cols)
    turns = (q * c) & (span - 1)
    scale = (rows * cols) ** -0.5
    cos = jnp.where(inside, cosine(turns, span) * scale, 0.0)
    sin = jnp.where(inside, cosine((turns - span // 4) & (span - 1), span) * scale, 0.0)
    turn = jnp.concatenate([jnp.where(imaginary, sin, cos), jnp.where(imaginary, cos, -sin)], axis=0)
    col_high_ref[...], col_low_ref[...] = halves(turn)


def make_table(feed_hbm, map_hbm, probe_hbm, mix_hbm, table_ref, feed_ref, map_ref, probe_ref, mix_ref, hops_ref, sems):
    edge = feed_ref.shape[2] // 4
    chunks = [(map_hbm.at[:, pl.ds(a * edge, edge)], map_ref.at[:, pl.ds(a * edge, edge)]) for a in range(4)]
    copies = fetch(sems, (feed_hbm, feed_ref), (probe_hbm, probe_ref), *chunks, (mix_hbm, mix_ref))
    copies[0].wait()
    copies[1].wait()
    units = 4 * edge

    def block(value, e):
        return value[:, e * edge : (e + 1) * edge]

    feed_re, feed_im = feed_ref[0], feed_ref[1]
    back_re = reflect_re * feed_re - reflect_im * feed_im
    back_im = reflect_re * feed_im + reflect_im * feed_re
    hops_ref[0:8, :] = feed_re
    hops_ref[8:16, :] = feed_im
    for a in range(4):
        e = a ^ 1
        enter = jnp.concatenate(
            [block(feed_re, e), block(feed_im, e), block(back_re, a), block(back_im, a)], axis=0
        )
        enter = jnp.concatenate(halves(enter), axis=0)
        copies[2 + a].wait()
        by_re = dot(enter, map_ref[0, a * edge : (a + 1) * edge, :])
        by_im = dot(enter, map_ref[1, a * edge : (a + 1) * edge, :])
        by_re = by_re[0:32] + by_re[32:64]
        by_im = by_im[0:32] + by_im[32:64]
        for first, at in ((1 + e, 0), (5 + a, 16)):
            hops_ref[first * 16 : first * 16 + 8, :] = by_re[at : at + 8] - by_im[at + 8 : at + 16]
            hops_ref[first * 16 + 8 : first * 16 + 16, :] = (
                by_re[at + 8 : at + 16] + by_im[at : at + 8]
            )
    probe_re, probe_im = probe_ref[0:1, :], probe_ref[1:2, :]
    probes = jnp.concatenate(halves(jnp.concatenate([probe_re, probe_im] + [probe_re] * 6, axis=0)), axis=0)
    through_re = dot(probes, map_ref[0], ((1,), (1,)))
    through_im = dot(probes, map_ref[1], ((1,), (1,)))
    through_re = through_re[0:8] + through_re[8:16]
    through_im = through_im[0:8] + through_im[8:16]
    total_re = probe_re + through_re[0:1] - through_im[1:2]
    total_im = probe_im + through_im[0:1] + through_re[1:2]

    def swapped(value):
        return jnp.concatenate([block(value, e ^ 1) for e in range(4)], axis=1)

    sub = lax.broadcasted_iota(jnp.int32, (8, units), 0)
    lane = lax.broadcasted_iota(jnp.int32, (8, units), 1)
    own = lane // edge == sub % 4
    passed = sub < 4
    out_re = jnp.where(passed, swapped(total_re), reflect_re * total_re - reflect_im * total_im)
    out_im = jnp.where(passed, swapped(total_im), reflect_re * total_im + reflect_im * total_re)
    leave = jnp.concatenate(
        [
            jnp.where(own, out_re, 0.0),
            jnp.where(own, out_im, 0.0),
            jnp.where(sub == 0, probe_re, jnp.where(sub == 1, probe_im, 0.0)),
        ],
        axis=0,
    )
    products = dot3(halves(leave), halves(hops_ref[...]), ((1,), (1,)))
    copies[6].wait()
    flat = jnp.concatenate([products[:, 8 * k : 8 * k + 8] for k in range(18)], axis=0)
    table = dot(mix_ref[...], jnp.concatenate(thirds(flat), axis=1))
    table = table[:, 0:8] + table[:, 8:16] + table[:, 16:24]
    wide = [table[k * ROWS : (k + 1) * ROWS, :] for k in range(CLASSES)]
    wide.append(jnp.zeros((ROWS, LANES - 8 * CLASSES), jnp.float32))
    table_ref[...] = jnp.concatenate(wide, axis=1)


def maker(row_at):
    return row_at % 16 < 4, row_at % 4 + 4 * (row_at // 16)


def pack_kernel(
    place, drive_hbm, flag_hbm, port_hbm, feed_hbm, map_hbm, probe_hbm, mix_hbm, out_ref,
    drive_ref, flag_ref, port_ref, feed_ref, map_ref, probe_ref, mix_ref, hops_ref, table_ref, piece_ref, sems, table_sems,
):
    makes, share = maker(place()[0])
    fetch(sems, (drive_hbm, drive_ref), (flag_hbm, flag_ref), (port_hbm, port_ref), wait=True)
    active = flag_ref[...].astype(jnp.float32)
    pieces = [drive_ref[x, s] * active for x in range(2) for s in range(STATES)]
    pieces.append(port_ref[...].astype(jnp.float32))
    pieces.append(jnp.zeros((BLOCK, LANES - USED), jnp.float32))
    piece_ref[...] = jnp.concatenate(pieces, axis=1)

    @pl.when(makes)
    def _():
        make_table(
            feed_hbm, map_hbm, probe_hbm, mix_hbm, table_ref,
            feed_ref, map_ref, probe_ref, mix_ref, hops_ref, table_sems,
        )
        part = table_ref[pl.ds(pl.multiple_of(share // 2 * 8, 8), 8), :]
        part = jnp.where(share % 2 == 0, pltpu.roll(part, USED, axis=1), pltpu.roll(part, USED - SHARE, axis=1))
        lane = lax.broadcasted_iota(jnp.int32, (BLOCK, LANES), 1)
        piece_ref[...] += jnp.where((lane >= USED) & (lane < USED + SHARE), part, 0.0)

    out_ref[...] = jnp.broadcast_to(piece_ref[...][None], out_ref.shape)


def stencil_kernel(place, rows, cols, cells_ref, row_high_ref, row_low_ref, out_ref, own_ref, coef_ref):
    _, col_at = place()
    across = cells_ref[...].T
    amps = [[across[(x * 4 + s) * 8 : (x * 4 + s) * 8 + 8] for s in range(STATES)] for x in range(2)]
    ports = across[64:72]

    sub = lax.broadcasted_iota(jnp.int32, (8, rows), 0).astype(jnp.float32)
    r = lax.broadcasted_iota(jnp.int32, (8, rows), 1)

    def flag(mask):
        return jnp.where(mask, 1.0, 0.0)

    north, south, north2, south2 = flag(r == 0), flag(r == rows - 1), flag(r == 1), flag(r == rows - 2)
    lane = lax.broadcasted_iota(jnp.int32, (BLOCK, LANES), 1)
    parts = [cells_ref[(k % 4 + 16 * (k // 4)) * BLOCK : (k % 4 + 16 * (k // 4) + 1) * BLOCK, :] for k in range(8)]
    firsts = [jnp.where(lane < SHARE, pltpu.roll(part, LANES - USED, axis=1), 0.0) for part in parts[0::2]]
    seconds = [
        jnp.where((lane >= SHARE) & (lane < 2 * SHARE), pltpu.roll(part, LANES - USED + SHARE, axis=1), 0.0)
        for part in parts[1::2]
    ]
    table = jnp.concatenate(halves(jnp.concatenate([a + b for a, b in zip(firsts, seconds)], axis=0)), axis=0)
    for j in range(BLOCK):
        c = col_at * BLOCK + j
        west, east = flag(c == 0), flag(c == cols - 1)
        west2, east2 = flag(c == 1), flag(c == cols - 2)
        chosen = flag(jnp.broadcast_to(ports[j : j + 1], (8, rows)) == sub)
        at_north, at_south = chosen * north, chosen * south
        kinds = [
            chosen, at_north, at_south, chosen * west, chosen * east,
            chosen * north2, chosen * south2, chosen * west2, chosen * east2,
            at_north * west, at_north * east, at_south * west, at_south * east,
            jnp.zeros((LANES - 8 * CLASSES, rows), jnp.float32),
        ]
        found = dot(table, jnp.concatenate(kinds, axis=0).astype(jnp.bfloat16))
        found = found[0:ROWS] + found[ROWS : 2 * ROWS]
        for half in range(rows // LANES):
            coef_ref[half, j * ROWS : (j + 1) * ROWS, :] = found[:, half * LANES : (half + 1) * LANES]

    def coef(index):
        return jnp.concatenate(
            [coef_ref[half, pl.ds(index, 8, stride=ROWS), :] for half in range(rows // LANES)], axis=1
        )

    def moved(value, dr):
        if dr == 0:
            return value
        value = pltpu.roll(value, dr % rows, axis=1)
        return jnp.where(r >= dr if dr > 0 else r < rows + dr, value, 0.0)

    sums = {}
    for d, (dr, dc) in enumerate(PLACES):
        k_re, k_im = coef(d), coef(13 + d)
        for s in range(STATES):
            a_re, a_im = amps[0][s], amps[1][s]
            for x, value in ((0, k_re * a_re - k_im * a_im), (1, k_re * a_im + k_im * a_re)):
                value = moved(value, dr)
                key = (dc, s, x)
                sums[key] = sums[key] + value if key in sums else value

    spread = jnp.concatenate(
        [
            jnp.concatenate([sums[dc, s, 0], sums[dc, s, 1]], axis=1)
            for dc in range(-2, 3)
            for s in range(STATES)
        ],
        axis=0,
    )
    turned = dot3(halves(spread), (row_high_ref[...], row_low_ref[...]))
    samples = OVER * BLOCK
    lane = lax.broadcasted_iota(jnp.int32, (8, LANES), 1)
    first, second = lane < samples, (lane >= samples) & (lane < samples + BLOCK)
    nothing = jnp.zeros((16, LANES), jnp.float32)
    mains, nears = [], []
    for x in range(2):
        main, near = nothing, nothing
        for i, dc in enumerate(range(-2, 3)):
            wave, own = jnp.zeros((8, LANES), jnp.float32), jnp.zeros((8, LANES), jnp.float32)
            for s in range(STATES):
                part = turned[(i * STATES + s) * 8 : (i * STATES + s) * 8 + 8, x * LANES : (x + 1) * LANES]
                a, b = jnp.where(first, part, 0.0), jnp.where(second, part, 0.0)
                wave = wave + (pltpu.roll(a, s * samples, axis=1) if s else a)
                own = own + pltpu.roll(b, (s - 1) * samples % LANES, axis=1) if s != 1 else own + b
            for_main = jnp.concatenate([wave, jnp.zeros((8, LANES), jnp.float32)], axis=0)
            for_near = jnp.concatenate([own, jnp.zeros((8, LANES), jnp.float32)], axis=0)
            shift = REACH + dc
            main = main + (pltpu.roll(for_main, shift, axis=0) if shift else for_main)
            near = near + (pltpu.roll(for_near, shift, axis=0) if shift else for_near)
        mains.append(main[0:WIDE])
        nears.append(
            near[0:1] + pltpu.roll(near, BLOCK, axis=1)[1:2]
            + pltpu.roll(near, 2 * BLOCK, axis=1)[10:11] + pltpu.roll(near, 3 * BLOCK, axis=1)[11:12]
        )
        own_ref[:, x * LANES : (x + 1) * LANES] = near
    piece = jnp.concatenate(mains + nears, axis=0)
    four = jnp.concatenate([piece] * 4, axis=0)
    for i in range(out_ref.shape[0] // (4 * PIECE)):
        out_ref[i * 4 * PIECE : (i + 1) * 4 * PIECE, :] = four


def pattern_kernel(place, blocks, got_ref, own_ref, col_high_ref, col_low_ref, currents_ref, far_ref):
    _, col_at = place()
    samples = OVER * BLOCK
    far = dot3((col_high_ref[...], col_low_ref[...]), halves(got_ref[...]))
    far = jnp.concatenate([far, jnp.zeros_like(far)], axis=0).T
    for x in range(2):
        for s in range(STATES):
            far_ref[x, s] = far[s * samples : (s + 1) * samples, x * samples : (x + 1) * samples]
    left, right = jnp.maximum(col_at - 1, 0), jnp.minimum(col_at + 1, blocks - 1)
    has_left, has_right = jnp.where(col_at > 0, 1.0, 0.0), jnp.where(col_at < blocks - 1, 1.0, 0.0)
    own = own_ref[...]
    for x in range(2):
        from_left = has_left * got_ref[pl.ds(left * PIECE + 2 * WIDE + x, 1), :]
        from_right = has_right * got_ref[pl.ds(right * PIECE + 2 * WIDE + x, 1), :]
        mine = own[:, x * LANES : (x + 1) * LANES]
        whole = jnp.concatenate(
            [
                mine[2:3] + pltpu.roll(from_left, LANES - 2 * BLOCK, axis=1),
                mine[3:4] + pltpu.roll(from_left, LANES - 3 * BLOCK, axis=1),
                mine[4:8],
                mine[8:9] + from_right,
                mine[9:10] + pltpu.roll(from_right, LANES - BLOCK, axis=1),
                jnp.zeros((LANES - BLOCK, LANES), jnp.float32),
            ],
            axis=0,
        ).T
        for s in range(STATES):
            currents_ref[x, s] = whole[s * samples : s * samples + BLOCK, 0:BLOCK]


def spot():
    return lax.axis_index("row"), lax.axis_index("col")


HBM = pl.BlockSpec(memory_space=pltpu.HBM)


def call(kernel, out_shape, scratch=(), flops=0, size=0, grant=40960, **options):
    return pl.pallas_call(
        kernel,
        out_shape=out_shape,
        scratch_shapes=list(scratch),
        compiler_params=pltpu.CompilerParams(vmem_limit_bytes=grant * 1024),
        cost_estimate=pl.CostEstimate(flops=flops, bytes_accessed=size, transcendentals=0),
        **options,
    )


def body(row_blocks, col_blocks, place, active_flags, port_index, drive_weights, feed_table, cell_map, probe_weights):
    rows, cols = row_blocks * BLOCK, col_blocks * BLOCK
    samples = OVER * BLOCK
    f32, b16 = jnp.float32, jnp.bfloat16
    shape = jax.ShapeDtypeStruct
    taken = (
        drive_weights, active_flags, port_index,
        feed_table, cell_map, probe_weights, jnp.asarray(path_matrix(), b16),
    )
    packed = call(
        functools.partial(pack_kernel, place),
        shape((row_blocks, BLOCK, LANES), f32),
        scratch=[pltpu.VMEM(x.shape, x.dtype) for x in taken]
        + [
            pltpu.VMEM((144, cell_map.shape[1]), f32),
            pltpu.VMEM((ROWS, LANES), f32),
            pltpu.VMEM((BLOCK, LANES), f32),
            pltpu.SemaphoreType.DMA((3,)),
            pltpu.SemaphoreType.DMA((7,)),
        ],
        in_specs=[HBM] * 7,
        name="pack",
        grant=61440,
    )(*taken)
    cells = lax.all_to_all(packed, "row", 0, 0).reshape(rows, LANES)
    row_high, row_low, col_high, col_low = call(
        functools.partial(turn_kernel, place, rows, cols),
        (
            shape((2 * rows, 2 * LANES), b16),
            shape((2 * rows, 2 * LANES), b16),
            shape((2 * samples, col_blocks * PIECE), b16),
            shape((2 * samples, col_blocks * PIECE), b16),
        ),
        flops=2 * 80 * 2 * 1024 * 1024,
        size=5 * 1024 * 1024,
        name="turns",
    )()
    pieces, own = call(
        functools.partial(stencil_kernel, place, rows, cols),
        (shape((col_blocks * PIECE, LANES), f32), shape((16, 2 * LANES), f32)),
        scratch=[pltpu.VMEM((rows // LANES, BLOCK * ROWS, LANES), f32)],
        name="stencil",
    )(cells, row_high, row_low)
    got = lax.all_to_all(pieces.reshape(col_blocks, PIECE // 2, 2, LANES), "col", 0, 0)
    return call(
        functools.partial(pattern_kernel, place, col_blocks),
        (shape((2, STATES, BLOCK, BLOCK), f32), shape((2, STATES, samples, samples), f32)),
        name="pattern",
    )(got.reshape(col_blocks * PIECE, LANES), own, col_high, col_low)


def solution(mesh):
    placed = (P("row", "col"), P("row", "col"), P(None, None, "row", "col"), P(), P(), P())
    return jax.shard_map(
        functools.partial(body, mesh.shape["row"], mesh.shape["col"], spot),
        mesh=mesh,
        in_specs=placed,
        out_specs=(P(None, None, "row", "col"), P(None, None, "row", "col")),
        check_vma=False,
    )
```

```python
import functools
import math

import jax
import jax.numpy as jnp
import numpy as np
from jax import lax
from jax.experimental import pallas as pl
from jax.experimental.pallas import tpu as pltpu
from jax.sharding import PartitionSpec as P

OVER = 4
PORTS = 8
STATES = 4
BLOCK = 8
REACH = 2
WIDE = 12
LANES = 128
FIRST_ROW = 10
FIRST_COL = 10
PIECE = 26
USED = 72

relaxation = 0.75
reflect_re = -0.3
reflect_im = 0.2

STEP = ((-1, 0), (1, 0), (0, -1), (0, 1))
PLACES = tuple(
    (dr, dc) for dr in range(-2, 3) for dc in range(-2, 3) if abs(dr) + abs(dc) <= 2
)
CLASSES = 13
SHARE = 52
ROWS = 32


def path_matrix():
    twice = relaxation * relaxation
    once = relaxation * (1.0 - relaxation) + relaxation
    mix = np.zeros((CLASSES * ROWS, 18 * 24), np.float32)

    def add(weight, first, second, place, kind):
        d = PLACES.index(place)
        for part, left, right, sign in ((0, 0, 0, 1), (0, 1, 1, -1), (1, 0, 1, 1), (1, 1, 0, 1)):
            at = 16 + right if second is None else right * 8 + second
            mix[kind * ROWS + part * 13 + d, (first * 2 + left) * 24 + at] += sign * weight

    def corner(e, f):
        return 9 + (min(e, f) % 2) * 2 + (max(e, f) % 2)

    add(1.0, 0, None, (0, 0), 0)
    for e in range(4):
        add(once, 0, e, STEP[e], 0)
        add(once, 0, 4 + e, (0, 0), 1 + e)
        for f in range(4):
            both = (STEP[e][0] + STEP[f][0], STEP[e][1] + STEP[f][1])
            crossed = e // 2 != f // 2
            add(twice, 1 + e, f, both, 0)
            if f == e ^ 1:
                add(-twice, 1 + e, f, both, 1 + e)
            if f != e:
                add(twice, 5 + e, f, STEP[f], 1 + e)
            if f == e:
                add(twice, 1 + e, 4 + f, STEP[e], 5 + e)
                add(twice, 5 + e, 4 + f, (0, 0), 1 + e)
            elif crossed:
                add(twice, 1 + e, 4 + f, STEP[e], 1 + f)
                add(twice, 5 + e, 4 + f, (0, 0), corner(e, f))
    return mix


def halves(value):
    high = value.astype(jnp.bfloat16)
    return high, (value - high.astype(jnp.float32)).astype(jnp.bfloat16)


def thirds(value):
    high, low = halves(value)
    return high, low, (value - high.astype(jnp.float32) - low.astype(jnp.float32)).astype(jnp.bfloat16)


def cosine(turns, length):
    centred = jnp.where(turns >= length // 2, length - turns, turns)
    angle = (length // 4 - centred).astype(jnp.float32) * (2.0 * math.pi / length)
    square = angle * angle
    value = 1.0 / 6227020800.0
    value = value * square - 1.0 / 39916800.0
    value = value * square + 1.0 / 362880.0
    value = value * square - 1.0 / 5040.0
    value = value * square + 1.0 / 120.0
    value = value * square - 1.0 / 6.0
    return angle + angle * square * value


def dot(left, right, dims=((1,), (0,))):
    return lax.dot_general(left, right, (dims, ((), ())), preferred_element_type=jnp.float32)


def dot3(left, right, dims=((1,), (0,))):
    high, low = left
    high_right, low_right = right
    return dot(high, high_right, dims) + (dot(low, high_right, dims) + dot(high, low_right, dims))


def fetch(sems, *pairs, wait=False):
    copies = [pltpu.make_async_copy(src, dst, sems.at[i]) for i, (src, dst) in enumerate(pairs)]
    for copy in copies:
        copy.start()
    if wait:
        for copy in copies:
            copy.wait()
    return copies


def turn_kernel(place, rows, cols, row_high_ref, row_low_ref, col_high_ref, col_low_ref):
    row_at, col_at = place()
    span = OVER * rows
    r = lax.broadcasted_iota(jnp.int32, (rows, LANES), 0)
    k = lax.broadcasted_iota(jnp.int32, (rows, LANES), 1)
    samples = OVER * BLOCK
    turns = (r * (row_at * samples + k)) & (span - 1)
    cos = jnp.where(k < samples, cosine(turns, span), 0.0)
    sin = jnp.where(k < samples, cosine((turns - span // 4) & (span - 1), span), 0.0)
    pick = (k >= samples) & (k < samples + BLOCK) & (r == row_at * BLOCK + k - samples)
    pick = jnp.where(pick, 1.0, 0.0)
    turn = jnp.concatenate(
        [
            jnp.concatenate([cos + pick, -sin], axis=1),
            jnp.concatenate([sin, cos + pick], axis=1),
        ],
        axis=0,
    )
    row_high_ref[...], row_low_ref[...] = halves(turn)

    span = OVER * cols
    blocks = cols // BLOCK
    shape = (samples, blocks * PIECE)
    q = lax.broadcasted_iota(jnp.int32, shape, 0) + col_at * samples
    k = lax.broadcasted_iota(jnp.int32, shape, 1)
    block = jnp.zeros(shape, jnp.int32)
    for b in range(1, blocks):
        block = block + jnp.where(k >= b * PIECE, 1, 0)
    at = k - block * PIECE
    imaginary = at >= WIDE
    c = (block + FIRST_COL) % blocks * BLOCK + at - jnp.where(imaginary, WIDE, 0) - REACH
    inside = (at < 2 * WIDE) & (c >= 0) & (c < cols)
    turns = (q * c) & (span - 1)
    scale = (rows * cols) ** -0.5
    cos = jnp.where(inside, cosine(turns, span) * scale, 0.0)
    sin = jnp.where(inside, cosine((turns - span // 4) & (span - 1), span) * scale, 0.0)
    turn = jnp.concatenate([jnp.where(imaginary, sin, cos), jnp.where(imaginary, cos, -sin)], axis=0)
    col_high_ref[...], col_low_ref[...] = halves(turn)


def make_table(feed_hbm, map_hbm, probe_hbm, mix_hbm, table_ref, feed_ref, map_ref, probe_ref, mix_ref, hops_ref, sems):
    edge = feed_ref.shape[2] // 4
    chunks = [(map_hbm.at[:, pl.ds(a * edge, edge)], map_ref.at[:, pl.ds(a * edge, edge)]) for a in range(4)]
    copies = fetch(sems, (feed_hbm, feed_ref), (probe_hbm, probe_ref), *chunks, (mix_hbm, mix_ref))
    copies[0].wait()
    copies[1].wait()
    units = 4 * edge

    def block(value, e):
        return value[:, e * edge : (e + 1) * edge]

    feed_re, feed_im = feed_ref[0], feed_ref[1]
    back_re = reflect_re * feed_re - reflect_im * feed_im
    back_im = reflect_re * feed_im + reflect_im * feed_re
    hops_ref[0:8, :] = feed_re
    hops_ref[8:16, :] = feed_im
    for a in range(4):
        e = a ^ 1
        enter = jnp.concatenate(
            [block(feed_re, e), block(feed_im, e), block(back_re, a), block(back_im, a)], axis=0
        )
        enter = jnp.concatenate(halves(enter), axis=0)
        copies[2 + a].wait()
        by_re = dot(enter, map_ref[0, a * edge : (a + 1) * edge, :])
        by_im = dot(enter, map_ref[1, a * edge : (a + 1) * edge, :])
        by_re = by_re[0:32] + by_re[32:64]
        by_im = by_im[0:32] + by_im[32:64]
        for first, at in ((1 + e, 0), (5 + a, 16)):
            hops_ref[first * 16 : first * 16 + 8, :] = by_re[at : at + 8] - by_im[at + 8 : at + 16]
            hops_ref[first * 16 + 8 : first * 16 + 16, :] = (
                by_re[at + 8 : at + 16] + by_im[at : at + 8]
            )
    probe_re, probe_im = probe_ref[0:1, :], probe_ref[1:2, :]
    probes = jnp.concatenate(halves(jnp.concatenate([probe_re, probe_im] + [probe_re] * 6, axis=0)), axis=0)
    through_re = dot(probes, map_ref[0], ((1,), (1,)))
    through_im = dot(probes, map_ref[1], ((1,), (1,)))
    through_re = through_re[0:8] + through_re[8:16]
    through_im = through_im[0:8] + through_im[8:16]
    total_re = probe_re + through_re[0:1] - through_im[1:2]
    total_im = probe_im + through_im[0:1] + through_re[1:2]

    def swapped(value):
        return jnp.concatenate([block(value, e ^ 1) for e in range(4)], axis=1)

    sub = lax.broadcasted_iota(jnp.int32, (8, units), 0)
    lane = lax.broadcasted_iota(jnp.int32, (8, units), 1)
    own = lane // edge == sub % 4
    passed = sub < 4
    out_re = jnp.where(passed, swapped(total_re), reflect_re * total_re - reflect_im * total_im)
    out_im = jnp.where(passed, swapped(total_im), reflect_re * total_im + reflect_im * total_re)
    leave = jnp.concatenate(
        [
            jnp.where(own, out_re, 0.0),
            jnp.where(own, out_im, 0.0),
            jnp.where(sub == 0, probe_re, jnp.where(sub == 1, probe_im, 0.0)),
        ],
        axis=0,
    )
    products = dot3(halves(leave), halves(hops_ref[...]), ((1,), (1,)))
    copies[6].wait()
    flat = jnp.concatenate([products[:, 8 * k : 8 * k + 8] for k in range(18)], axis=0)
    table = dot(mix_ref[...], jnp.concatenate(thirds(flat), axis=1))
    table = table[:, 0:8] + table[:, 8:16] + table[:, 16:24]
    wide = [table[k * ROWS : (k + 1) * ROWS, :] for k in range(CLASSES)]
    wide.append(jnp.zeros((ROWS, LANES - 8 * CLASSES), jnp.float32))
    table_ref[...] = jnp.concatenate(wide, axis=1)


def maker(row_at):
    return row_at % 16 < 4, row_at % 4 + 4 * (row_at // 16)


def pack_kernel(
    place, drive_hbm, flag_hbm, port_hbm, feed_hbm, map_hbm, probe_hbm, mix_hbm, out_ref,
    drive_ref, flag_ref, port_ref, feed_ref, map_ref, probe_ref, mix_ref, hops_ref, table_ref, piece_ref, sems, table_sems,
):
    makes, share = maker(place()[0])
    fetch(sems, (drive_hbm, drive_ref), (flag_hbm, flag_ref), (port_hbm, port_ref), wait=True)
    active = flag_ref[...].astype(jnp.float32)
    pieces = [drive_ref[x, s] * active for x in range(2) for s in range(STATES)]
    pieces.append(port_ref[...].astype(jnp.float32))
    pieces.append(jnp.zeros((BLOCK, LANES - USED), jnp.float32))
    piece_ref[...] = jnp.concatenate(pieces, axis=1)

    @pl.when(makes)
    def _():
        make_table(
            feed_hbm, map_hbm, probe_hbm, mix_hbm, table_ref,
            feed_ref, map_ref, probe_ref, mix_ref, hops_ref, table_sems,
        )
        part = table_ref[pl.ds(pl.multiple_of(share // 2 * 8, 8), 8), :]
        part = jnp.where(share % 2 == 0, pltpu.roll(part, USED, axis=1), pltpu.roll(part, USED - SHARE, axis=1))
        lane = lax.broadcasted_iota(jnp.int32, (BLOCK, LANES), 1)
        piece_ref[...] += jnp.where((lane >= USED) & (lane < USED + SHARE), part, 0.0)

    out_ref[...] = jnp.broadcast_to(piece_ref[...][None], out_ref.shape)


def stencil_kernel(place, rows, cols, cells_ref, row_high_ref, row_low_ref, out_ref, own_ref, coef_ref):
    _, col_at = place()
    start = (rows // BLOCK - FIRST_ROW) * BLOCK
    across = jnp.concatenate([cells_ref[start:, :], cells_ref[:start, :]], axis=0).T
    amps = [[across[(x * 4 + s) * 8 : (x * 4 + s) * 8 + 8] for s in range(STATES)] for x in range(2)]
    ports = across[64:72]

    sub = lax.broadcasted_iota(jnp.int32, (8, rows), 0).astype(jnp.float32)
    r = lax.broadcasted_iota(jnp.int32, (8, rows), 1)

    def flag(mask):
        return jnp.where(mask, 1.0, 0.0)

    north, south, north2, south2 = flag(r == 0), flag(r == rows - 1), flag(r == 1), flag(r == rows - 2)
    lane = lax.broadcasted_iota(jnp.int32, (BLOCK, LANES), 1)
    makers = [(k % 4 + 16 * (k // 4) - FIRST_ROW) * BLOCK % rows for k in range(8)]
    parts = [cells_ref[k : k + BLOCK, :] for k in makers]
    firsts = [jnp.where(lane < SHARE, pltpu.roll(part, LANES - USED, axis=1), 0.0) for part in parts[0::2]]
    seconds = [
        jnp.where((lane >= SHARE) & (lane < 2 * SHARE), pltpu.roll(part, LANES - USED + SHARE, axis=1), 0.0)
        for part in parts[1::2]
    ]
    table = jnp.concatenate(halves(jnp.concatenate([a + b for a, b in zip(firsts, seconds)], axis=0)), axis=0)
    for j in range(BLOCK):
        c = col_at * BLOCK + j
        west, east = flag(c == 0), flag(c == cols - 1)
        west2, east2 = flag(c == 1), flag(c == cols - 2)
        chosen = flag(jnp.broadcast_to(ports[j : j + 1], (8, rows)) == sub)
        at_north, at_south = chosen * north, chosen * south
        kinds = [
            chosen, at_north, at_south, chosen * west, chosen * east,
            chosen * north2, chosen * south2, chosen * west2, chosen * east2,
            at_north * west, at_north * east, at_south * west, at_south * east,
            jnp.zeros((LANES - 8 * CLASSES, rows), jnp.float32),
        ]
        found = dot(table, jnp.concatenate(kinds, axis=0).astype(jnp.bfloat16))
        found = found[0:ROWS] + found[ROWS : 2 * ROWS]
        for half in range(rows // LANES):
            coef_ref[half, j * ROWS : (j + 1) * ROWS, :] = found[:, half * LANES : (half + 1) * LANES]

    def coef(index):
        return jnp.concatenate(
            [coef_ref[half, pl.ds(index, 8, stride=ROWS), :] for half in range(rows // LANES)], axis=1
        )

    def moved(value, dr):
        if dr == 0:
            return value
        value = pltpu.roll(value, dr % rows, axis=1)
        return jnp.where(r >= dr if dr > 0 else r < rows + dr, value, 0.0)

    sums = {}
    for d, (dr, dc) in enumerate(PLACES):
        k_re, k_im = coef(d), coef(13 + d)
        for s in range(STATES):
            a_re, a_im = amps[0][s], amps[1][s]
            for x, value in ((0, k_re * a_re - k_im * a_im), (1, k_re * a_im + k_im * a_re)):
                value = moved(value, dr)
                key = (dc, s, x)
                sums[key] = sums[key] + value if key in sums else value

    spread = jnp.concatenate(
        [
            jnp.concatenate([sums[dc, s, 0], sums[dc, s, 1]], axis=1)
            for dc in range(-2, 3)
            for s in range(STATES)
        ],
        axis=0,
    )
    turned = dot3(halves(spread), (row_high_ref[...], row_low_ref[...]))
    samples = OVER * BLOCK
    lane = lax.broadcasted_iota(jnp.int32, (8, LANES), 1)
    first, second = lane < samples, (lane >= samples) & (lane < samples + BLOCK)
    nothing = jnp.zeros((16, LANES), jnp.float32)
    mains, nears = [], []
    for x in range(2):
        main, near = nothing, nothing
        for i, dc in enumerate(range(-2, 3)):
            wave, own = jnp.zeros((8, LANES), jnp.float32), jnp.zeros((8, LANES), jnp.float32)
            for s in range(STATES):
                part = turned[(i * STATES + s) * 8 : (i * STATES + s) * 8 + 8, x * LANES : (x + 1) * LANES]
                a, b = jnp.where(first, part, 0.0), jnp.where(second, part, 0.0)
                wave = wave + (pltpu.roll(a, s * samples, axis=1) if s else a)
                own = own + pltpu.roll(b, (s - 1) * samples % LANES, axis=1) if s != 1 else own + b
            for_main = jnp.concatenate([wave, jnp.zeros((8, LANES), jnp.float32)], axis=0)
            for_near = jnp.concatenate([own, jnp.zeros((8, LANES), jnp.float32)], axis=0)
            shift = REACH + dc
            main = main + (pltpu.roll(for_main, shift, axis=0) if shift else for_main)
            near = near + (pltpu.roll(for_near, shift, axis=0) if shift else for_near)
        mains.append(main[0:WIDE])
        nears.append(
            near[0:1] + pltpu.roll(near, BLOCK, axis=1)[1:2]
            + pltpu.roll(near, 2 * BLOCK, axis=1)[10:11] + pltpu.roll(near, 3 * BLOCK, axis=1)[11:12]
        )
        own_ref[:, x * LANES : (x + 1) * LANES] = near
    piece = jnp.concatenate(mains + nears, axis=0)
    four = jnp.concatenate([piece] * 4, axis=0)
    for i in range(out_ref.shape[0] // (4 * PIECE)):
        out_ref[i * 4 * PIECE : (i + 1) * 4 * PIECE, :] = four


def pattern_kernel(place, blocks, got_ref, own_ref, col_high_ref, col_low_ref, currents_ref, far_ref):
    _, col_at = place()
    samples = OVER * BLOCK
    far = dot3((col_high_ref[...], col_low_ref[...]), halves(got_ref[...]))
    far = jnp.concatenate([far, jnp.zeros_like(far)], axis=0).T
    for x in range(2):
        for s in range(STATES):
            far_ref[x, s] = far[s * samples : (s + 1) * samples, x * samples : (x + 1) * samples]
    left, right = (col_at + blocks - 1 - FIRST_COL) % blocks, (col_at + blocks + 1 - FIRST_COL) % blocks
    has_left, has_right = jnp.where(col_at > 0, 1.0, 0.0), jnp.where(col_at < blocks - 1, 1.0, 0.0)
    own = own_ref[...]
    for x in range(2):
        from_left = has_left * got_ref[pl.ds(left * PIECE + 2 * WIDE + x, 1), :]
        from_right = has_right * got_ref[pl.ds(right * PIECE + 2 * WIDE + x, 1), :]
        mine = own[:, x * LANES : (x + 1) * LANES]
        whole = jnp.concatenate(
            [
                mine[2:3] + pltpu.roll(from_left, LANES - 2 * BLOCK, axis=1),
                mine[3:4] + pltpu.roll(from_left, LANES - 3 * BLOCK, axis=1),
                mine[4:8],
                mine[8:9] + from_right,
                mine[9:10] + pltpu.roll(from_right, LANES - BLOCK, axis=1),
                jnp.zeros((LANES - BLOCK, LANES), jnp.float32),
            ],
            axis=0,
        ).T
        for s in range(STATES):
            currents_ref[x, s] = whole[s * samples : s * samples + BLOCK, 0:BLOCK]


def spot():
    return lax.axis_index("row"), lax.axis_index("col")


HBM = pl.BlockSpec(memory_space=pltpu.HBM)


def call(kernel, out_shape, scratch=(), flops=0, size=0, grant=40960, **options):
    return pl.pallas_call(
        kernel,
        out_shape=out_shape,
        scratch_shapes=list(scratch),
        compiler_params=pltpu.CompilerParams(vmem_limit_bytes=grant * 1024),
        cost_estimate=pl.CostEstimate(flops=flops, bytes_accessed=size, transcendentals=0),
        **options,
    )


def exchange(pieces, axis, first):
    size = pieces.shape[0]
    order = [(first + k) % size for k in range(size)]
    return lax.all_to_all(pieces, axis, 0, 0, axis_index_groups=[order])


def body(row_blocks, col_blocks, place, active_flags, port_index, drive_weights, feed_table, cell_map, probe_weights):
    rows, cols = row_blocks * BLOCK, col_blocks * BLOCK
    samples = OVER * BLOCK
    f32, b16 = jnp.float32, jnp.bfloat16
    shape = jax.ShapeDtypeStruct
    taken = (
        drive_weights, active_flags, port_index,
        feed_table, cell_map, probe_weights, jnp.asarray(path_matrix(), b16),
    )
    packed = call(
        functools.partial(pack_kernel, place),
        shape((row_blocks, BLOCK, LANES), f32),
        scratch=[pltpu.VMEM(x.shape, x.dtype) for x in taken]
        + [
            pltpu.VMEM((144, cell_map.shape[1]), f32),
            pltpu.VMEM((ROWS, LANES), f32),
            pltpu.VMEM((BLOCK, LANES), f32),
            pltpu.SemaphoreType.DMA((3,)),
            pltpu.SemaphoreType.DMA((7,)),
        ],
        in_specs=[HBM] * 7,
        name="pack",
        grant=61440,
    )(*taken)
    cells = exchange(packed, "row", FIRST_ROW).reshape(rows, LANES)
    row_high, row_low, col_high, col_low = call(
        functools.partial(turn_kernel, place, rows, cols),
        (
            shape((2 * rows, 2 * LANES), b16),
            shape((2 * rows, 2 * LANES), b16),
            shape((2 * samples, col_blocks * PIECE), b16),
            shape((2 * samples, col_blocks * PIECE), b16),
        ),
        flops=2 * 80 * 2 * 1024 * 1024,
        size=5 * 1024 * 1024,
        name="turns",
    )()
    pieces, own = call(
        functools.partial(stencil_kernel, place, rows, cols),
        (shape((col_blocks * PIECE, LANES), f32), shape((16, 2 * LANES), f32)),
        scratch=[pltpu.VMEM((rows // LANES, BLOCK * ROWS, LANES), f32)],
        name="stencil",
    )(cells, row_high, row_low)
    got = exchange(pieces.reshape(col_blocks, PIECE // 2, 2, LANES), "col", FIRST_COL)
    return call(
        functools.partial(pattern_kernel, place, col_blocks),
        (shape((2, STATES, BLOCK, BLOCK), f32), shape((2, STATES, samples, samples), f32)),
        name="pattern",
    )(got.reshape(col_blocks * PIECE, LANES), own, col_high, col_low)


def solution(mesh):
    placed = (P("row", "col"), P("row", "col"), P(None, None, "row", "col"), P(), P(), P())
    return jax.shard_map(
        functools.partial(body, mesh.shape["row"], mesh.shape["col"], spot),
        mesh=mesh,
        in_specs=placed,
        out_specs=(P(None, None, "row", "col"), P(None, None, "row", "col")),
        check_vma=False,
    )
```

```python
import functools
import math

import jax
import jax.numpy as jnp
import numpy as np
from jax import lax
from jax.experimental import pallas as pl
from jax.experimental.pallas import tpu as pltpu
from jax.sharding import PartitionSpec as P

OVER = 4
PORTS = 8
STATES = 4
BLOCK = 8
REACH = 2
WIDE = 12
LANES = 128
ROW_ORDER = tuple((15 + k) % 32 for k in range(32))
COL_ORDER = tuple((14 + k) % 16 for k in range(16))
PIECE = 26
USED = 72

relaxation = 0.75
reflect_re = -0.3
reflect_im = 0.2

STEP = ((-1, 0), (1, 0), (0, -1), (0, 1))
PLACES = tuple(
    (dr, dc) for dr in range(-2, 3) for dc in range(-2, 3) if abs(dr) + abs(dc) <= 2
)
CLASSES = 13
SHARE = 52
ROWS = 32


def path_matrix():
    twice = relaxation * relaxation
    once = relaxation * (1.0 - relaxation) + relaxation
    mix = np.zeros((CLASSES * ROWS, 18 * 24), np.float32)

    def add(weight, first, second, place, kind):
        d = PLACES.index(place)
        for part, left, right, sign in ((0, 0, 0, 1), (0, 1, 1, -1), (1, 0, 1, 1), (1, 1, 0, 1)):
            at = 16 + right if second is None else right * 8 + second
            mix[kind * ROWS + part * 13 + d, (first * 2 + left) * 24 + at] += sign * weight

    def corner(e, f):
        return 9 + (min(e, f) % 2) * 2 + (max(e, f) % 2)

    add(1.0, 0, None, (0, 0), 0)
    for e in range(4):
        add(once, 0, e, STEP[e], 0)
        add(once, 0, 4 + e, (0, 0), 1 + e)
        for f in range(4):
            both = (STEP[e][0] + STEP[f][0], STEP[e][1] + STEP[f][1])
            crossed = e // 2 != f // 2
            add(twice, 1 + e, f, both, 0)
            if f == e ^ 1:
                add(-twice, 1 + e, f, both, 1 + e)
            if f != e:
                add(twice, 5 + e, f, STEP[f], 1 + e)
            if f == e:
                add(twice, 1 + e, 4 + f, STEP[e], 5 + e)
                add(twice, 5 + e, 4 + f, (0, 0), 1 + e)
            elif crossed:
                add(twice, 1 + e, 4 + f, STEP[e], 1 + f)
                add(twice, 5 + e, 4 + f, (0, 0), corner(e, f))
    return mix


def halves(value):
    high = value.astype(jnp.bfloat16)
    return high, (value - high.astype(jnp.float32)).astype(jnp.bfloat16)


def thirds(value):
    high, low = halves(value)
    return high, low, (value - high.astype(jnp.float32) - low.astype(jnp.float32)).astype(jnp.bfloat16)


def cosine(turns, length):
    centred = jnp.where(turns >= length // 2, length - turns, turns)
    angle = (length // 4 - centred).astype(jnp.float32) * (2.0 * math.pi / length)
    square = angle * angle
    value = 1.0 / 6227020800.0
    value = value * square - 1.0 / 39916800.0
    value = value * square + 1.0 / 362880.0
    value = value * square - 1.0 / 5040.0
    value = value * square + 1.0 / 120.0
    value = value * square - 1.0 / 6.0
    return angle + angle * square * value


def dot(left, right, dims=((1,), (0,))):
    return lax.dot_general(left, right, (dims, ((), ())), preferred_element_type=jnp.float32)


def dot3(left, right, dims=((1,), (0,))):
    high, low = left
    high_right, low_right = right
    both = dot(jnp.concatenate([high, low], axis=0), high_right, dims)
    size = high.shape[0]
    return both[:size] + (both[size:] + dot(high, low_right, dims))


def fetch(sems, *pairs, wait=False):
    copies = [pltpu.make_async_copy(src, dst, sems.at[i]) for i, (src, dst) in enumerate(pairs)]
    for copy in copies:
        copy.start()
    if wait:
        for copy in copies:
            copy.wait()
    return copies


def turn_kernel(place, rows, cols, row_high_ref, row_low_ref, col_high_ref, col_low_ref):
    row_at, col_at = place()
    span = OVER * rows
    r = lax.broadcasted_iota(jnp.int32, (rows, LANES), 0)
    k = lax.broadcasted_iota(jnp.int32, (rows, LANES), 1)
    samples = OVER * BLOCK
    turns = (r * (row_at * samples + k)) & (span - 1)
    cos = jnp.where(k < samples, cosine(turns, span), 0.0)
    sin = jnp.where(k < samples, cosine((turns - span // 4) & (span - 1), span), 0.0)
    pick = (k >= samples) & (k < samples + BLOCK) & (r == row_at * BLOCK + k - samples)
    pick = jnp.where(pick, 1.0, 0.0)
    turn = jnp.concatenate(
        [
            jnp.concatenate([cos + pick, -sin], axis=1),
            jnp.concatenate([sin, cos + pick], axis=1),
        ],
        axis=0,
    )
    row_high_ref[...], row_low_ref[...] = halves(turn)

    span = OVER * cols
    blocks = cols // BLOCK
    shape = (samples, blocks * PIECE)
    q = lax.broadcasted_iota(jnp.int32, shape, 0) + col_at * samples
    k = lax.broadcasted_iota(jnp.int32, shape, 1)
    block = jnp.full(shape, COL_ORDER[0], jnp.int32)
    at = k
    for b in range(1, blocks):
        block = block + jnp.where(k >= b * PIECE, COL_ORDER[b] - COL_ORDER[b - 1], 0)
        at = at - jnp.where(k >= b * PIECE, PIECE, 0)
    imaginary = at >= WIDE
    c = block * BLOCK + at - jnp.where(imaginary, WIDE, 0) - REACH
    inside = (at < 2 * WIDE) & (c >= 0) & (c < cols)
    turns = (q * c) & (span - 1)
    scale = (rows * cols) ** -0.5
    cos = jnp.where(inside, cosine(turns, span) * scale, 0.0)
    sin = jnp.where(inside, cosine((turns - span // 4) & (span - 1), span) * scale, 0.0)
    turn = jnp.concatenate([jnp.where(imaginary, sin, cos), jnp.where(imaginary, cos, -sin)], axis=0)
    col_high_ref[...], col_low_ref[...] = halves(turn)


def make_table(feed_hbm, map_hbm, probe_hbm, mix_hbm, table_ref, feed_ref, map_ref, probe_ref, mix_ref, hops_ref, sems):
    edge = feed_ref.shape[2] // 4
    chunks = [(map_hbm.at[:, pl.ds(a * edge, edge)], map_ref.at[:, pl.ds(a * edge, edge)]) for a in range(4)]
    copies = fetch(sems, (feed_hbm, feed_ref), (probe_hbm, probe_ref), *chunks, (mix_hbm, mix_ref))
    copies[0].wait()
    copies[1].wait()
    units = 4 * edge

    def block(value, e):
        return value[:, e * edge : (e + 1) * edge]

    feed_re, feed_im = feed_ref[0], feed_ref[1]
    back_re = reflect_re * feed_re - reflect_im * feed_im
    back_im = reflect_re * feed_im + reflect_im * feed_re
    hops_ref[0:8, :] = feed_re
    hops_ref[8:16, :] = feed_im
    for a in range(4):
        e = a ^ 1
        enter = jnp.concatenate(
            [block(feed_re, e), block(feed_im, e), block(back_re, a), block(back_im, a)], axis=0
        )
        enter = jnp.concatenate(halves(enter), axis=0)
        copies[2 + a].wait()
        by_re = dot(enter, map_ref[0, a * edge : (a + 1) * edge, :])
        by_im = dot(enter, map_ref[1, a * edge : (a + 1) * edge, :])
        by_re = by_re[0:32] + by_re[32:64]
        by_im = by_im[0:32] + by_im[32:64]
        for first, at in ((1 + e, 0), (5 + a, 16)):
            hops_ref[first * 16 : first * 16 + 8, :] = by_re[at : at + 8] - by_im[at + 8 : at + 16]
            hops_ref[first * 16 + 8 : first * 16 + 16, :] = (
                by_re[at + 8 : at + 16] + by_im[at : at + 8]
            )
    probe_re, probe_im = probe_ref[0:1, :], probe_ref[1:2, :]
    probes = jnp.concatenate(halves(jnp.concatenate([probe_re, probe_im] + [probe_re] * 6, axis=0)), axis=0)
    through_re = dot(probes, map_ref[0], ((1,), (1,)))
    through_im = dot(probes, map_ref[1], ((1,), (1,)))
    through_re = through_re[0:8] + through_re[8:16]
    through_im = through_im[0:8] + through_im[8:16]
    total_re = probe_re + through_re[0:1] - through_im[1:2]
    total_im = probe_im + through_im[0:1] + through_re[1:2]

    def swapped(value):
        return jnp.concatenate([block(value, e ^ 1) for e in range(4)], axis=1)

    sub = lax.broadcasted_iota(jnp.int32, (8, units), 0)
    lane = lax.broadcasted_iota(jnp.int32, (8, units), 1)
    own = lane // edge == sub % 4
    passed = sub < 4
    out_re = jnp.where(passed, swapped(total_re), reflect_re * total_re - reflect_im * total_im)
    out_im = jnp.where(passed, swapped(total_im), reflect_re * total_im + reflect_im * total_re)
    leave = jnp.concatenate(
        [
            jnp.where(own, out_re, 0.0),
            jnp.where(own, out_im, 0.0),
            jnp.where(sub == 0, probe_re, jnp.where(sub == 1, probe_im, 0.0)),
        ],
        axis=0,
    )
    products = dot3(halves(leave), halves(hops_ref[...]), ((1,), (1,)))
    copies[6].wait()
    flat = jnp.concatenate([products[:, 8 * k : 8 * k + 8] for k in range(18)], axis=0)
    table = dot(mix_ref[...], jnp.concatenate(thirds(flat), axis=1))
    table = table[:, 0:8] + table[:, 8:16] + table[:, 16:24]
    wide = [table[k * ROWS : (k + 1) * ROWS, :] for k in range(CLASSES)]
    wide.append(jnp.zeros((ROWS, LANES - 8 * CLASSES), jnp.float32))
    table_ref[...] = jnp.concatenate(wide, axis=1)


def maker(row_at):
    return row_at % 16 < 4, row_at % 4 + 4 * (row_at // 16)


def pack_kernel(
    place, drive_hbm, flag_hbm, port_hbm, feed_hbm, map_hbm, probe_hbm, mix_hbm, out_ref,
    drive_ref, flag_ref, port_ref, feed_ref, map_ref, probe_ref, mix_ref, hops_ref, table_ref, piece_ref, sems, table_sems,
):
    makes, share = maker(place()[0])
    fetch(sems, (drive_hbm, drive_ref), (flag_hbm, flag_ref), (port_hbm, port_ref), wait=True)
    active = flag_ref[...].astype(jnp.float32)
    pieces = [drive_ref[x, s] * active for x in range(2) for s in range(STATES)]
    pieces.append(port_ref[...].astype(jnp.float32))
    pieces.append(jnp.zeros((BLOCK, LANES - USED), jnp.float32))
    piece_ref[...] = jnp.concatenate(pieces, axis=1)

    @pl.when(makes)
    def _():
        make_table(
            feed_hbm, map_hbm, probe_hbm, mix_hbm, table_ref,
            feed_ref, map_ref, probe_ref, mix_ref, hops_ref, table_sems,
        )
        part = table_ref[pl.ds(pl.multiple_of(share // 2 * 8, 8), 8), :]
        part = jnp.where(share % 2 == 0, pltpu.roll(part, USED, axis=1), pltpu.roll(part, USED - SHARE, axis=1))
        lane = lax.broadcasted_iota(jnp.int32, (BLOCK, LANES), 1)
        piece_ref[...] += jnp.where((lane >= USED) & (lane < USED + SHARE), part, 0.0)

    out_ref[...] = jnp.broadcast_to(piece_ref[...][None], out_ref.shape)


def stencil_kernel(place, rows, cols, cells_ref, row_high_ref, row_low_ref, out_ref, own_ref, coef_ref):
    _, col_at = place()
    slots = [ROW_ORDER.index(k) * BLOCK for k in range(rows // BLOCK)]
    across = jnp.concatenate([cells_ref[k : k + BLOCK, :] for k in slots], axis=0).T
    amps = [[across[(x * 4 + s) * 8 : (x * 4 + s) * 8 + 8] for s in range(STATES)] for x in range(2)]
    ports = across[64:72]

    sub = lax.broadcasted_iota(jnp.int32, (8, rows), 0).astype(jnp.float32)
    r = lax.broadcasted_iota(jnp.int32, (8, rows), 1)

    def flag(mask):
        return jnp.where(mask, 1.0, 0.0)

    north, south, north2, south2 = flag(r == 0), flag(r == rows - 1), flag(r == 1), flag(r == rows - 2)
    lane = lax.broadcasted_iota(jnp.int32, (BLOCK, LANES), 1)
    makers = [slots[k % 4 + 16 * (k // 4)] for k in range(8)]
    parts = [cells_ref[k : k + BLOCK, :] for k in makers]
    firsts = [jnp.where(lane < SHARE, pltpu.roll(part, LANES - USED, axis=1), 0.0) for part in parts[0::2]]
    seconds = [
        jnp.where((lane >= SHARE) & (lane < 2 * SHARE), pltpu.roll(part, LANES - USED + SHARE, axis=1), 0.0)
        for part in parts[1::2]
    ]
    table = jnp.concatenate(halves(jnp.concatenate([a + b for a, b in zip(firsts, seconds)], axis=0)), axis=0)
    for j in range(BLOCK):
        c = col_at * BLOCK + j
        west, east = flag(c == 0), flag(c == cols - 1)
        west2, east2 = flag(c == 1), flag(c == cols - 2)
        chosen = flag(jnp.broadcast_to(ports[j : j + 1], (8, rows)) == sub)
        at_north, at_south = chosen * north, chosen * south
        kinds = [
            chosen, at_north, at_south, chosen * west, chosen * east,
            chosen * north2, chosen * south2, chosen * west2, chosen * east2,
            at_north * west, at_north * east, at_south * west, at_south * east,
            jnp.zeros((LANES - 8 * CLASSES, rows), jnp.float32),
        ]
        found = dot(table, jnp.concatenate(kinds, axis=0).astype(jnp.bfloat16))
        found = found[0:ROWS] + found[ROWS : 2 * ROWS]
        for half in range(rows // LANES):
            coef_ref[half, j * ROWS : (j + 1) * ROWS, :] = found[:, half * LANES : (half + 1) * LANES]

    def coef(index):
        return jnp.concatenate(
            [coef_ref[half, pl.ds(index, 8, stride=ROWS), :] for half in range(rows // LANES)], axis=1
        )

    def moved(value, dr):
        if dr == 0:
            return value
        value = pltpu.roll(value, dr % rows, axis=1)
        return jnp.where(r >= dr if dr > 0 else r < rows + dr, value, 0.0)

    sums = {}
    for d, (dr, dc) in enumerate(PLACES):
        k_re, k_im = coef(d), coef(13 + d)
        for s in range(STATES):
            a_re, a_im = amps[0][s], amps[1][s]
            for x, value in ((0, k_re * a_re - k_im * a_im), (1, k_re * a_im + k_im * a_re)):
                value = moved(value, dr)
                key = (dc, s, x)
                sums[key] = sums[key] + value if key in sums else value

    spread = jnp.concatenate(
        [
            jnp.concatenate([sums[dc, s, 0], sums[dc, s, 1]], axis=1)
            for dc in range(-2, 3)
            for s in range(STATES)
        ],
        axis=0,
    )
    turned = dot3(halves(spread), (row_high_ref[...], row_low_ref[...]))
    samples = OVER * BLOCK
    lane = lax.broadcasted_iota(jnp.int32, (8, LANES), 1)
    first, second = lane < samples, (lane >= samples) & (lane < samples + BLOCK)
    nothing = jnp.zeros((16, LANES), jnp.float32)
    mains, nears = [], []
    for x in range(2):
        main, near = nothing, nothing
        for i, dc in enumerate(range(-2, 3)):
            wave, own = jnp.zeros((8, LANES), jnp.float32), jnp.zeros((8, LANES), jnp.float32)
            for s in range(STATES):
                part = turned[(i * STATES + s) * 8 : (i * STATES + s) * 8 + 8, x * LANES : (x + 1) * LANES]
                a, b = jnp.where(first, part, 0.0), jnp.where(second, part, 0.0)
                wave = wave + (pltpu.roll(a, s * samples, axis=1) if s else a)
                own = own + pltpu.roll(b, (s - 1) * samples % LANES, axis=1) if s != 1 else own + b
            for_main = jnp.concatenate([wave, jnp.zeros((8, LANES), jnp.float32)], axis=0)
            for_near = jnp.concatenate([own, jnp.zeros((8, LANES), jnp.float32)], axis=0)
            shift = REACH + dc
            main = main + (pltpu.roll(for_main, shift, axis=0) if shift else for_main)
            near = near + (pltpu.roll(for_near, shift, axis=0) if shift else for_near)
        mains.append(main[0:WIDE])
        nears.append(
            near[0:1] + pltpu.roll(near, BLOCK, axis=1)[1:2]
            + pltpu.roll(near, 2 * BLOCK, axis=1)[10:11] + pltpu.roll(near, 3 * BLOCK, axis=1)[11:12]
        )
        own_ref[:, x * LANES : (x + 1) * LANES] = near
    piece = jnp.concatenate(mains + nears, axis=0)
    four = jnp.concatenate([piece] * 4, axis=0)
    for i in range(out_ref.shape[0] // (4 * PIECE)):
        out_ref[i * 4 * PIECE : (i + 1) * 4 * PIECE, :] = four


def pattern_kernel(place, blocks, got_ref, own_ref, col_high_ref, col_low_ref, currents_ref, far_ref):
    _, col_at = place()
    samples = OVER * BLOCK
    far = dot3((col_high_ref[...], col_low_ref[...]), halves(got_ref[...]))
    far = jnp.concatenate([far, jnp.zeros_like(far)], axis=0).T
    for x in range(2):
        for s in range(STATES):
            far_ref[x, s] = far[s * samples : (s + 1) * samples, x * samples : (x + 1) * samples]
    left, right = 0, 0
    for b in range(blocks):
        left = jnp.where(col_at == b + 1, COL_ORDER.index(b), left)
        right = jnp.where(col_at == b - 1, COL_ORDER.index(b), right)
    has_left, has_right = jnp.where(col_at > 0, 1.0, 0.0), jnp.where(col_at < blocks - 1, 1.0, 0.0)
    own = own_ref[...]
    for x in range(2):
        from_left = has_left * got_ref[pl.ds(left * PIECE + 2 * WIDE + x, 1), :]
        from_right = has_right * got_ref[pl.ds(right * PIECE + 2 * WIDE + x, 1), :]
        mine = own[:, x * LANES : (x + 1) * LANES]
        whole = jnp.concatenate(
            [
                mine[2:3] + pltpu.roll(from_left, LANES - 2 * BLOCK, axis=1),
                mine[3:4] + pltpu.roll(from_left, LANES - 3 * BLOCK, axis=1),
                mine[4:8],
                mine[8:9] + from_right,
                mine[9:10] + pltpu.roll(from_right, LANES - BLOCK, axis=1),
                jnp.zeros((LANES - BLOCK, LANES), jnp.float32),
            ],
            axis=0,
        ).T
        for s in range(STATES):
            currents_ref[x, s] = whole[s * samples : s * samples + BLOCK, 0:BLOCK]


def spot():
    return lax.axis_index("row"), lax.axis_index("col")


HBM = pl.BlockSpec(memory_space=pltpu.HBM)


def call(kernel, out_shape, scratch=(), flops=0, size=0, grant=40960, **options):
    return pl.pallas_call(
        kernel,
        out_shape=out_shape,
        scratch_shapes=list(scratch),
        compiler_params=pltpu.CompilerParams(vmem_limit_bytes=grant * 1024),
        cost_estimate=pl.CostEstimate(flops=flops, bytes_accessed=size, transcendentals=0),
        **options,
    )


def exchange(pieces, axis, order):
    return lax.all_to_all(pieces, axis, 0, 0, axis_index_groups=[list(order)])


def body(row_blocks, col_blocks, place, active_flags, port_index, drive_weights, feed_table, cell_map, probe_weights):
    rows, cols = row_blocks * BLOCK, col_blocks * BLOCK
    samples = OVER * BLOCK
    f32, b16 = jnp.float32, jnp.bfloat16
    shape = jax.ShapeDtypeStruct
    taken = (
        drive_weights, active_flags, port_index,
        feed_table, cell_map, probe_weights, jnp.asarray(path_matrix(), b16),
    )
    packed = call(
        functools.partial(pack_kernel, place),
        shape((row_blocks, BLOCK, LANES), f32),
        scratch=[pltpu.VMEM(x.shape, x.dtype) for x in taken]
        + [
            pltpu.VMEM((144, cell_map.shape[1]), f32),
            pltpu.VMEM((ROWS, LANES), f32),
            pltpu.VMEM((BLOCK, LANES), f32),
            pltpu.SemaphoreType.DMA((3,)),
            pltpu.SemaphoreType.DMA((7,)),
        ],
        in_specs=[HBM] * 7,
        name="pack",
        grant=61440,
    )(*taken)
    cells = exchange(packed, "row", ROW_ORDER).reshape(rows, LANES)
    row_high, row_low, col_high, col_low = call(
        functools.partial(turn_kernel, place, rows, cols),
        (
            shape((2 * rows, 2 * LANES), b16),
            shape((2 * rows, 2 * LANES), b16),
            shape((2 * samples, col_blocks * PIECE), b16),
            shape((2 * samples, col_blocks * PIECE), b16),
        ),
        flops=2 * 80 * 2 * 1024 * 1024,
        size=5 * 1024 * 1024,
        name="turns",
    )()
    pieces, own = call(
        functools.partial(stencil_kernel, place, rows, cols),
        (shape((col_blocks * PIECE, LANES), f32), shape((16, 2 * LANES), f32)),
        scratch=[pltpu.VMEM((rows // LANES, BLOCK * ROWS, LANES), f32)],
        name="stencil",
    )(cells, row_high, row_low)
    got = exchange(pieces.reshape(col_blocks, PIECE // 2, 2, LANES), "col", COL_ORDER)
    return call(
        functools.partial(pattern_kernel, place, col_blocks),
        (shape((2, STATES, BLOCK, BLOCK), f32), shape((2, STATES, samples, samples), f32)),
        name="pattern",
    )(got.reshape(col_blocks * PIECE, LANES), own, col_high, col_low)


def solution(mesh):
    placed = (P("row", "col"), P("row", "col"), P(None, None, "row", "col"), P(), P(), P())
    return jax.shard_map(
        functools.partial(body, mesh.shape["row"], mesh.shape["col"], spot),
        mesh=mesh,
        in_specs=placed,
        out_specs=(P(None, None, "row", "col"), P(None, None, "row", "col")),
        check_vma=False,
    )
```

```python
import functools
import math

import jax
import jax.numpy as jnp
import numpy as np
from jax import lax
from jax.experimental import pallas as pl
from jax.experimental.pallas import tpu as pltpu
from jax.sharding import PartitionSpec as P

OVER = 4
PORTS = 8
STATES = 4
BLOCK = 8
REACH = 2
WIDE = 12
LANES = 128
ROW_ORDER = tuple((15 + k) % 32 for k in range(32))
COL_ORDER = tuple((14 + k) % 16 for k in range(16))
PIECE = 26
USED = 72

relaxation = 0.75
reflect_re = -0.3
reflect_im = 0.2

STEP = ((-1, 0), (1, 0), (0, -1), (0, 1))
PLACES = tuple(
    (dr, dc) for dr in range(-2, 3) for dc in range(-2, 3) if abs(dr) + abs(dc) <= 2
)
CLASSES = 13
SHARE = 52
ROWS = 32


def path_matrix():
    twice = relaxation * relaxation
    once = relaxation * (1.0 - relaxation) + relaxation
    mix = np.zeros((CLASSES * ROWS, 18 * 24), np.float32)

    def add(weight, first, second, place, kind):
        d = PLACES.index(place)
        for part, left, right, sign in ((0, 0, 0, 1), (0, 1, 1, -1), (1, 0, 1, 1), (1, 1, 0, 1)):
            at = 16 + right if second is None else right * 8 + second
            mix[kind * ROWS + part * 13 + d, (first * 2 + left) * 24 + at] += sign * weight

    def corner(e, f):
        return 9 + (min(e, f) % 2) * 2 + (max(e, f) % 2)

    add(1.0, 0, None, (0, 0), 0)
    for e in range(4):
        add(once, 0, e, STEP[e], 0)
        add(once, 0, 4 + e, (0, 0), 1 + e)
        for f in range(4):
            both = (STEP[e][0] + STEP[f][0], STEP[e][1] + STEP[f][1])
            crossed = e // 2 != f // 2
            add(twice, 1 + e, f, both, 0)
            if f == e ^ 1:
                add(-twice, 1 + e, f, both, 1 + e)
            if f != e:
                add(twice, 5 + e, f, STEP[f], 1 + e)
            if f == e:
                add(twice, 1 + e, 4 + f, STEP[e], 5 + e)
                add(twice, 5 + e, 4 + f, (0, 0), 1 + e)
            elif crossed:
                add(twice, 1 + e, 4 + f, STEP[e], 1 + f)
                add(twice, 5 + e, 4 + f, (0, 0), corner(e, f))
    return mix


def halves(value):
    high = value.astype(jnp.bfloat16)
    return high, (value - high.astype(jnp.float32)).astype(jnp.bfloat16)


def thirds(value):
    high, low = halves(value)
    return high, low, (value - high.astype(jnp.float32) - low.astype(jnp.float32)).astype(jnp.bfloat16)


def cosine(turns, length):
    centred = jnp.where(turns >= length // 2, length - turns, turns)
    angle = (length // 4 - centred).astype(jnp.float32) * (2.0 * math.pi / length)
    square = angle * angle
    value = 1.0 / 6227020800.0
    value = value * square - 1.0 / 39916800.0
    value = value * square + 1.0 / 362880.0
    value = value * square - 1.0 / 5040.0
    value = value * square + 1.0 / 120.0
    value = value * square - 1.0 / 6.0
    return angle + angle * square * value


def dot(left, right, dims=((1,), (0,))):
    return lax.dot_general(left, right, (dims, ((), ())), preferred_element_type=jnp.float32)


def dot3(left, right, dims=((1,), (0,))):
    high, low = left
    high_right, low_right = right
    both = dot(jnp.concatenate([high, low], axis=0), high_right, dims)
    size = high.shape[0]
    return both[:size] + (both[size:] + dot(high, low_right, dims))


def fetch(sems, *pairs):
    copies = [pltpu.make_async_copy(src, dst, sems.at[i]) for i, (src, dst) in enumerate(pairs)]
    for copy in copies:
        copy.start()
    return copies


def make_turns(place, rows, cols, row_high_ref, row_low_ref, col_high_ref, col_low_ref):
    row_at, col_at = place()
    span = OVER * rows
    r = lax.broadcasted_iota(jnp.int32, (rows, LANES), 0)
    k = lax.broadcasted_iota(jnp.int32, (rows, LANES), 1)
    samples = OVER * BLOCK
    turns = (r * (row_at * samples + k)) & (span - 1)
    cos = jnp.where(k < samples, cosine(turns, span), 0.0)
    sin = jnp.where(k < samples, cosine((turns - span // 4) & (span - 1), span), 0.0)
    pick = (k >= samples) & (k < samples + BLOCK) & (r == row_at * BLOCK + k - samples)
    pick = jnp.where(pick, 1.0, 0.0)
    turn = jnp.concatenate(
        [
            jnp.concatenate([cos + pick, -sin], axis=1),
            jnp.concatenate([sin, cos + pick], axis=1),
        ],
        axis=0,
    )
    row_high_ref[...], row_low_ref[...] = halves(turn)

    span = OVER * cols
    blocks = cols // BLOCK
    shape = (samples, blocks * PIECE)
    q = lax.broadcasted_iota(jnp.int32, shape, 0) + col_at * samples
    k = lax.broadcasted_iota(jnp.int32, shape, 1)
    block = jnp.full(shape, COL_ORDER[0], jnp.int32)
    at = k
    for b in range(1, blocks):
        block = block + jnp.where(k >= b * PIECE, COL_ORDER[b] - COL_ORDER[b - 1], 0)
        at = at - jnp.where(k >= b * PIECE, PIECE, 0)
    imaginary = at >= WIDE
    c = block * BLOCK + at - jnp.where(imaginary, WIDE, 0) - REACH
    inside = (at < 2 * WIDE) & (c >= 0) & (c < cols)
    turns = (q * c) & (span - 1)
    scale = (rows * cols) ** -0.5
    cos = jnp.where(inside, cosine(turns, span) * scale, 0.0)
    sin = jnp.where(inside, cosine((turns - span // 4) & (span - 1), span) * scale, 0.0)
    turn = jnp.concatenate([jnp.where(imaginary, sin, cos), jnp.where(imaginary, cos, -sin)], axis=0)
    col_high_ref[...], col_low_ref[...] = halves(turn)


def make_table(feed_hbm, map_hbm, probe_hbm, mix_hbm, table_ref, feed_ref, map_ref, probe_ref, mix_ref, hops_ref, sems):
    edge = feed_ref.shape[2] // 4
    chunks = [(map_hbm.at[:, pl.ds(a * edge, edge)], map_ref.at[:, pl.ds(a * edge, edge)]) for a in range(4)]
    copies = fetch(sems, (feed_hbm, feed_ref), (probe_hbm, probe_ref), *chunks, (mix_hbm, mix_ref))
    copies[0].wait()
    copies[1].wait()
    units = 4 * edge

    def block(value, e):
        return value[:, e * edge : (e + 1) * edge]

    feed_re, feed_im = feed_ref[0], feed_ref[1]
    back_re = reflect_re * feed_re - reflect_im * feed_im
    back_im = reflect_re * feed_im + reflect_im * feed_re
    hops_ref[0:8, :] = feed_re
    hops_ref[8:16, :] = feed_im
    for a in range(4):
        e = a ^ 1
        enter = jnp.concatenate(
            [block(feed_re, e), block(feed_im, e), block(back_re, a), block(back_im, a)], axis=0
        )
        enter = jnp.concatenate(halves(enter), axis=0)
        copies[2 + a].wait()
        by_re = dot(enter, map_ref[0, a * edge : (a + 1) * edge, :])
        by_im = dot(enter, map_ref[1, a * edge : (a + 1) * edge, :])
        by_re = by_re[0:32] + by_re[32:64]
        by_im = by_im[0:32] + by_im[32:64]
        for first, at in ((1 + e, 0), (5 + a, 16)):
            hops_ref[first * 16 : first * 16 + 8, :] = by_re[at : at + 8] - by_im[at + 8 : at + 16]
            hops_ref[first * 16 + 8 : first * 16 + 16, :] = (
                by_re[at + 8 : at + 16] + by_im[at : at + 8]
            )
    probe_re, probe_im = probe_ref[0:1, :], probe_ref[1:2, :]
    probes = jnp.concatenate(halves(jnp.concatenate([probe_re, probe_im] + [probe_re] * 6, axis=0)), axis=0)
    through_re = dot(probes, map_ref[0], ((1,), (1,)))
    through_im = dot(probes, map_ref[1], ((1,), (1,)))
    through_re = through_re[0:8] + through_re[8:16]
    through_im = through_im[0:8] + through_im[8:16]
    total_re = probe_re + through_re[0:1] - through_im[1:2]
    total_im = probe_im + through_im[0:1] + through_re[1:2]

    def swapped(value):
        return jnp.concatenate([block(value, e ^ 1) for e in range(4)], axis=1)

    sub = lax.broadcasted_iota(jnp.int32, (8, units), 0)
    lane = lax.broadcasted_iota(jnp.int32, (8, units), 1)
    own = lane // edge == sub % 4
    passed = sub < 4
    out_re = jnp.where(passed, swapped(total_re), reflect_re * total_re - reflect_im * total_im)
    out_im = jnp.where(passed, swapped(total_im), reflect_re * total_im + reflect_im * total_re)
    leave = jnp.concatenate(
        [
            jnp.where(own, out_re, 0.0),
            jnp.where(own, out_im, 0.0),
            jnp.where(sub == 0, probe_re, jnp.where(sub == 1, probe_im, 0.0)),
        ],
        axis=0,
    )
    products = dot3(halves(leave), halves(hops_ref[...]), ((1,), (1,)))
    copies[6].wait()
    flat = jnp.concatenate([products[:, 8 * k : 8 * k + 8] for k in range(18)], axis=0)
    table = dot(mix_ref[...], jnp.concatenate(thirds(flat), axis=1))
    table = table[:, 0:8] + table[:, 8:16] + table[:, 16:24]
    wide = [table[k * ROWS : (k + 1) * ROWS, :] for k in range(CLASSES)]
    wide.append(jnp.zeros((ROWS, LANES - 8 * CLASSES), jnp.float32))
    table_ref[...] = jnp.concatenate(wide, axis=1)


def maker(row_at):
    return row_at % 16 < 4, row_at % 4 + 4 * (row_at // 16)


def pack_kernel(
    place, rows, cols, drive_hbm, flag_hbm, port_hbm, feed_hbm, map_hbm, probe_hbm, mix_hbm,
    out_ref, row_high_ref, row_low_ref, col_high_ref, col_low_ref,
    drive_ref, flag_ref, port_ref, feed_ref, map_ref, probe_ref, mix_ref, hops_ref, table_ref, piece_ref, sems, table_sems,
):
    makes, share = maker(place()[0])
    copies = fetch(sems, (drive_hbm, drive_ref), (flag_hbm, flag_ref), (port_hbm, port_ref))
    make_turns(place, rows, cols, row_high_ref, row_low_ref, col_high_ref, col_low_ref)
    for copy in copies:
        copy.wait()
    active = flag_ref[...].astype(jnp.float32)
    pieces = [drive_ref[x, s] * active for x in range(2) for s in range(STATES)]
    pieces.append(port_ref[...].astype(jnp.float32))
    pieces.append(jnp.zeros((BLOCK, LANES - USED), jnp.float32))
    piece_ref[...] = jnp.concatenate(pieces, axis=1)

    @pl.when(makes)
    def _():
        make_table(
            feed_hbm, map_hbm, probe_hbm, mix_hbm, table_ref,
            feed_ref, map_ref, probe_ref, mix_ref, hops_ref, table_sems,
        )
        part = table_ref[pl.ds(pl.multiple_of(share // 2 * 8, 8), 8), :]
        part = jnp.where(share % 2 == 0, pltpu.roll(part, USED, axis=1), pltpu.roll(part, USED - SHARE, axis=1))
        lane = lax.broadcasted_iota(jnp.int32, (BLOCK, LANES), 1)
        piece_ref[...] += jnp.where((lane >= USED) & (lane < USED + SHARE), part, 0.0)

    out_ref[...] = jnp.broadcast_to(piece_ref[...][None], out_ref.shape)


def stencil_kernel(place, rows, cols, cells_ref, row_high_ref, row_low_ref, out_ref, own_ref, coef_ref):
    _, col_at = place()
    slots = [ROW_ORDER.index(k) * BLOCK for k in range(rows // BLOCK)]
    across = jnp.concatenate([cells_ref[k : k + BLOCK, :] for k in slots], axis=0).T
    amps = [[across[(x * 4 + s) * 8 : (x * 4 + s) * 8 + 8] for s in range(STATES)] for x in range(2)]
    ports = across[64:72]

    sub = lax.broadcasted_iota(jnp.int32, (8, rows), 0).astype(jnp.float32)
    r = lax.broadcasted_iota(jnp.int32, (8, rows), 1)

    def flag(mask):
        return jnp.where(mask, 1.0, 0.0)

    none = jnp.zeros((8, rows), jnp.float32)
    north, south, north2, south2 = flag(r == 0), flag(r == rows - 1), flag(r == 1), flag(r == rows - 2)
    lane = lax.broadcasted_iota(jnp.int32, (BLOCK, LANES), 1)
    makers = [slots[k % 4 + 16 * (k // 4)] for k in range(8)]
    parts = [cells_ref[k : k + BLOCK, :] for k in makers]
    firsts = [jnp.where(lane < SHARE, pltpu.roll(part, LANES - USED, axis=1), 0.0) for part in parts[0::2]]
    seconds = [
        jnp.where((lane >= SHARE) & (lane < 2 * SHARE), pltpu.roll(part, LANES - USED + SHARE, axis=1), 0.0)
        for part in parts[1::2]
    ]
    table = jnp.concatenate(halves(jnp.concatenate([a + b for a, b in zip(firsts, seconds)], axis=0)), axis=0)
    for j in range(BLOCK):
        c = col_at * BLOCK + j
        chosen = flag(jnp.broadcast_to(ports[j : j + 1], (8, rows)) == sub)
        at_north, at_south = chosen * north, chosen * south
        kinds = [chosen, at_north, at_south, none, none, chosen * north2, chosen * south2] + [none] * 6
        if j in (0, BLOCK - 1):
            edge, first, second = (flag(c == 0), 9, 11) if j == 0 else (flag(c == cols - 1), 10, 12)
            kinds[3 if j == 0 else 4] = chosen * edge
            kinds[first], kinds[second] = at_north * edge, at_south * edge
        if j in (1, BLOCK - 2):
            kinds[7 if j == 1 else 8] = chosen * (flag(c == 1) if j == 1 else flag(c == cols - 2))
        kinds.append(jnp.zeros((LANES - 8 * CLASSES, rows), jnp.float32))
        found = dot(table, jnp.concatenate(kinds, axis=0).astype(jnp.bfloat16))
        found = found[0:ROWS] + found[ROWS : 2 * ROWS]
        for half in range(rows // LANES):
            coef_ref[half, j * ROWS : (j + 1) * ROWS, :] = found[:, half * LANES : (half + 1) * LANES]

    def coef(index):
        return jnp.concatenate(
            [coef_ref[half, pl.ds(index, 8, stride=ROWS), :] for half in range(rows // LANES)], axis=1
        )

    def moved(value, dr):
        if dr == 0:
            return value
        value = pltpu.roll(value, dr % rows, axis=1)
        return jnp.where(r >= dr if dr > 0 else r < rows + dr, value, 0.0)

    sums = {}
    for d, (dr, dc) in enumerate(PLACES):
        k_re, k_im = coef(d), coef(13 + d)
        for s in range(STATES):
            a_re, a_im = amps[0][s], amps[1][s]
            for x, value in ((0, k_re * a_re - k_im * a_im), (1, k_re * a_im + k_im * a_re)):
                value = moved(value, dr)
                key = (dc, s, x)
                sums[key] = sums[key] + value if key in sums else value

    spread = jnp.concatenate(
        [
            jnp.concatenate([sums[dc, s, 0], sums[dc, s, 1]], axis=1)
            for dc in range(-2, 3)
            for s in range(STATES)
        ],
        axis=0,
    )
    turned = dot3(halves(spread), (row_high_ref[...], row_low_ref[...]))
    samples = OVER * BLOCK
    lane = lax.broadcasted_iota(jnp.int32, (8, LANES), 1)
    first, second = lane < samples, (lane >= samples) & (lane < samples + BLOCK)
    nothing = jnp.zeros((16, LANES), jnp.float32)
    mains, nears = [], []
    for x in range(2):
        main, near = nothing, nothing
        for i, dc in enumerate(range(-2, 3)):
            wave, own = jnp.zeros((8, LANES), jnp.float32), jnp.zeros((8, LANES), jnp.float32)
            for s in range(STATES):
                part = turned[(i * STATES + s) * 8 : (i * STATES + s) * 8 + 8, x * LANES : (x + 1) * LANES]
                a, b = jnp.where(first, part, 0.0), jnp.where(second, part, 0.0)
                wave = wave + (pltpu.roll(a, s * samples, axis=1) if s else a)
                own = own + pltpu.roll(b, (s - 1) * samples % LANES, axis=1) if s != 1 else own + b
            for_main = jnp.concatenate([wave, jnp.zeros((8, LANES), jnp.float32)], axis=0)
            for_near = jnp.concatenate([own, jnp.zeros((8, LANES), jnp.float32)], axis=0)
            shift = REACH + dc
            main = main + (pltpu.roll(for_main, shift, axis=0) if shift else for_main)
            near = near + (pltpu.roll(for_near, shift, axis=0) if shift else for_near)
        mains.append(main[0:WIDE])
        nears.append(
            near[0:1] + pltpu.roll(near, BLOCK, axis=1)[1:2]
            + pltpu.roll(near, 2 * BLOCK, axis=1)[10:11] + pltpu.roll(near, 3 * BLOCK, axis=1)[11:12]
        )
        own_ref[:, x * LANES : (x + 1) * LANES] = near
    piece = jnp.concatenate(mains + nears, axis=0)
    four = jnp.concatenate([piece] * 4, axis=0)
    for i in range(out_ref.shape[0] // (4 * PIECE)):
        out_ref[i * 4 * PIECE : (i + 1) * 4 * PIECE, :] = four


def pattern_kernel(place, blocks, got_ref, own_ref, col_high_ref, col_low_ref, currents_ref, far_ref):
    _, col_at = place()
    samples = OVER * BLOCK
    far = dot3((col_high_ref[...], col_low_ref[...]), halves(got_ref[...]))
    left, right = 0, 0
    for b in range(blocks):
        left = jnp.where(col_at == b + 1, COL_ORDER.index(b), left)
        right = jnp.where(col_at == b - 1, COL_ORDER.index(b), right)
    has_left, has_right = jnp.where(col_at > 0, 1.0, 0.0), jnp.where(col_at < blocks - 1, 1.0, 0.0)
    own = own_ref[...]
    stacked = [far]
    for x in range(2):
        from_left = has_left * got_ref[pl.ds(left * PIECE + 2 * WIDE + x, 1), :]
        from_right = has_right * got_ref[pl.ds(right * PIECE + 2 * WIDE + x, 1), :]
        mine = own[:, x * LANES : (x + 1) * LANES]
        stacked += [
            mine[2:3] + pltpu.roll(from_left, LANES - 2 * BLOCK, axis=1),
            mine[3:4] + pltpu.roll(from_left, LANES - 3 * BLOCK, axis=1),
            mine[4:8],
            mine[8:9] + from_right,
            mine[9:10] + pltpu.roll(from_right, LANES - BLOCK, axis=1),
        ]
    stacked.append(jnp.zeros((LANES - 2 * samples - 2 * BLOCK, LANES), jnp.float32))
    flat = jnp.concatenate(stacked, axis=0).T
    for x in range(2):
        at = 2 * samples + x * BLOCK
        for s in range(STATES):
            far_ref[x, s] = flat[s * samples : (s + 1) * samples, x * samples : (x + 1) * samples]
            currents_ref[x, s] = flat[s * samples : s * samples + BLOCK, at : at + BLOCK]


def spot():
    return lax.axis_index("row"), lax.axis_index("col")


HBM = pl.BlockSpec(memory_space=pltpu.HBM)


def call(kernel, out_shape, scratch=(), flops=0, size=0, grant=40960, **options):
    return pl.pallas_call(
        kernel,
        out_shape=out_shape,
        scratch_shapes=list(scratch),
        compiler_params=pltpu.CompilerParams(vmem_limit_bytes=grant * 1024),
        cost_estimate=pl.CostEstimate(flops=flops, bytes_accessed=size, transcendentals=0),
        **options,
    )


def exchange(pieces, axis, order):
    return lax.all_to_all(pieces, axis, 0, 0, axis_index_groups=[list(order)])


def body(row_blocks, col_blocks, place, active_flags, port_index, drive_weights, feed_table, cell_map, probe_weights):
    rows, cols = row_blocks * BLOCK, col_blocks * BLOCK
    samples = OVER * BLOCK
    f32, b16 = jnp.float32, jnp.bfloat16
    shape = jax.ShapeDtypeStruct
    taken = (
        drive_weights, active_flags, port_index,
        feed_table, cell_map, probe_weights, jnp.asarray(path_matrix(), b16),
    )
    packed, row_high, row_low, col_high, col_low = call(
        functools.partial(pack_kernel, place, rows, cols),
        (
            pltpu.VMEM((row_blocks, BLOCK, LANES), f32),
            pltpu.VMEM((2 * rows, 2 * LANES), b16),
            pltpu.VMEM((2 * rows, 2 * LANES), b16),
            pltpu.VMEM((2 * samples, col_blocks * PIECE), b16),
            pltpu.VMEM((2 * samples, col_blocks * PIECE), b16),
        ),
        scratch=[pltpu.VMEM(x.shape, x.dtype) for x in taken]
        + [
            pltpu.VMEM((144, cell_map.shape[1]), f32),
            pltpu.VMEM((ROWS, LANES), f32),
            pltpu.VMEM((BLOCK, LANES), f32),
            pltpu.SemaphoreType.DMA((3,)),
            pltpu.SemaphoreType.DMA((7,)),
        ],
        in_specs=[HBM] * 7,
        name="pack",
        grant=57344,
    )(*taken)
    cells = exchange(packed, "row", ROW_ORDER).reshape(rows, LANES)
    pieces, own = call(
        functools.partial(stencil_kernel, place, rows, cols),
        (shape((col_blocks * PIECE, LANES), f32), shape((16, 2 * LANES), f32)),
        scratch=[pltpu.VMEM((rows // LANES, BLOCK * ROWS, LANES), f32)],
        name="stencil",
    )(cells, row_high, row_low)
    got = exchange(pieces.reshape(col_blocks, PIECE // 2, 2, LANES), "col", COL_ORDER)
    return call(
        functools.partial(pattern_kernel, place, col_blocks),
        (shape((2, STATES, BLOCK, BLOCK), f32), shape((2, STATES, samples, samples), f32)),
        name="pattern",
    )(got.reshape(col_blocks * PIECE, LANES), own, col_high, col_low)


def solution(mesh):
    placed = (P("row", "col"), P("row", "col"), P(None, None, "row", "col"), P(), P(), P())
    return jax.shard_map(
        functools.partial(body, mesh.shape["row"], mesh.shape["col"], spot),
        mesh=mesh,
        in_specs=placed,
        out_specs=(P(None, None, "row", "col"), P(None, None, "row", "col")),
        check_vma=False,
    )
```

```python
import functools
import math

import jax
import jax.numpy as jnp
import numpy as np
from jax import lax
from jax.experimental import pallas as pl
from jax.experimental.pallas import tpu as pltpu
from jax.sharding import PartitionSpec as P

OVER = 4
PORTS = 8
STATES = 4
BLOCK = 8
REACH = 2
WIDE = 12
LANES = 128
ROW_ORDER = tuple((15 + k) % 32 for k in range(32))
COL_ORDER = (14, 4, 5, 7, 6, 0, 1, 3, 8, 9, 11, 2, 10, 12, 13, 15)
MAKERS = (5, 1, 2, 3, 16, 17, 18, 19)
PIECE = 26
USED = 72

relaxation = 0.75
reflect_re = -0.3
reflect_im = 0.2

STEP = ((-1, 0), (1, 0), (0, -1), (0, 1))
PLACES = tuple(
    (dr, dc) for dr in range(-2, 3) for dc in range(-2, 3) if abs(dr) + abs(dc) <= 2
)
CLASSES = 13
SHARE = 52
ROWS = 32


def path_matrix():
    twice = relaxation * relaxation
    once = relaxation * (1.0 - relaxation) + relaxation
    mix = np.zeros((CLASSES * ROWS, 18 * 24), np.float32)

    def add(weight, first, second, place, kind):
        d = PLACES.index(place)
        for part, left, right, sign in ((0, 0, 0, 1), (0, 1, 1, -1), (1, 0, 1, 1), (1, 1, 0, 1)):
            at = 16 + right if second is None else right * 8 + second
            mix[kind * ROWS + part * 13 + d, (first * 2 + left) * 24 + at] += sign * weight

    def corner(e, f):
        return 9 + (min(e, f) % 2) * 2 + (max(e, f) % 2)

    add(1.0, 0, None, (0, 0), 0)
    for e in range(4):
        add(once, 0, e, STEP[e], 0)
        add(once, 0, 4 + e, (0, 0), 1 + e)
        for f in range(4):
            both = (STEP[e][0] + STEP[f][0], STEP[e][1] + STEP[f][1])
            crossed = e // 2 != f // 2
            add(twice, 1 + e, f, both, 0)
            if f == e ^ 1:
                add(-twice, 1 + e, f, both, 1 + e)
            if f != e:
                add(twice, 5 + e, f, STEP[f], 1 + e)
            if f == e:
                add(twice, 1 + e, 4 + f, STEP[e], 5 + e)
                add(twice, 5 + e, 4 + f, (0, 0), 1 + e)
            elif crossed:
                add(twice, 1 + e, 4 + f, STEP[e], 1 + f)
                add(twice, 5 + e, 4 + f, (0, 0), corner(e, f))
    return mix


def halves(value):
    high = value.astype(jnp.bfloat16)
    return high, (value - high.astype(jnp.float32)).astype(jnp.bfloat16)


def thirds(value):
    high, low = halves(value)
    return high, low, (value - high.astype(jnp.float32) - low.astype(jnp.float32)).astype(jnp.bfloat16)


def cosine(turns, length):
    centred = jnp.where(turns >= length // 2, length - turns, turns)
    angle = (length // 4 - centred).astype(jnp.float32) * (2.0 * math.pi / length)
    square = angle * angle
    value = 1.0 / 6227020800.0
    value = value * square - 1.0 / 39916800.0
    value = value * square + 1.0 / 362880.0
    value = value * square - 1.0 / 5040.0
    value = value * square + 1.0 / 120.0
    value = value * square - 1.0 / 6.0
    return angle + angle * square * value


def dot(left, right, dims=((1,), (0,))):
    return lax.dot_general(left, right, (dims, ((), ())), preferred_element_type=jnp.float32)


def dot3(left, right, dims=((1,), (0,))):
    high, low = left
    high_right, low_right = right
    both = dot(jnp.concatenate([high, low], axis=0), high_right, dims)
    size = high.shape[0]
    return both[:size] + (both[size:] + dot(high, low_right, dims))


def fetch(sems, *pairs):
    copies = [pltpu.make_async_copy(src, dst, sems.at[i]) for i, (src, dst) in enumerate(pairs)]
    for copy in copies:
        copy.start()
    return copies


def make_turns(place, rows, cols, row_high_ref, row_low_ref, col_high_ref, col_low_ref):
    row_at, col_at = place()
    span = OVER * rows
    r = lax.broadcasted_iota(jnp.int32, (rows, LANES), 0)
    k = lax.broadcasted_iota(jnp.int32, (rows, LANES), 1)
    samples = OVER * BLOCK
    turns = (r * (row_at * samples + k)) & (span - 1)
    cos = jnp.where(k < samples, cosine(turns, span), 0.0)
    sin = jnp.where(k < samples, cosine((turns - span // 4) & (span - 1), span), 0.0)
    pick = (k >= samples) & (k < samples + BLOCK) & (r == row_at * BLOCK + k - samples)
    pick = jnp.where(pick, 1.0, 0.0)
    turn = jnp.concatenate(
        [
            jnp.concatenate([cos + pick, -sin], axis=1),
            jnp.concatenate([sin, cos + pick], axis=1),
        ],
        axis=0,
    )
    row_high_ref[...], row_low_ref[...] = halves(turn)

    span = OVER * cols
    blocks = cols // BLOCK
    shape = (samples, blocks * PIECE)
    q = lax.broadcasted_iota(jnp.int32, shape, 0) + col_at * samples
    k = lax.broadcasted_iota(jnp.int32, shape, 1)
    block = jnp.full(shape, COL_ORDER[0], jnp.int32)
    at = k
    for b in range(1, blocks):
        block = block + jnp.where(k >= b * PIECE, COL_ORDER[b] - COL_ORDER[b - 1], 0)
        at = at - jnp.where(k >= b * PIECE, PIECE, 0)
    imaginary = at >= WIDE
    c = block * BLOCK + at - jnp.where(imaginary, WIDE, 0) - REACH
    inside = (at < 2 * WIDE) & (c >= 0) & (c < cols)
    turns = (q * c) & (span - 1)
    scale = (rows * cols) ** -0.5
    cos = jnp.where(inside, cosine(turns, span) * scale, 0.0)
    sin = jnp.where(inside, cosine((turns - span // 4) & (span - 1), span) * scale, 0.0)
    turn = jnp.concatenate([jnp.where(imaginary, sin, cos), jnp.where(imaginary, cos, -sin)], axis=0)
    col_high_ref[...], col_low_ref[...] = halves(turn)


def make_table(feed_hbm, map_hbm, probe_hbm, mix_hbm, table_ref, feed_ref, map_ref, probe_ref, mix_ref, hops_ref, sems):
    edge = feed_ref.shape[2] // 4
    chunks = [(map_hbm.at[:, pl.ds(a * edge, edge)], map_ref.at[:, pl.ds(a * edge, edge)]) for a in range(4)]
    copies = fetch(sems, (feed_hbm, feed_ref), (probe_hbm, probe_ref), *chunks, (mix_hbm, mix_ref))
    copies[0].wait()
    copies[1].wait()
    units = 4 * edge

    def block(value, e):
        return value[:, e * edge : (e + 1) * edge]

    feed_re, feed_im = feed_ref[0], feed_ref[1]
    back_re = reflect_re * feed_re - reflect_im * feed_im
    back_im = reflect_re * feed_im + reflect_im * feed_re
    hops_ref[0:8, :] = feed_re
    hops_ref[8:16, :] = feed_im
    for a in range(4):
        e = a ^ 1
        enter = jnp.concatenate(
            [block(feed_re, e), block(feed_im, e), block(back_re, a), block(back_im, a)], axis=0
        )
        enter = jnp.concatenate(halves(enter), axis=0)
        copies[2 + a].wait()
        by_re = dot(enter, map_ref[0, a * edge : (a + 1) * edge, :])
        by_im = dot(enter, map_ref[1, a * edge : (a + 1) * edge, :])
        by_re = by_re[0:32] + by_re[32:64]
        by_im = by_im[0:32] + by_im[32:64]
        for first, at in ((1 + e, 0), (5 + a, 16)):
            hops_ref[first * 16 : first * 16 + 8, :] = by_re[at : at + 8] - by_im[at + 8 : at + 16]
            hops_ref[first * 16 + 8 : first * 16 + 16, :] = (
                by_re[at + 8 : at + 16] + by_im[at : at + 8]
            )
    probe_re, probe_im = probe_ref[0:1, :], probe_ref[1:2, :]
    probes = jnp.concatenate(halves(jnp.concatenate([probe_re, probe_im] + [probe_re] * 6, axis=0)), axis=0)
    through_re = dot(probes, map_ref[0], ((1,), (1,)))
    through_im = dot(probes, map_ref[1], ((1,), (1,)))
    through_re = through_re[0:8] + through_re[8:16]
    through_im = through_im[0:8] + through_im[8:16]
    total_re = probe_re + through_re[0:1] - through_im[1:2]
    total_im = probe_im + through_im[0:1] + through_re[1:2]

    def swapped(value):
        return jnp.concatenate([block(value, e ^ 1) for e in range(4)], axis=1)

    sub = lax.broadcasted_iota(jnp.int32, (8, units), 0)
    lane = lax.broadcasted_iota(jnp.int32, (8, units), 1)
    own = lane // edge == sub % 4
    passed = sub < 4
    out_re = jnp.where(passed, swapped(total_re), reflect_re * total_re - reflect_im * total_im)
    out_im = jnp.where(passed, swapped(total_im), reflect_re * total_im + reflect_im * total_re)
    leave = jnp.concatenate(
        [
            jnp.where(own, out_re, 0.0),
            jnp.where(own, out_im, 0.0),
            jnp.where(sub == 0, probe_re, jnp.where(sub == 1, probe_im, 0.0)),
        ],
        axis=0,
    )
    products = dot3(halves(leave), halves(hops_ref[...]), ((1,), (1,)))
    copies[6].wait()
    flat = jnp.concatenate([products[:, 8 * k : 8 * k + 8] for k in range(18)], axis=0)
    table = dot(mix_ref[...], jnp.concatenate(thirds(flat), axis=1))
    table = table[:, 0:8] + table[:, 8:16] + table[:, 16:24]
    wide = [table[k * ROWS : (k + 1) * ROWS, :] for k in range(CLASSES)]
    wide.append(jnp.zeros((ROWS, LANES - 8 * CLASSES), jnp.float32))
    table_ref[...] = jnp.concatenate(wide, axis=1)


def maker(row_at):
    makes, share = row_at < 0, row_at * 0
    for k, member in enumerate(MAKERS):
        makes = makes | (row_at == member)
        share = jnp.where(row_at == member, k, share)
    return makes, share


def pack_kernel(
    place, rows, cols, drive_hbm, flag_hbm, port_hbm, feed_hbm, map_hbm, probe_hbm, mix_hbm,
    out_ref, row_high_ref, row_low_ref, col_high_ref, col_low_ref,
    drive_ref, flag_ref, port_ref, feed_ref, map_ref, probe_ref, mix_ref, hops_ref, table_ref, piece_ref, sems, table_sems,
):
    makes, share = maker(place()[0])
    copies = fetch(sems, (drive_hbm, drive_ref), (flag_hbm, flag_ref), (port_hbm, port_ref))
    make_turns(place, rows, cols, row_high_ref, row_low_ref, col_high_ref, col_low_ref)
    for copy in copies:
        copy.wait()
    active = flag_ref[...].astype(jnp.float32)
    pieces = [drive_ref[x, s] * active for x in range(2) for s in range(STATES)]
    pieces.append(port_ref[...].astype(jnp.float32))
    pieces.append(jnp.zeros((BLOCK, LANES - USED), jnp.float32))
    piece_ref[...] = jnp.concatenate(pieces, axis=1)

    @pl.when(makes)
    def _():
        make_table(
            feed_hbm, map_hbm, probe_hbm, mix_hbm, table_ref,
            feed_ref, map_ref, probe_ref, mix_ref, hops_ref, table_sems,
        )
        part = table_ref[pl.ds(pl.multiple_of(share // 2 * 8, 8), 8), :]
        part = jnp.where(share % 2 == 0, pltpu.roll(part, USED, axis=1), pltpu.roll(part, USED - SHARE, axis=1))
        lane = lax.broadcasted_iota(jnp.int32, (BLOCK, LANES), 1)
        piece_ref[...] += jnp.where((lane >= USED) & (lane < USED + SHARE), part, 0.0)

    out_ref[...] = jnp.broadcast_to(piece_ref[...][None], out_ref.shape)


def stencil_kernel(place, rows, cols, cells_ref, row_high_ref, row_low_ref, out_ref, own_ref, coef_ref):
    _, col_at = place()
    slots = [ROW_ORDER.index(k) * BLOCK for k in range(rows // BLOCK)]
    across = jnp.concatenate([cells_ref[k : k + BLOCK, :] for k in slots], axis=0).T
    amps = [[across[(x * 4 + s) * 8 : (x * 4 + s) * 8 + 8] for s in range(STATES)] for x in range(2)]
    ports = across[64:72]

    sub = lax.broadcasted_iota(jnp.int32, (8, rows), 0).astype(jnp.float32)
    r = lax.broadcasted_iota(jnp.int32, (8, rows), 1)

    def flag(mask):
        return jnp.where(mask, 1.0, 0.0)

    none = jnp.zeros((8, rows), jnp.float32)
    north, south, north2, south2 = flag(r == 0), flag(r == rows - 1), flag(r == 1), flag(r == rows - 2)
    lane = lax.broadcasted_iota(jnp.int32, (BLOCK, LANES), 1)
    makers = [slots[k] for k in MAKERS]
    parts = [cells_ref[k : k + BLOCK, :] for k in makers]
    firsts = [jnp.where(lane < SHARE, pltpu.roll(part, LANES - USED, axis=1), 0.0) for part in parts[0::2]]
    seconds = [
        jnp.where((lane >= SHARE) & (lane < 2 * SHARE), pltpu.roll(part, LANES - USED + SHARE, axis=1), 0.0)
        for part in parts[1::2]
    ]
    table = jnp.concatenate(halves(jnp.concatenate([a + b for a, b in zip(firsts, seconds)], axis=0)), axis=0)
    for j in range(BLOCK):
        c = col_at * BLOCK + j
        chosen = flag(jnp.broadcast_to(ports[j : j + 1], (8, rows)) == sub)
        at_north, at_south = chosen * north, chosen * south
        kinds = [chosen, at_north, at_south, none, none, chosen * north2, chosen * south2] + [none] * 6
        if j in (0, BLOCK - 1):
            edge, first, second = (flag(c == 0), 9, 11) if j == 0 else (flag(c == cols - 1), 10, 12)
            kinds[3 if j == 0 else 4] = chosen * edge
            kinds[first], kinds[second] = at_north * edge, at_south * edge
        if j in (1, BLOCK - 2):
            kinds[7 if j == 1 else 8] = chosen * (flag(c == 1) if j == 1 else flag(c == cols - 2))
        kinds.append(jnp.zeros((LANES - 8 * CLASSES, rows), jnp.float32))
        found = dot(table, jnp.concatenate(kinds, axis=0).astype(jnp.bfloat16))
        found = found[0:ROWS] + found[ROWS : 2 * ROWS]
        for half in range(rows // LANES):
            coef_ref[half, j * ROWS : (j + 1) * ROWS, :] = found[:, half * LANES : (half + 1) * LANES]

    def coef(index):
        return jnp.concatenate(
            [coef_ref[half, pl.ds(index, 8, stride=ROWS), :] for half in range(rows // LANES)], axis=1
        )

    def moved(value, dr):
        if dr == 0:
            return value
        value = pltpu.roll(value, dr % rows, axis=1)
        return jnp.where(r >= dr if dr > 0 else r < rows + dr, value, 0.0)

    sums = {}
    for d, (dr, dc) in enumerate(PLACES):
        k_re, k_im = coef(d), coef(13 + d)
        for s in range(STATES):
            a_re, a_im = amps[0][s], amps[1][s]
            for x, value in ((0, k_re * a_re - k_im * a_im), (1, k_re * a_im + k_im * a_re)):
                value = moved(value, dr)
                key = (dc, s, x)
                sums[key] = sums[key] + value if key in sums else value

    spread = jnp.concatenate(
        [
            jnp.concatenate([sums[dc, s, 0], sums[dc, s, 1]], axis=1)
            for dc in range(-2, 3)
            for s in range(STATES)
        ],
        axis=0,
    )
    turned = dot3(halves(spread), (row_high_ref[...], row_low_ref[...]))
    samples = OVER * BLOCK
    lane = lax.broadcasted_iota(jnp.int32, (8, LANES), 1)
    first, second = lane < samples, (lane >= samples) & (lane < samples + BLOCK)
    nothing = jnp.zeros((16, LANES), jnp.float32)
    mains, nears = [], []
    for x in range(2):
        main, near = nothing, nothing
        for i, dc in enumerate(range(-2, 3)):
            wave, own = jnp.zeros((8, LANES), jnp.float32), jnp.zeros((8, LANES), jnp.float32)
            for s in range(STATES):
                part = turned[(i * STATES + s) * 8 : (i * STATES + s) * 8 + 8, x * LANES : (x + 1) * LANES]
                a, b = jnp.where(first, part, 0.0), jnp.where(second, part, 0.0)
                wave = wave + (pltpu.roll(a, s * samples, axis=1) if s else a)
                own = own + pltpu.roll(b, (s - 1) * samples % LANES, axis=1) if s != 1 else own + b
            for_main = jnp.concatenate([wave, jnp.zeros((8, LANES), jnp.float32)], axis=0)
            for_near = jnp.concatenate([own, jnp.zeros((8, LANES), jnp.float32)], axis=0)
            shift = REACH + dc
            main = main + (pltpu.roll(for_main, shift, axis=0) if shift else for_main)
            near = near + (pltpu.roll(for_near, shift, axis=0) if shift else for_near)
        mains.append(main[0:WIDE])
        nears.append(
            near[0:1] + pltpu.roll(near, BLOCK, axis=1)[1:2]
            + pltpu.roll(near, 2 * BLOCK, axis=1)[10:11] + pltpu.roll(near, 3 * BLOCK, axis=1)[11:12]
        )
        own_ref[:, x * LANES : (x + 1) * LANES] = near
    piece = jnp.concatenate(mains + nears, axis=0)
    four = jnp.concatenate([piece] * 4, axis=0)
    for i in range(out_ref.shape[0] // (4 * PIECE)):
        out_ref[i * 4 * PIECE : (i + 1) * 4 * PIECE, :] = four


def pattern_kernel(place, blocks, got_ref, own_ref, col_high_ref, col_low_ref, currents_ref, far_ref):
    _, col_at = place()
    samples = OVER * BLOCK
    far = dot3((col_high_ref[...], col_low_ref[...]), halves(got_ref[...]))
    left, right = 0, 0
    for b in range(blocks):
        left = jnp.where(col_at == b + 1, COL_ORDER.index(b), left)
        right = jnp.where(col_at == b - 1, COL_ORDER.index(b), right)
    has_left, has_right = jnp.where(col_at > 0, 1.0, 0.0), jnp.where(col_at < blocks - 1, 1.0, 0.0)
    own = own_ref[...]
    stacked = [far]
    for x in range(2):
        from_left = has_left * got_ref[pl.ds(left * PIECE + 2 * WIDE + x, 1), :]
        from_right = has_right * got_ref[pl.ds(right * PIECE + 2 * WIDE + x, 1), :]
        mine = own[:, x * LANES : (x + 1) * LANES]
        stacked += [
            mine[2:3] + pltpu.roll(from_left, LANES - 2 * BLOCK, axis=1),
            mine[3:4] + pltpu.roll(from_left, LANES - 3 * BLOCK, axis=1),
            mine[4:8],
            mine[8:9] + from_right,
            mine[9:10] + pltpu.roll(from_right, LANES - BLOCK, axis=1),
        ]
    stacked.append(jnp.zeros((LANES - 2 * samples - 2 * BLOCK, LANES), jnp.float32))
    flat = jnp.concatenate(stacked, axis=0).T
    for x in range(2):
        at = 2 * samples + x * BLOCK
        for s in range(STATES):
            far_ref[x, s] = flat[s * samples : (s + 1) * samples, x * samples : (x + 1) * samples]
            currents_ref[x, s] = flat[s * samples : s * samples + BLOCK, at : at + BLOCK]


def spot():
    return lax.axis_index("row"), lax.axis_index("col")


HBM = pl.BlockSpec(memory_space=pltpu.HBM)


def call(kernel, out_shape, scratch=(), flops=0, size=0, grant=40960, **options):
    return pl.pallas_call(
        kernel,
        out_shape=out_shape,
        scratch_shapes=list(scratch),
        compiler_params=pltpu.CompilerParams(vmem_limit_bytes=grant * 1024),
        cost_estimate=pl.CostEstimate(flops=flops, bytes_accessed=size, transcendentals=0),
        **options,
    )


def exchange(pieces, axis, order):
    return lax.all_to_all(pieces, axis, 0, 0, axis_index_groups=[list(order)])


def body(row_blocks, col_blocks, place, active_flags, port_index, drive_weights, feed_table, cell_map, probe_weights):
    rows, cols = row_blocks * BLOCK, col_blocks * BLOCK
    samples = OVER * BLOCK
    f32, b16 = jnp.float32, jnp.bfloat16
    shape = jax.ShapeDtypeStruct
    taken = (
        drive_weights, active_flags, port_index,
        feed_table, cell_map, probe_weights, jnp.asarray(path_matrix(), b16),
    )
    packed, row_high, row_low, col_high, col_low = call(
        functools.partial(pack_kernel, place, rows, cols),
        (
            pltpu.VMEM((row_blocks, BLOCK, LANES), f32),
            pltpu.VMEM((2 * rows, 2 * LANES), b16),
            pltpu.VMEM((2 * rows, 2 * LANES), b16),
            pltpu.VMEM((2 * samples, col_blocks * PIECE), b16),
            pltpu.VMEM((2 * samples, col_blocks * PIECE), b16),
        ),
        scratch=[pltpu.VMEM(x.shape, x.dtype) for x in taken]
        + [
            pltpu.VMEM((144, cell_map.shape[1]), f32),
            pltpu.VMEM((ROWS, LANES), f32),
            pltpu.VMEM((BLOCK, LANES), f32),
            pltpu.SemaphoreType.DMA((3,)),
            pltpu.SemaphoreType.DMA((7,)),
        ],
        in_specs=[HBM] * 7,
        name="pack",
        grant=57344,
    )(*taken)
    cells = exchange(packed, "row", ROW_ORDER).reshape(rows, LANES)
    pieces, own = call(
        functools.partial(stencil_kernel, place, rows, cols),
        (shape((col_blocks * PIECE, LANES), f32), shape((16, 2 * LANES), f32)),
        scratch=[pltpu.VMEM((rows // LANES, BLOCK * ROWS, LANES), f32)],
        name="stencil",
    )(cells, row_high, row_low)
    got = exchange(pieces.reshape(col_blocks, PIECE // 2, 2, LANES), "col", COL_ORDER)
    return call(
        functools.partial(pattern_kernel, place, col_blocks),
        (shape((2, STATES, BLOCK, BLOCK), f32), shape((2, STATES, samples, samples), f32)),
        name="pattern",
    )(got.reshape(col_blocks * PIECE, LANES), own, col_high, col_low)


def solution(mesh):
    placed = (P("row", "col"), P("row", "col"), P(None, None, "row", "col"), P(), P(), P())
    return jax.shard_map(
        functools.partial(body, mesh.shape["row"], mesh.shape["col"], spot),
        mesh=mesh,
        in_specs=placed,
        out_specs=(P(None, None, "row", "col"), P(None, None, "row", "col")),
        check_vma=False,
    )
```

```python
import functools
import math

import jax
import jax.numpy as jnp
import numpy as np
from jax import lax
from jax.experimental import pallas as pl
from jax.experimental.pallas import tpu as pltpu
from jax.sharding import PartitionSpec as P

OVER = 4
PORTS = 8
STATES = 4
BLOCK = 8
REACH = 2
WIDE = 12
LANES = 128
ROW_ORDER = tuple((15 + k) % 32 for k in range(32))
COL_ORDER = tuple((14 + k) % 16 for k in range(16))
PIECE = 26
USED = 72

relaxation = 0.75
reflect_re = -0.3
reflect_im = 0.2

STEP = ((-1, 0), (1, 0), (0, -1), (0, 1))
PLACES = tuple(
    (dr, dc) for dr in range(-2, 3) for dc in range(-2, 3) if abs(dr) + abs(dc) <= 2
)
CLASSES = 13
SHARE = 52
ROWS = 32


def path_matrix():
    twice = relaxation * relaxation
    once = relaxation * (1.0 - relaxation) + relaxation
    mix = np.zeros((CLASSES * ROWS, 18 * 24), np.float32)

    def add(weight, first, second, place, kind):
        d = PLACES.index(place)
        for part, left, right, sign in ((0, 0, 0, 1), (0, 1, 1, -1), (1, 0, 1, 1), (1, 1, 0, 1)):
            at = 16 + right if second is None else right * 8 + second
            mix[kind * ROWS + part * 13 + d, (first * 2 + left) * 24 + at] += sign * weight

    def corner(e, f):
        return 9 + (min(e, f) % 2) * 2 + (max(e, f) % 2)

    add(1.0, 0, None, (0, 0), 0)
    for e in range(4):
        add(once, 0, e, STEP[e], 0)
        add(once, 0, 4 + e, (0, 0), 1 + e)
        for f in range(4):
            both = (STEP[e][0] + STEP[f][0], STEP[e][1] + STEP[f][1])
            crossed = e // 2 != f // 2
            add(twice, 1 + e, f, both, 0)
            if f == e ^ 1:
                add(-twice, 1 + e, f, both, 1 + e)
            if f != e:
                add(twice, 5 + e, f, STEP[f], 1 + e)
            if f == e:
                add(twice, 1 + e, 4 + f, STEP[e], 5 + e)
                add(twice, 5 + e, 4 + f, (0, 0), 1 + e)
            elif crossed:
                add(twice, 1 + e, 4 + f, STEP[e], 1 + f)
                add(twice, 5 + e, 4 + f, (0, 0), corner(e, f))
    return mix


def halves(value):
    high = value.astype(jnp.bfloat16)
    return high, (value - high.astype(jnp.float32)).astype(jnp.bfloat16)


def thirds(value):
    high, low = halves(value)
    return high, low, (value - high.astype(jnp.float32) - low.astype(jnp.float32)).astype(jnp.bfloat16)


def cosine(turns, length):
    centred = jnp.where(turns >= length // 2, length - turns, turns)
    angle = (length // 4 - centred).astype(jnp.float32) * (2.0 * math.pi / length)
    square = angle * angle
    value = 1.0 / 6227020800.0
    value = value * square - 1.0 / 39916800.0
    value = value * square + 1.0 / 362880.0
    value = value * square - 1.0 / 5040.0
    value = value * square + 1.0 / 120.0
    value = value * square - 1.0 / 6.0
    return angle + angle * square * value


def dot(left, right, dims=((1,), (0,))):
    return lax.dot_general(left, right, (dims, ((), ())), preferred_element_type=jnp.float32)


def dot3(left, right, dims=((1,), (0,))):
    high, low = left
    high_right, low_right = right
    both = dot(jnp.concatenate([high, low], axis=0), high_right, dims)
    size = high.shape[0]
    return both[:size] + (both[size:] + dot(high, low_right, dims))


def fetch(sems, *pairs):
    copies = [pltpu.make_async_copy(src, dst, sems.at[i]) for i, (src, dst) in enumerate(pairs)]
    for copy in copies:
        copy.start()
    return copies


def make_turns(place, rows, cols, row_high_ref, row_low_ref, col_high_ref, col_low_ref):
    row_at, col_at = place()
    span = OVER * rows
    r = lax.broadcasted_iota(jnp.int32, (rows, LANES), 0)
    k = lax.broadcasted_iota(jnp.int32, (rows, LANES), 1)
    samples = OVER * BLOCK
    turns = (r * (row_at * samples + k)) & (span - 1)
    cos = jnp.where(k < samples, cosine(turns, span), 0.0)
    sin = jnp.where(k < samples, cosine((turns - span // 4) & (span - 1), span), 0.0)
    pick = (k >= samples) & (k < samples + BLOCK) & (r == row_at * BLOCK + k - samples)
    pick = jnp.where(pick, 1.0, 0.0)
    turn = jnp.concatenate(
        [
            jnp.concatenate([cos + pick, -sin], axis=1),
            jnp.concatenate([sin, cos + pick], axis=1),
        ],
        axis=0,
    )
    row_high_ref[...], row_low_ref[...] = halves(turn)

    span = OVER * cols
    blocks = cols // BLOCK
    shape = (samples, blocks * PIECE)
    q = lax.broadcasted_iota(jnp.int32, shape, 0) + col_at * samples
    k = lax.broadcasted_iota(jnp.int32, shape, 1)
    block = jnp.full(shape, COL_ORDER[0], jnp.int32)
    at = k
    for b in range(1, blocks):
        block = block + jnp.where(k >= b * PIECE, COL_ORDER[b] - COL_ORDER[b - 1], 0)
        at = at - jnp.where(k >= b * PIECE, PIECE, 0)
    imaginary = at >= WIDE
    c = block * BLOCK + at - jnp.where(imaginary, WIDE, 0) - REACH
    inside = (at < 2 * WIDE) & (c >= 0) & (c < cols)
    turns = (q * c) & (span - 1)
    scale = (rows * cols) ** -0.5
    cos = jnp.where(inside, cosine(turns, span) * scale, 0.0)
    sin = jnp.where(inside, cosine((turns - span // 4) & (span - 1), span) * scale, 0.0)
    turn = jnp.concatenate([jnp.where(imaginary, sin, cos), jnp.where(imaginary, cos, -sin)], axis=0)
    col_high_ref[...], col_low_ref[...] = halves(turn)


def make_table(feed_hbm, map_hbm, probe_hbm, mix_hbm, table_ref, feed_ref, map_ref, probe_ref, mix_ref, hops_ref, sems):
    edge = feed_ref.shape[2] // 4
    chunks = [(map_hbm.at[:, pl.ds(a * edge, edge)], map_ref.at[:, pl.ds(a * edge, edge)]) for a in range(4)]
    copies = fetch(sems, (feed_hbm, feed_ref), (probe_hbm, probe_ref), *chunks, (mix_hbm, mix_ref))
    copies[0].wait()
    copies[1].wait()
    units = 4 * edge

    def block(value, e):
        return value[:, e * edge : (e + 1) * edge]

    feed_re, feed_im = feed_ref[0], feed_ref[1]
    back_re = reflect_re * feed_re - reflect_im * feed_im
    back_im = reflect_re * feed_im + reflect_im * feed_re
    hops_ref[0:8, :] = feed_re
    hops_ref[8:16, :] = feed_im
    for a in range(4):
        e = a ^ 1
        enter = jnp.concatenate(
            [block(feed_re, e), block(feed_im, e), block(back_re, a), block(back_im, a)], axis=0
        )
        enter = jnp.concatenate(halves(enter), axis=0)
        copies[2 + a].wait()
        by_re = dot(enter, map_ref[0, a * edge : (a + 1) * edge, :])
        by_im = dot(enter, map_ref[1, a * edge : (a + 1) * edge, :])
        by_re = by_re[0:32] + by_re[32:64]
        by_im = by_im[0:32] + by_im[32:64]
        for first, at in ((1 + e, 0), (5 + a, 16)):
            hops_ref[first * 16 : first * 16 + 8, :] = by_re[at : at + 8] - by_im[at + 8 : at + 16]
            hops_ref[first * 16 + 8 : first * 16 + 16, :] = (
                by_re[at + 8 : at + 16] + by_im[at : at + 8]
            )
    probe_re, probe_im = probe_ref[0:1, :], probe_ref[1:2, :]
    probes = jnp.concatenate(halves(jnp.concatenate([probe_re, probe_im] + [probe_re] * 6, axis=0)), axis=0)
    through_re = dot(probes, map_ref[0], ((1,), (1,)))
    through_im = dot(probes, map_ref[1], ((1,), (1,)))
    through_re = through_re[0:8] + through_re[8:16]
    through_im = through_im[0:8] + through_im[8:16]
    total_re = probe_re + through_re[0:1] - through_im[1:2]
    total_im = probe_im + through_im[0:1] + through_re[1:2]

    def swapped(value):
        return jnp.concatenate([block(value, e ^ 1) for e in range(4)], axis=1)

    sub = lax.broadcasted_iota(jnp.int32, (8, units), 0)
    lane = lax.broadcasted_iota(jnp.int32, (8, units), 1)
    own = lane // edge == sub % 4
    passed = sub < 4
    out_re = jnp.where(passed, swapped(total_re), reflect_re * total_re - reflect_im * total_im)
    out_im = jnp.where(passed, swapped(total_im), reflect_re * total_im + reflect_im * total_re)
    leave = jnp.concatenate(
        [
            jnp.where(own, out_re, 0.0),
            jnp.where(own, out_im, 0.0),
            jnp.where(sub == 0, probe_re, jnp.where(sub == 1, probe_im, 0.0)),
        ],
        axis=0,
    )
    products = dot3(halves(leave), halves(hops_ref[...]), ((1,), (1,)))
    copies[6].wait()
    flat = jnp.concatenate([products[:, 8 * k : 8 * k + 8] for k in range(18)], axis=0)
    table = dot(mix_ref[...], jnp.concatenate(thirds(flat), axis=1))
    table = table[:, 0:8] + table[:, 8:16] + table[:, 16:24]
    wide = [table[k * ROWS : (k + 1) * ROWS, :] for k in range(CLASSES)]
    wide.append(jnp.zeros((ROWS, LANES - 8 * CLASSES), jnp.float32))
    table_ref[...] = jnp.concatenate(wide, axis=1)


def maker(row_at):
    return row_at % 16 < 4, row_at % 4 + 4 * (row_at // 16)


def pack_kernel(
    place, rows, cols, drive_hbm, flag_hbm, port_hbm, feed_hbm, map_hbm, probe_hbm, mix_hbm,
    out_ref, row_high_ref, row_low_ref, col_high_ref, col_low_ref,
    drive_ref, flag_ref, port_ref, feed_ref, map_ref, probe_ref, mix_ref, hops_ref, table_ref, piece_ref, sems, table_sems,
):
    makes, share = maker(place()[0])
    copies = fetch(sems, (drive_hbm, drive_ref), (flag_hbm, flag_ref), (port_hbm, port_ref))
    make_turns(place, rows, cols, row_high_ref, row_low_ref, col_high_ref, col_low_ref)
    for copy in copies:
        copy.wait()
    active = flag_ref[...].astype(jnp.float32)
    pieces = [drive_ref[x, s] * active for x in range(2) for s in range(STATES)]
    pieces.append(port_ref[...].astype(jnp.float32))
    pieces.append(jnp.zeros((BLOCK, LANES - USED), jnp.float32))
    piece_ref[...] = jnp.concatenate(pieces, axis=1)

    @pl.when(makes)
    def _():
        make_table(
            feed_hbm, map_hbm, probe_hbm, mix_hbm, table_ref,
            feed_ref, map_ref, probe_ref, mix_ref, hops_ref, table_sems,
        )
        part = table_ref[pl.ds(pl.multiple_of(share // 2 * 8, 8), 8), :]
        part = jnp.where(share % 2 == 0, pltpu.roll(part, USED, axis=1), pltpu.roll(part, USED - SHARE, axis=1))
        lane = lax.broadcasted_iota(jnp.int32, (BLOCK, LANES), 1)
        piece_ref[...] += jnp.where((lane >= USED) & (lane < USED + SHARE), part, 0.0)

    out_ref[...] = jnp.broadcast_to(piece_ref[...][None], out_ref.shape)


def stencil_kernel(place, rows, cols, cells_ref, row_high_ref, row_low_ref, out_ref, own_ref, coef_ref):
    _, col_at = place()
    slots = [ROW_ORDER.index(k) * BLOCK for k in range(rows // BLOCK)]
    across = jnp.concatenate([cells_ref[k : k + BLOCK, :] for k in slots], axis=0).T
    amps = [[across[(x * 4 + s) * 8 : (x * 4 + s) * 8 + 8] for s in range(STATES)] for x in range(2)]
    ports = across[64:72]

    sub = lax.broadcasted_iota(jnp.int32, (8, rows), 0).astype(jnp.float32)
    r = lax.broadcasted_iota(jnp.int32, (8, rows), 1)

    def flag(mask):
        return jnp.where(mask, 1.0, 0.0)

    none = jnp.zeros((8, rows), jnp.float32)
    north, south, north2, south2 = flag(r == 0), flag(r == rows - 1), flag(r == 1), flag(r == rows - 2)
    lane = lax.broadcasted_iota(jnp.int32, (BLOCK, LANES), 1)
    makers = [slots[k % 4 + 16 * (k // 4)] for k in range(8)]
    parts = [cells_ref[k : k + BLOCK, :] for k in makers]
    firsts = [jnp.where(lane < SHARE, pltpu.roll(part, LANES - USED, axis=1), 0.0) for part in parts[0::2]]
    seconds = [
        jnp.where((lane >= SHARE) & (lane < 2 * SHARE), pltpu.roll(part, LANES - USED + SHARE, axis=1), 0.0)
        for part in parts[1::2]
    ]
    table = jnp.concatenate(halves(jnp.concatenate([a + b for a, b in zip(firsts, seconds)], axis=0)), axis=0)
    for j in range(BLOCK):
        c = col_at * BLOCK + j
        chosen = flag(jnp.broadcast_to(ports[j : j + 1], (8, rows)) == sub)
        at_north, at_south = chosen * north, chosen * south
        kinds = [chosen, at_north, at_south, none, none, chosen * north2, chosen * south2] + [none] * 6
        if j in (0, BLOCK - 1):
            edge, first, second = (flag(c == 0), 9, 11) if j == 0 else (flag(c == cols - 1), 10, 12)
            kinds[3 if j == 0 else 4] = chosen * edge
            kinds[first], kinds[second] = at_north * edge, at_south * edge
        if j in (1, BLOCK - 2):
            kinds[7 if j == 1 else 8] = chosen * (flag(c == 1) if j == 1 else flag(c == cols - 2))
        kinds.append(jnp.zeros((LANES - 8 * CLASSES, rows), jnp.float32))
        found = dot(table, jnp.concatenate(kinds, axis=0).astype(jnp.bfloat16))
        found = found[0:ROWS] + found[ROWS : 2 * ROWS]
        for half in range(rows // LANES):
            coef_ref[half, j * ROWS : (j + 1) * ROWS, :] = found[:, half * LANES : (half + 1) * LANES]

    def coef(index):
        return jnp.concatenate(
            [coef_ref[half, pl.ds(index, 8, stride=ROWS), :] for half in range(rows // LANES)], axis=1
        )

    def moved(value, dr):
        if dr == 0:
            return value
        value = pltpu.roll(value, dr % rows, axis=1)
        return jnp.where(r >= dr if dr > 0 else r < rows + dr, value, 0.0)

    sums = {}
    for d, (dr, dc) in enumerate(PLACES):
        k_re, k_im = coef(d), coef(13 + d)
        for s in range(STATES):
            a_re, a_im = amps[0][s], amps[1][s]
            for x, value in ((0, k_re * a_re - k_im * a_im), (1, k_re * a_im + k_im * a_re)):
                value = moved(value, dr)
                key = (dc, s, x)
                sums[key] = sums[key] + value if key in sums else value

    spread = jnp.concatenate(
        [
            jnp.concatenate([sums[dc, s, 0], sums[dc, s, 1]], axis=1)
            for dc in range(-2, 3)
            for s in range(STATES)
        ],
        axis=0,
    )
    turned = dot3(halves(spread), (row_high_ref[...], row_low_ref[...]))
    samples = OVER * BLOCK
    lane = lax.broadcasted_iota(jnp.int32, (8, LANES), 1)
    first, second = lane < samples, (lane >= samples) & (lane < samples + BLOCK)
    nothing = jnp.zeros((16, LANES), jnp.float32)
    mains, nears = [], []
    for x in range(2):
        main, near = nothing, nothing
        for i, dc in enumerate(range(-2, 3)):
            wave, own = jnp.zeros((8, LANES), jnp.float32), jnp.zeros((8, LANES), jnp.float32)
            for s in range(STATES):
                part = turned[(i * STATES + s) * 8 : (i * STATES + s) * 8 + 8, x * LANES : (x + 1) * LANES]
                a, b = jnp.where(first, part, 0.0), jnp.where(second, part, 0.0)
                wave = wave + (pltpu.roll(a, s * samples, axis=1) if s else a)
                own = own + pltpu.roll(b, (s - 1) * samples % LANES, axis=1) if s != 1 else own + b
            for_main = jnp.concatenate([wave, jnp.zeros((8, LANES), jnp.float32)], axis=0)
            for_near = jnp.concatenate([own, jnp.zeros((8, LANES), jnp.float32)], axis=0)
            shift = REACH + dc
            main = main + (pltpu.roll(for_main, shift, axis=0) if shift else for_main)
            near = near + (pltpu.roll(for_near, shift, axis=0) if shift else for_near)
        mains.append(main[0:WIDE])
        nears.append(
            near[0:1] + pltpu.roll(near, BLOCK, axis=1)[1:2]
            + pltpu.roll(near, 2 * BLOCK, axis=1)[10:11] + pltpu.roll(near, 3 * BLOCK, axis=1)[11:12]
        )
        own_ref[:, x * LANES : (x + 1) * LANES] = near
    piece = jnp.concatenate(mains + nears, axis=0)
    four = jnp.concatenate([piece] * 4, axis=0)
    for i in range(out_ref.shape[0] // (4 * PIECE)):
        out_ref[i * 4 * PIECE : (i + 1) * 4 * PIECE, :] = four


def pattern_kernel(place, blocks, got_ref, own_ref, col_high_ref, col_low_ref, currents_hbm, far_hbm, currents_ref, far_ref, sems):
    _, col_at = place()
    samples = OVER * BLOCK
    far = dot3((col_high_ref[...], col_low_ref[...]), halves(got_ref[...]))
    left, right = 0, 0
    for b in range(blocks):
        left = jnp.where(col_at == b + 1, COL_ORDER.index(b), left)
        right = jnp.where(col_at == b - 1, COL_ORDER.index(b), right)
    has_left, has_right = jnp.where(col_at > 0, 1.0, 0.0), jnp.where(col_at < blocks - 1, 1.0, 0.0)
    own = own_ref[...]
    stacked = [far]
    for x in range(2):
        from_left = has_left * got_ref[pl.ds(left * PIECE + 2 * WIDE + x, 1), :]
        from_right = has_right * got_ref[pl.ds(right * PIECE + 2 * WIDE + x, 1), :]
        mine = own[:, x * LANES : (x + 1) * LANES]
        stacked += [
            mine[2:3] + pltpu.roll(from_left, LANES - 2 * BLOCK, axis=1),
            mine[3:4] + pltpu.roll(from_left, LANES - 3 * BLOCK, axis=1),
            mine[4:8],
            mine[8:9] + from_right,
            mine[9:10] + pltpu.roll(from_right, LANES - BLOCK, axis=1),
        ]
    stacked.append(jnp.zeros((LANES - 2 * samples - 2 * BLOCK, LANES), jnp.float32))
    flat = jnp.concatenate(stacked, axis=0).T
    copies = []
    for x in range(2):
        at = 2 * samples + x * BLOCK
        for s in range(STATES):
            far_ref[x, s] = flat[s * samples : (s + 1) * samples, x * samples : (x + 1) * samples]
            currents_ref[x, s] = flat[s * samples : s * samples + BLOCK, at : at + BLOCK]
        copies += fetch(sems.at[x], (far_ref.at[x], far_hbm.at[x]), (currents_ref.at[x], currents_hbm.at[x]))
    for copy in copies:
        copy.wait()


def spot():
    return lax.axis_index("row"), lax.axis_index("col")


HBM = pl.BlockSpec(memory_space=pltpu.HBM)


def call(kernel, out_shape, scratch=(), flops=0, size=0, grant=40960, **options):
    return pl.pallas_call(
        kernel,
        out_shape=out_shape,
        scratch_shapes=list(scratch),
        compiler_params=pltpu.CompilerParams(vmem_limit_bytes=grant * 1024),
        cost_estimate=pl.CostEstimate(flops=flops, bytes_accessed=size, transcendentals=0),
        **options,
    )


def exchange(pieces, axis, order):
    return lax.all_to_all(pieces, axis, 0, 0, axis_index_groups=[list(order)])


def body(row_blocks, col_blocks, place, active_flags, port_index, drive_weights, feed_table, cell_map, probe_weights):
    rows, cols = row_blocks * BLOCK, col_blocks * BLOCK
    samples = OVER * BLOCK
    f32, b16 = jnp.float32, jnp.bfloat16
    shape = jax.ShapeDtypeStruct
    taken = (
        drive_weights, active_flags, port_index,
        feed_table, cell_map, probe_weights, jnp.asarray(path_matrix(), b16),
    )
    packed, row_high, row_low, col_high, col_low = call(
        functools.partial(pack_kernel, place, rows, cols),
        (
            pltpu.VMEM((row_blocks, BLOCK, LANES), f32),
            pltpu.VMEM((2 * rows, 2 * LANES), b16),
            pltpu.VMEM((2 * rows, 2 * LANES), b16),
            pltpu.VMEM((2 * samples, col_blocks * PIECE), b16),
            pltpu.VMEM((2 * samples, col_blocks * PIECE), b16),
        ),
        scratch=[pltpu.VMEM(x.shape, x.dtype) for x in taken]
        + [
            pltpu.VMEM((144, cell_map.shape[1]), f32),
            pltpu.VMEM((ROWS, LANES), f32),
            pltpu.VMEM((BLOCK, LANES), f32),
            pltpu.SemaphoreType.DMA((3,)),
            pltpu.SemaphoreType.DMA((7,)),
        ],
        in_specs=[HBM] * 7,
        name="pack",
        grant=57344,
    )(*taken)
    cells = exchange(packed, "row", ROW_ORDER).reshape(rows, LANES)
    pieces, own = call(
        functools.partial(stencil_kernel, place, rows, cols),
        (shape((col_blocks * PIECE, LANES), f32), shape((16, 2 * LANES), f32)),
        scratch=[pltpu.VMEM((rows // LANES, BLOCK * ROWS, LANES), f32)],
        name="stencil",
    )(cells, row_high, row_low)
    got = exchange(pieces.reshape(col_blocks, PIECE // 2, 2, LANES), "col", COL_ORDER)
    return call(
        functools.partial(pattern_kernel, place, col_blocks),
        (shape((2, STATES, BLOCK, BLOCK), f32), shape((2, STATES, samples, samples), f32)),
        scratch=[
            pltpu.VMEM((2, STATES, BLOCK, BLOCK), f32),
            pltpu.VMEM((2, STATES, samples, samples), f32),
            pltpu.SemaphoreType.DMA((2, 2)),
        ],
        out_specs=(HBM, HBM),
        name="pattern",
    )(got.reshape(col_blocks * PIECE, LANES), own, col_high, col_low)


def solution(mesh):
    placed = (P("row", "col"), P("row", "col"), P(None, None, "row", "col"), P(), P(), P())
    return jax.shard_map(
        functools.partial(body, mesh.shape["row"], mesh.shape["col"], spot),
        mesh=mesh,
        in_specs=placed,
        out_specs=(P(None, None, "row", "col"), P(None, None, "row", "col")),
        check_vma=False,
    )
```
